32 devices in a mesh: mem: 8 (over z, x), sub: 4 (over y, core).
Axes of the slice: x: 2, y: 2, z: 4, core: 2. Of those that a mesh axis runs over, the one named last changes fastest.
Arguments:
- ensemble: float32 [32, 3, 128, 2048], P('mem', None, 'sub'), may hold values from -6 to 6
- sea_depth: float32 [128, 2048], P('sub'), may hold values from 0.5 to 2
- cutoff: int32 [128, 2048], P('sub', 'mem'), may hold values from 16 to 64
- obs_index: int32 [4, 256], replicated, may hold values from 0 to 262143
- obs_value: float32 [4, 256], replicated, may hold values from -6 to 6
- obs_var: float32 [4, 256], replicated, may hold values from 0.5 to 2
Outputs:
- analysis: float32 [32, 3, 128, 2048], P(None, None, 'sub', 'mem')
The draws below stay inside these ranges and needn't reach their ends.
All inputs are finite; a program needn't handle non-finite values.
Results may differ from the reference program's by a relative error of at most 0.0001.
Values sent between devices are 32-bit elements; how exact they have to be, the bound alone decides.
No kernel may reach another device: no remote copies, remote signals or barrier semaphores. Data moves between devices by JAX's collectives and lax.ppermute only.
A program may use at most 192 MiB of HBM per device.

```python
import math
import jax
import jax.numpy as jnp
from jax import lax

MEMBERS = 32
ROWS_DEV = 32
NX = 128
NY = 2048
STEPS = 4
NOBS = 256
BATCHES = 4


def set_ends(result, stream_key, least, largest):
    dims = result.shape
    index_at = [jax.random.randint(jax.random.fold_in(stream_key, axis), (), 0, dims[axis]) for axis in range(len(dims))]
    result = result.at[tuple(index_at)].set(least)
    longest = dims.index(max(dims))
    index_at[longest] = (index_at[longest] + 1) % dims[longest]
    return result.at[tuple(index_at)].set(largest)


def block_scale(key, shape, split, low, top_value):
    def one(dim, shards_of):
        heights = jax.random.uniform(jax.random.fold_in(jax.random.fold_in(key, 6), dim), (shards_of,), jnp.float32, low / len(split), top_value / len(split))
        return jnp.repeat(jnp.exp(heights), shape[dim] // shards_of).reshape((-1,) + (1,) * (len(shape) - dim - 1))

    loudness = one(*split[0])
    for cut in split[1:]:
        loudness = loudness * one(*cut)
    return loudness


def normal_values(rng, dims, spread, bound, shards=(), held_as=jnp.bfloat16):
    values = spread * jax.random.normal(rng, dims, jnp.float32)
    if shards:
        values = values * block_scale(rng, dims, shards, -0.22, 0.18)
    return jnp.clip(values, -bound, bound).astype(held_as)


def setup_inputs(seed: int = 0) -> dict:
    key_of = jax.random.split(jax.random.key(seed), 7)
    ensemble = normal_values(key_of[0], (MEMBERS, 3, NX, NY), 1.0, 6.0, ((0, 8), (2, 4)), jnp.float32)
    sea_depth = jnp.clip(jnp.exp(math.log(2.0) - 1.3862944 * jax.random.uniform(key_of[1], (NX, NY), jnp.float32) ** block_scale(key_of[1], (NX, NY), ((0, 4),), -0.2, 0.2)), 0.5, 2.0)
    cutoff = set_ends(jax.random.randint(key_of[2], (NX, NY), max(2, ROWS_DEV // 2), 2 * ROWS_DEV + 1), jax.random.fold_in(key_of[2], 1), max(2, ROWS_DEV // 2), 2 * ROWS_DEV).astype(jnp.int32)
    obs_index = set_ends(jax.random.randint(key_of[3], (BATCHES, NOBS), 0, NX * NY), jax.random.fold_in(key_of[3], 1), 0, (NX * NY) - 1).astype(jnp.int32)
    obs_value = normal_values(key_of[4], (BATCHES, NOBS), 1.0, 6.0, (), jnp.float32)
    obs_var = jnp.clip(jnp.exp(jax.random.uniform(key_of[5], (BATCHES, NOBS), jnp.float32, math.log(0.5), math.log(2.0))), 0.5, 2.0)
    return dict(ensemble=ensemble, sea_depth=sea_depth, cutoff=cutoff, obs_index=obs_index, obs_value=obs_value, obs_var=obs_var)


step_size = 0.3
coriolis = 0.2
highest = lax.Precision.HIGHEST

def centred(field, axis):
    return (jnp.roll(field, -1, axis) - jnp.roll(field, 1, axis)) * 0.5

def localize(obs_x, obs_y, cell_x, cell_y, radius_sq, size_x, size_y):
    gap_x = jnp.abs(cell_x[None, :] - obs_x[:, None])
    gap_x = jnp.minimum(gap_x, size_x - gap_x)
    gap_y = jnp.abs(cell_y[None, :] - obs_y[:, None])
    gap_y = jnp.minimum(gap_y, size_y - gap_y)
    dist_sq = (gap_x * gap_x + gap_y * gap_y).astype(jnp.float32)
    dist_ratio = dist_sq / radius_sq[None, :]
    return jnp.square(jnp.maximum(1.0 - dist_ratio, 0.0))

def analysis_weights(prior_obs, values, variance):
    member_count = prior_obs.shape[1]
    obs_mean = jnp.mean(prior_obs, 1)
    obs_anom = prior_obs - obs_mean[:, None]
    innov_cov = jnp.dot(obs_anom, obs_anom.T, precision=highest) / (member_count - 1) + jnp.diag(variance)
    factor = jnp.linalg.cholesky(innov_cov)
    right_side = jnp.concatenate([(values - obs_mean)[:, None], obs_anom], 1)
    solved = jax.scipy.linalg.cho_solve((factor, True), right_side)
    return (obs_anom, solved[:, :1] - 0.5 * solved[:, 1:])

def reference(ensemble, sea_depth, cutoff, obs_index, obs_value, obs_var):
    height = ensemble[:, 0]
    east_wind = ensemble[:, 1]
    north_wind = ensemble[:, 2]
    for step_id in range(STEPS):
        east_new = east_wind + step_size * (coriolis * north_wind - centred(height, 1))
        north_new = north_wind + step_size * (-coriolis * east_wind - centred(height, 2))
        divergence = centred(sea_depth * east_new, 1) + centred(sea_depth * north_new, 2)
        height = height - step_size * divergence
        east_wind = east_new
        north_wind = north_new
    point_state = jnp.stack([height, east_wind, north_wind], 1)
    grid_rows = jnp.transpose(point_state, (2, 0, 1, 3))
    col_ids = jnp.arange(NY, dtype=jnp.int32)
    row_ids = jnp.arange(NX, dtype=jnp.int32)
    radius_sq = jnp.square(cutoff.astype(jnp.float32))
    for batch_id in range(BATCHES):
        obs_cell = obs_index[batch_id]
        obs_x = (obs_cell // NY).astype(jnp.int32)
        obs_y = (obs_cell % NY).astype(jnp.int32)
        prior_obs = grid_rows[obs_x, :, 0, obs_y]
        obs_anom, weights_mix = analysis_weights(prior_obs, obs_value[batch_id], obs_var[batch_id])

        def update_row(items):
            grid_row, row_id, row_radius = items
            state_anom = grid_row - jnp.mean(grid_row, 0)
            cross_cov = jnp.einsum('om,mfy->ofy', obs_anom, state_anom, precision=highest) / (MEMBERS - 1)
            loc_weight = localize(obs_x, obs_y, jnp.zeros((NY,), jnp.int32) + row_id, col_ids, row_radius, NX, NY)
            loc_gain = cross_cov * loc_weight[:, None, :]
            return grid_row + jnp.einsum('om,ofy->mfy', weights_mix, loc_gain, precision=highest)
        grid_rows = lax.map(update_row, (grid_rows, row_ids, radius_sq))
    return jnp.transpose(grid_rows, (1, 2, 0, 3))
```

```python
import functools

import jax
import jax.numpy as jnp
from jax import lax
from jax.experimental import pallas as pl
from jax.experimental.pallas import tpu as pltpu
from jax.sharding import PartitionSpec as P

STEPS = 4
HALO = 2 * STEPS
LANES = 128
OBS_BLOCK = 64
ROW_TILE = 8
VMEM_LIMIT = 48 * 2**20

step_size = 0.3
coriolis = 0.2
highest = lax.Precision.HIGHEST

NT = (((1,), (1,)), ((), ()))
TN = (((0,), (0,)), ((), ()))


def params():
    return pltpu.CompilerParams(vmem_limit_bytes=VMEM_LIMIT)


def vmem(count=1):
    return [pl.BlockSpec(memory_space=pltpu.VMEM)] * count


def smem(count=1):
    return [pl.BlockSpec(memory_space=pltpu.SMEM)] * count


def split_bf16(value):
    high = value.astype(jnp.bfloat16)
    low = (value - high.astype(jnp.float32)).astype(jnp.bfloat16)
    return high, low


def centred(field, axis):
    length = field.shape[axis]
    return pltpu.roll(field, length - 1, axis) - pltpu.roll(field, 1, axis)


def forecast_kernel(ens_ref, up_ref, down_ref, depth_ref, out_ref):
    height, east, north = [
        jnp.concatenate([up_ref[0, f], ens_ref[0, f], down_ref[0, f]], 0) for f in range(3)
    ]
    depth = depth_ref[...]
    half = 0.5 * step_size
    turn = step_size * coriolis
    for _ in range(STEPS):
        east_new = east + turn * north - half * centred(height, 0)
        north_new = north - turn * east - half * centred(height, 1)
        height = height - half * (centred(depth * east_new, 0) + centred(depth * north_new, 1))
        east, north = east_new, north_new
    rows = ens_ref.shape[2]
    blocks, _, _, tiles = out_ref.shape[:4]
    for f, field in enumerate((height, east, north)):
        for d in range(blocks):
            for t in range(tiles):
                first = (d * tiles + t) * LANES
                out_ref[d, 0, f, t] = field[HALO : HALO + rows, first : first + LANES]


def forecast(ensemble, up, down, depth, blocks):
    members, fields, rows, columns = ensemble.shape
    tiles = columns // blocks // LANES
    return pl.pallas_call(
        forecast_kernel,
        grid=(members,),
        in_specs=[
            pl.BlockSpec((1, fields, rows, columns), lambda m: (m, 0, 0, 0)),
            pl.BlockSpec((1, fields, HALO, columns), lambda m: (m, 0, 0, 0)),
            pl.BlockSpec((1, fields, HALO, columns), lambda m: (m, 0, 0, 0)),
            pl.BlockSpec((rows + 2 * HALO, columns), lambda m: (0, 0)),
        ],
        out_specs=pl.BlockSpec(
            (blocks, 1, fields, tiles, rows, LANES), lambda m: (0, m, 0, 0, 0, 0)
        ),
        out_shape=jax.ShapeDtypeStruct(
            (blocks, members, fields, tiles, rows, LANES), jnp.float32
        ),
        compiler_params=params(),
        name="forecast",
    )(ensemble, up, down, depth)


def pick_kernel(base_ref, lane_ref, place_ref, height_ref, out_ref):
    blocks, members, _, tiles, rows, _ = height_ref.shape
    flat = height_ref.reshape(blocks * members * tiles * rows, LANES)
    lanes = lax.broadcasted_iota(jnp.int32, (members, LANES), 1)
    unroll = 16

    def group(g, _):
        def some(i, acc):
            for j in range(unroll):
                k = i * unroll + j
                o = g * LANES + k
                row = flat[pl.ds(base_ref[o], members, stride=tiles * rows), :]
                row = pltpu.roll(row, lane_ref[o], 1)
                acc = jnp.where(lanes == place_ref[o], row, acc)
            return acc

        acc = lax.fori_loop(
            0, LANES // unroll, some, jnp.zeros((members, LANES), jnp.float32)
        )
        out_ref[:, pl.ds(pl.multiple_of(g * LANES, LANES), LANES)] = acc
        return 0

    lax.fori_loop(0, out_ref.shape[1] // LANES, group, 0)


def pick_heights(sent, obs_x, obs_y, x_start):
    blocks, members, fields, tiles, rows, _ = sent.shape
    count = obs_x.shape[0]
    col_block = tiles * LANES
    local_x = obs_x - x_start
    inside = (local_x >= 0) & (local_x < rows)
    safe_x = jnp.where(inside, local_x, 0)
    block = obs_y // col_block
    tile = (obs_y % col_block) // LANES
    base = (block * members * tiles + tile) * rows + safe_x
    place = jnp.arange(count, dtype=jnp.int32) % LANES
    shift = (place - obs_y % LANES) % LANES
    place = jnp.where(inside, place, -1)
    return pl.pallas_call(
        pick_kernel,
        grid=(1,),
        in_specs=smem(3)
        + [pl.BlockSpec((blocks, members, 1, tiles, rows, LANES), lambda i: (0,) * 6)],
        out_specs=pl.BlockSpec((members, count), lambda i: (0, 0)),
        out_shape=jax.ShapeDtypeStruct((members, count), jnp.float32),
        compiler_params=params(),
        name="pick",
    )(base, shift, place, sent)


def pick_radius(cutoff, obs_x, obs_y, x_start, y_start):
    rows, columns = cutoff.shape
    radius_sq = jnp.square(cutoff.astype(jnp.float32))
    row_is = (obs_x[:, None] - x_start == jnp.arange(rows)[None, :]).astype(jnp.float32)
    col_is = obs_y[:, None] - y_start == jnp.arange(columns)[None, :]
    by_row = jnp.dot(row_is, radius_sq, precision=highest)
    return jnp.sum(jnp.where(col_is, by_row, 0.0), 1)


def exchange(value, axis, distance):
    size = lax.axis_size(axis)
    return lax.ppermute(value, axis, [(i, i ^ distance) for i in range(size)])


def sum_over(value, axis):
    distance = 1
    while distance < lax.axis_size(axis):
        value = value + exchange(value, axis, distance)
        distance *= 2
    return value


def gather_over(value, axis):
    here = lax.axis_index(axis)
    distance = 1
    while distance < lax.axis_size(axis):
        other = exchange(value, axis, distance)
        lower = (here & distance) == 0
        value = jnp.where(
            lower, jnp.concatenate([value, other], 0), jnp.concatenate([other, value], 0)
        )
        distance *= 2
    return value


def apart_sq(a, b, size):
    gap = jnp.abs(a - b)
    gap = jnp.minimum(gap, size - gap)
    return gap * gap


def chain_kernel(
    sizes,
    start_ref,
    heights_ref,
    radius_ref,
    row_ref,
    col_ref,
    value_ref,
    variance_ref,
    cutoff_ref,
    lhs1_ref,
    lhs2_ref,
    place_ref,
    count_ref,
):
    size_x, size_y = sizes
    members = heights_ref.shape[0]
    batches, count = value_ref.shape
    rows, columns = cutoff_ref.shape
    x_start = start_ref[0]
    y_start = start_ref[1]
    reach = jnp.max(cutoff_ref[...])
    reach_sq = reach * reach

    heights = heights_ref[...]
    before = (
        lax.broadcasted_iota(jnp.int32, (count, count), 0)
        <= lax.broadcasted_iota(jnp.int32, (count, count), 1)
    ).astype(jnp.bfloat16)
    slot = lax.broadcasted_iota(jnp.int32, (count, count), 0)
    member_row = lax.broadcasted_iota(jnp.int32, (members, LANES + count), 0)
    eye = (
        lax.broadcasted_iota(jnp.int32, (members, members), 0)
        == lax.broadcasted_iota(jnp.int32, (members, members), 1)
    ).astype(jnp.float32)

    for b in range(batches):
        here = slice(b * count, (b + 1) * count)
        prior = heights[:, here]
        mean = jnp.mean(prior, 0, keepdims=True)
        anom = prior - mean
        precision = 1.0 / variance_ref[b : b + 1, :]
        innov = value_ref[b : b + 1, :] - mean
        scaled = anom * precision
        inner = eye + lax.dot_general(
            scaled, anom, NT, precision=highest, preferred_element_type=jnp.float32
        ) / (members - 1)
        proj = jnp.sum(scaled * innov, 1, keepdims=True)
        system = jnp.concatenate(
            [inner, proj, jnp.zeros((members, LANES - members - 1), jnp.float32), scaled], 1
        )
        for k in range(members):
            pivot_row = system[k : k + 1, :] / system[k : k + 1, k : k + 1]
            system = jnp.where(
                member_row == k, pivot_row, system - system[:, k : k + 1] * pivot_row
            )
        solved_proj = system[:, members : members + 1]
        solved_anom = system[:, LANES:]
        solved_innov = precision * (
            innov - jnp.sum(anom * solved_proj, 0, keepdims=True) / (members - 1)
        )
        mix = (solved_innov - 0.5 * solved_anom) / (members - 1)

        obs_x = row_ref[0:1, here]
        obs_y = row_ref[1:2, here]
        off_x = jnp.where(obs_x >= x_start, obs_x - x_start, obs_x - x_start + size_x)
        off_y = jnp.where(obs_y >= y_start, obs_y - y_start, obs_y - y_start + size_y)
        gap_x = jnp.where(off_x < rows, 0, jnp.minimum(off_x - (rows - 1), size_x - off_x))
        gap_y = jnp.where(off_y < columns, 0, jnp.minimum(off_y - (columns - 1), size_y - off_y))
        reaches = gap_x * gap_x + gap_y * gap_y < reach_sq
        flags = jnp.broadcast_to(reaches.astype(jnp.float32), (8, count))
        ranks = jnp.dot(
            flags.astype(jnp.bfloat16), before, preferred_element_type=jnp.float32
        )
        rank = jnp.where(reaches, ranks[0:1, :].astype(jnp.int32) - 1, -1)
        chosen = (slot == rank).astype(jnp.float32)
        count_ref[b] = jnp.sum(flags[0:1, :]).astype(jnp.int32)

        near_anom = lax.dot_general(
            chosen, anom, NT, precision=highest, preferred_element_type=jnp.float32
        )
        high, low = split_bf16(near_anom)
        lhs1_ref[b] = jnp.concatenate([high, high, low], 1)
        near_mix = lax.dot_general(
            mix, chosen, NT, precision=highest, preferred_element_type=jnp.float32
        )
        high, low = split_bf16(near_mix)
        for k in range(count // OBS_BLOCK):
            part = slice(k * OBS_BLOCK, (k + 1) * OBS_BLOCK)
            lhs2_ref[b, k] = jnp.concatenate([high[:, part], high[:, part], low[:, part]], 1)
        where = jnp.concatenate(
            [
                jnp.broadcast_to(obs_x, (LANES, count)),
                jnp.broadcast_to(obs_y, (LANES, count)),
            ],
            0,
        ).astype(jnp.float32)
        place_ref[b] = lax.dot_general(
            chosen, where, NT, precision=highest, preferred_element_type=jnp.float32
        )

        if b + 1 < batches:
            later = slice((b + 1) * count, batches * count)
            ahead = heights[:, later]
            ahead_anom = ahead - jnp.mean(ahead, 0, keepdims=True)
            cross = lax.dot_general(
                anom, ahead_anom, TN, precision=highest, preferred_element_type=jnp.float32
            )
            dist_sq = apart_sq(col_ref[:, b : b + 1], row_ref[0:1, later], size_x) + apart_sq(
                col_ref[:, batches + b : batches + b + 1], row_ref[1:2, later], size_y
            )
            ratio = dist_sq.astype(jnp.float32) / radius_ref[:, later]
            gain = cross * jnp.square(jnp.maximum(1.0 - ratio, 0.0))
            ahead = ahead + jnp.dot(
                mix, gain, precision=highest, preferred_element_type=jnp.float32
            )
            heights = jnp.concatenate([heights[:, : (b + 1) * count], ahead], 1)


def chain(start, heights, radius_sq, obs_x, obs_y, values, variance, cutoff, sizes):
    members = heights.shape[0]
    batches, count = values.shape
    row_form = jnp.stack([obs_x.reshape(-1), obs_y.reshape(-1)], 0)
    col_form = jnp.concatenate([obs_x, obs_y], 0).T
    return pl.pallas_call(
        functools.partial(chain_kernel, sizes),
        in_specs=smem() + vmem(7),
        out_specs=vmem(3) + smem(),
        out_shape=[
            jax.ShapeDtypeStruct((batches, count, 3 * members), jnp.bfloat16),
            jax.ShapeDtypeStruct(
                (batches, count // OBS_BLOCK, members, 3 * OBS_BLOCK), jnp.bfloat16
            ),
            jax.ShapeDtypeStruct((batches, count, 2 * LANES), jnp.float32),
            jax.ShapeDtypeStruct((batches,), jnp.int32),
        ],
        compiler_params=params(),
        name="chain",
    )(start, heights, radius_sq, row_form, col_form, values, variance, cutoff)


def update_kernel(
    sizes,
    start_ref,
    count_ref,
    state_ref,
    cutoff_ref,
    lhs1_ref,
    lhs2_ref,
    place_ref,
    out_ref,
    members_ref,
    rhs_ref,
    back_ref,
):
    size_x, size_y = float(sizes[0]), float(sizes[1])
    members, fields, tiles, rows, _ = state_ref.shape
    batches = lhs1_ref.shape[0]
    cells = rows * LANES
    flat = state_ref.reshape(members * fields * tiles * rows, LANES)
    flat_back = back_ref.reshape(members * fields * rows, LANES)
    row0 = (start_ref[0] + pl.program_id(0) * rows).astype(jnp.float32)
    lane = lax.broadcasted_iota(jnp.int32, (1, LANES), 1).astype(jnp.float32)

    def contribution(b, k, t):
        first = k * OBS_BLOCK
        if not isinstance(k, int):
            first = pl.multiple_of(first, OBS_BLOCK)
        part = pl.ds(first, OBS_BLOCK)
        obs_x = place_ref[b, part, :LANES]
        obs_y = place_ref[b, part, LANES:]
        col0 = (start_ref[1] + t * LANES).astype(jnp.float32)
        dist_y = apart_sq(obs_y, lane + col0, size_y)
        weights = []
        for r in range(rows):
            radius = cutoff_ref[r : r + 1, t * LANES : (t + 1) * LANES].astype(jnp.float32)
            ratio = (dist_y + apart_sq(obs_x, row0 + r, size_x)) * (1.0 / (radius * radius))
            weights.append(jnp.square(jnp.maximum(1.0 - ratio, 0.0)))
        weights = jnp.concatenate(weights, 1)
        cross = jnp.dot(
            lhs1_ref[b, part, :], rhs_ref[...], preferred_element_type=jnp.float32
        )
        gain = cross * jnp.concatenate([weights] * fields, 1)
        high, low = split_bf16(gain)
        return jnp.dot(
            lhs2_ref[b, k],
            jnp.concatenate([high, low, high], 0),
            preferred_element_type=jnp.float32,
        )

    for t in range(tiles):
        for f in range(fields):
            for r in range(rows):
                place = f * cells + r * LANES
                members_ref[:, place : place + LANES] = flat[
                    pl.ds((f * tiles + t) * rows + r, members, stride=fields * tiles * rows), :
                ]
        for b in range(batches):
            state = members_ref[...]
            high, low = split_bf16(state - jnp.mean(state, 0, keepdims=True))
            rhs_ref[...] = jnp.concatenate([high, low, high], 0)
            members_ref[...] = state + contribution(b, 0, t)

            def more(k, _):
                members_ref[...] += contribution(b, k, t)
                return 0

            blocks = (count_ref[b] + (OBS_BLOCK - 1)) // OBS_BLOCK
            lax.fori_loop(1, blocks, more, 0)
        for f in range(fields):
            for r in range(rows):
                place = f * cells + r * LANES
                flat_back[pl.ds(f * rows + r, members, stride=fields * rows), :] = members_ref[
                    :, place : place + LANES
                ]
        out_ref[:, :, :, t * LANES : (t + 1) * LANES] = back_ref[...]


def update(start, counts, state, cutoff, lhs1, lhs2, place, sizes):
    members, fields, tiles, rows, _ = state.shape
    columns = tiles * LANES
    width = fields * ROW_TILE * LANES

    def whole(array):
        return pl.BlockSpec(array.shape, lambda i: (0,) * array.ndim)

    return pl.pallas_call(
        functools.partial(update_kernel, sizes),
        grid=(rows // ROW_TILE,),
        in_specs=smem(2)
        + [
            pl.BlockSpec(
                (members, fields, tiles, ROW_TILE, LANES), lambda i: (0, 0, 0, i, 0)
            ),
            pl.BlockSpec((ROW_TILE, columns), lambda i: (i, 0)),
            whole(lhs1),
            whole(lhs2),
            whole(place),
        ],
        out_specs=pl.BlockSpec(
            (members, fields, ROW_TILE, columns), lambda i: (0, 0, i, 0)
        ),
        out_shape=jax.ShapeDtypeStruct((members, fields, rows, columns), jnp.float32),
        scratch_shapes=[
            pltpu.VMEM((members, width), jnp.float32),
            pltpu.VMEM((3 * members, width), jnp.bfloat16),
            pltpu.VMEM((members, fields, ROW_TILE, LANES), jnp.float32),
        ],
        compiler_params=params(),
        name="update",
    )(start, counts, state, cutoff, lhs1, lhs2, place)


def row_halos(block, axis):
    size = lax.axis_size(axis)
    onward = [(i, (i + 1) % size) for i in range(size)]
    backward = [(j, i) for i, j in onward]
    rows = block.shape[-2]
    last = lax.slice_in_dim(block, rows - HALO, rows, axis=block.ndim - 2)
    leading = lax.slice_in_dim(block, 0, HALO, axis=block.ndim - 2)
    return lax.ppermute(last, axis, onward), lax.ppermute(leading, axis, backward)


def local(ensemble, sea_depth, cutoff, obs_index, obs_value, obs_var):
    blocks = lax.axis_size("mem")
    members, fields, rows, size_y = ensemble.shape
    col_block = size_y // blocks
    size_x = rows * lax.axis_size("sub")
    sizes = (size_x, size_y)
    x_start = lax.axis_index("sub") * rows
    y_start = lax.axis_index("mem") * col_block
    start = jnp.stack([x_start, y_start]).astype(jnp.int32)
    obs_x = obs_index // size_y
    obs_y = obs_index % size_y
    flat_x = obs_x.reshape(-1)
    flat_y = obs_y.reshape(-1)

    up, down = row_halos(ensemble, "sub")
    depth_up, depth_down = row_halos(sea_depth, "sub")
    depth = jnp.concatenate([depth_up, sea_depth, depth_down], 0)
    sent = forecast(ensemble, up, down, depth, blocks)

    radius_part = pick_radius(cutoff, flat_x, flat_y, x_start, y_start)
    heights_part = pick_heights(sent, flat_x, flat_y, x_start)
    part = jnp.concatenate([heights_part, radius_part[None, :]], 0)
    part = jnp.pad(part, ((0, -part.shape[0] % 8), (0, 0)))
    every = gather_over(sum_over(part, "sub")[None], "mem")
    heights = every[:, :members].reshape(blocks * members, -1)
    radius_sq = jnp.sum(every[:, members], 0)[None, :]

    received = lax.all_to_all(sent, "mem", split_axis=0, concat_axis=0, tiled=True)
    state = received.reshape((blocks * members,) + received.shape[2:])
    lhs1, lhs2, place, counts = chain(
        start, heights, radius_sq, obs_x, obs_y, obs_value, obs_var, cutoff, sizes
    )
    return update(start, counts, state, cutoff, lhs1, lhs2, place, sizes)


def solution(mesh):
    return jax.shard_map(
        local,
        mesh=mesh,
        in_specs=(P("mem", None, "sub", None), P("sub", None), P("sub", "mem"), P(), P(), P()),
        out_specs=P(None, None, "sub", "mem"),
        check_vma=False,
    )
```

```python
import functools

import jax
import jax.numpy as jnp
from jax import lax
from jax.experimental import pallas as pl
from jax.experimental.pallas import tpu as pltpu
from jax.sharding import PartitionSpec as P

STEPS = 4
HALO = 2 * STEPS
LANES = 128
OBS_BLOCK = 64
ROW_TILE = 8
VMEM_LIMIT = 48 * 2**20

step_size = 0.3
coriolis = 0.2
highest = lax.Precision.HIGHEST

NT = (((1,), (1,)), ((), ()))
TN = (((0,), (0,)), ((), ()))


def params():
    return pltpu.CompilerParams(vmem_limit_bytes=VMEM_LIMIT)


def vmem(count=1):
    return [pl.BlockSpec(memory_space=pltpu.VMEM)] * count


def smem(count=1):
    return [pl.BlockSpec(memory_space=pltpu.SMEM)] * count


def split_bf16(value):
    high = value.astype(jnp.bfloat16)
    low = (value - high.astype(jnp.float32)).astype(jnp.bfloat16)
    return high, low


def centred(field, axis):
    length = field.shape[axis]
    return pltpu.roll(field, length - 1, axis) - pltpu.roll(field, 1, axis)


def forecast_steps(window, depth):
    height, east, north = window
    half = 0.5 * step_size
    turn = step_size * coriolis
    for _ in range(STEPS):
        east_new = east + turn * north - half * centred(height, 0)
        north_new = north - turn * east - half * centred(height, 1)
        height = height - half * (centred(depth * east_new, 0) + centred(depth * north_new, 1))
        east, north = east_new, north_new
    return height, east, north


def send_rows(out_ref, fields, pieces):
    blocks, _, _, tiles = out_ref.shape[:4]
    for f, field in enumerate(fields):
        for d in range(blocks):
            for t in range(tiles):
                first = (d * tiles + t) * LANES
                for row, length, place in pieces:
                    out_ref[d, 0, f, t, place : place + length] = field[
                        row : row + length, first : first + LANES
                    ]


def inner_kernel(ens_ref, depth_ref, out_ref):
    rows = ens_ref.shape[2]
    done = forecast_steps([ens_ref[0, f] for f in range(3)], depth_ref[...])
    send_rows(out_ref, done, [(HALO, rows - 2 * HALO, 0)])


def outer_kernel(ens_ref, up_ref, down_ref, depth_ref, out_ref):
    rows = ens_ref.shape[2]
    window = [jnp.concatenate([up_ref[0, f], ens_ref[0, f], down_ref[0, f]], 0) for f in range(3)]
    done = forecast_steps(window, depth_ref[...])
    send_rows(out_ref, done, [(HALO, HALO, 0), (rows, HALO, HALO)])


def forecast(kernel, name, out_rows, depth, blocks, *pieces):
    members, fields, _, columns = pieces[0].shape
    tiles = columns // blocks // LANES
    return pl.pallas_call(
        kernel,
        grid=(members,),
        in_specs=[
            pl.BlockSpec((1,) + piece.shape[1:], lambda m: (m, 0, 0, 0)) for piece in pieces
        ]
        + [pl.BlockSpec(depth.shape, lambda m: (0, 0))],
        out_specs=pl.BlockSpec(
            (blocks, 1, fields, tiles, out_rows, LANES), lambda m: (0, m, 0, 0, 0, 0)
        ),
        out_shape=jax.ShapeDtypeStruct(
            (blocks, members, fields, tiles, out_rows, LANES), jnp.float32
        ),
        compiler_params=params(),
        name=name,
    )(*pieces, depth)


def list_kernel(shape, start_ref, x_ref, y_ref, inner_ref, outer_ref, count_ref):
    members, tiles, rows = shape
    x_start = start_ref[0]
    col_block = tiles * LANES
    inner_rows = rows - 2 * HALO
    outer_rows = 2 * HALO

    def one(o, counts):
        n_inner, n_outer = counts
        x = x_ref[o] - x_start
        y = y_ref[o]
        block = y // col_block
        tile = (y % col_block) // LANES
        lane = y % LANES
        is_inner = (x >= HALO) & (x < rows - HALO)
        is_outer = (x >= 0) & (x < rows) & jnp.logical_not(is_inner)
        stack = block * members * tiles + tile
        outer_x = jnp.where(x < HALO, x, x - inner_rows)
        inner_ref[0, n_inner] = o
        inner_ref[1, n_inner] = stack * inner_rows + x - HALO
        inner_ref[2, n_inner] = lane
        outer_ref[0, n_outer] = o
        outer_ref[1, n_outer] = stack * outer_rows + outer_x
        outer_ref[2, n_outer] = lane
        return n_inner + is_inner.astype(jnp.int32), n_outer + is_outer.astype(jnp.int32)

    zero = jnp.int32(0)
    n_inner, n_outer = lax.fori_loop(0, x_ref.shape[0], one, (zero, zero))
    count_ref[0] = n_inner
    count_ref[1] = n_outer


def list_observations(shape, start, flat_x, flat_y):
    count = flat_x.shape[0]
    return pl.pallas_call(
        functools.partial(list_kernel, shape),
        in_specs=smem(3),
        out_specs=smem(3),
        out_shape=[
            jax.ShapeDtypeStruct((3, count), jnp.int32),
            jax.ShapeDtypeStruct((3, count), jnp.int32),
            jax.ShapeDtypeStruct((2,), jnp.int32),
        ],
        name="list",
    )(start, flat_x, flat_y)


def pick_kernel(which, list_ref, count_ref, height_ref, start_ref, out_ref):
    blocks, members, _, tiles, rows, _ = height_ref.shape
    flat = height_ref.reshape(blocks * members * tiles * rows, LANES)
    lanes = lax.broadcasted_iota(jnp.int32, (members, LANES), 1)
    out_ref[...] = start_ref[...]

    def one(i, _):
        o = list_ref[0, i]
        place = o % LANES
        row = flat[pl.ds(list_ref[1, i], members, stride=tiles * rows), :]
        row = pltpu.roll(row, (place - list_ref[2, i]) % LANES, 1)
        group = pl.ds(pl.multiple_of(o - place, LANES), LANES)
        out_ref[:members, group] = jnp.where(lanes == place, row, out_ref[:members, group])
        return 0

    lax.fori_loop(0, count_ref[which], one, 0)


def pick_heights(which, lists, counts, sent, begin):
    blocks, members, fields, tiles, rows, _ = sent.shape
    return pl.pallas_call(
        functools.partial(pick_kernel, which),
        grid=(1,),
        in_specs=smem(2)
        + [
            pl.BlockSpec((blocks, members, 1, tiles, rows, LANES), lambda i: (0,) * 6),
            pl.BlockSpec(begin.shape, lambda i: (0, 0)),
        ],
        out_specs=pl.BlockSpec(begin.shape, lambda i: (0, 0)),
        out_shape=jax.ShapeDtypeStruct(begin.shape, jnp.float32),
        compiler_params=params(),
        name="pick",
    )(lists, counts, sent, begin)


def pick_radius(cutoff, obs_x, obs_y, x_start, y_start):
    rows, columns = cutoff.shape
    radius_sq = jnp.square(cutoff.astype(jnp.float32))
    row_is = (obs_x[:, None] - x_start == jnp.arange(rows)[None, :]).astype(jnp.float32)
    col_is = obs_y[:, None] - y_start == jnp.arange(columns)[None, :]
    by_row = jnp.dot(row_is, radius_sq, precision=highest)
    return jnp.sum(jnp.where(col_is, by_row, 0.0), 1)


def exchange(value, axis, distance):
    size = lax.axis_size(axis)
    return lax.ppermute(value, axis, [(i, i ^ distance) for i in range(size)])


def sum_over(value, axis):
    distance = 1
    while distance < lax.axis_size(axis):
        value = value + exchange(value, axis, distance)
        distance *= 2
    return value


def gather_over(value, axis):
    here = lax.axis_index(axis)
    distance = 1
    while distance < lax.axis_size(axis):
        other = exchange(value, axis, distance)
        lower = (here & distance) == 0
        value = jnp.where(
            lower, jnp.concatenate([value, other], 0), jnp.concatenate([other, value], 0)
        )
        distance *= 2
    return value


def apart_sq(a, b, size):
    gap = jnp.abs(a - b)
    gap = jnp.minimum(gap, size - gap)
    return gap * gap


def chain_kernel(
    sizes,
    start_ref,
    heights_ref,
    radius_ref,
    row_ref,
    col_ref,
    value_ref,
    variance_ref,
    cutoff_ref,
    lhs1_ref,
    lhs2_ref,
    place_ref,
    count_ref,
):
    size_x, size_y = sizes
    members = heights_ref.shape[0]
    batches, count = value_ref.shape
    rows, columns = cutoff_ref.shape
    x_start = start_ref[0]
    y_start = start_ref[1]
    reach = jnp.max(cutoff_ref[...])
    reach_sq = reach * reach

    heights = heights_ref[...]
    before = (
        lax.broadcasted_iota(jnp.int32, (count, count), 0)
        <= lax.broadcasted_iota(jnp.int32, (count, count), 1)
    ).astype(jnp.bfloat16)
    slot = lax.broadcasted_iota(jnp.int32, (count, count), 0)
    member_row = lax.broadcasted_iota(jnp.int32, (members, LANES + count), 0)
    eye = (
        lax.broadcasted_iota(jnp.int32, (members, members), 0)
        == lax.broadcasted_iota(jnp.int32, (members, members), 1)
    ).astype(jnp.float32)

    for b in range(batches):
        here = slice(b * count, (b + 1) * count)
        prior = heights[:, here]
        mean = jnp.mean(prior, 0, keepdims=True)
        anom = prior - mean
        precision = 1.0 / variance_ref[b : b + 1, :]
        innov = value_ref[b : b + 1, :] - mean
        scaled = anom * precision
        inner = eye + lax.dot_general(
            scaled, anom, NT, precision=highest, preferred_element_type=jnp.float32
        ) / (members - 1)
        proj = jnp.sum(scaled * innov, 1, keepdims=True)
        system = jnp.concatenate(
            [inner, proj, jnp.zeros((members, LANES - members - 1), jnp.float32), scaled], 1
        )
        for k in range(members):
            pivot_row = system[k : k + 1, :] / system[k : k + 1, k : k + 1]
            system = jnp.where(
                member_row == k, pivot_row, system - system[:, k : k + 1] * pivot_row
            )
        solved_proj = system[:, members : members + 1]
        solved_anom = system[:, LANES:]
        solved_innov = precision * (
            innov - jnp.sum(anom * solved_proj, 0, keepdims=True) / (members - 1)
        )
        mix = (solved_innov - 0.5 * solved_anom) / (members - 1)

        obs_x = row_ref[0:1, here]
        obs_y = row_ref[1:2, here]
        off_x = jnp.where(obs_x >= x_start, obs_x - x_start, obs_x - x_start + size_x)
        off_y = jnp.where(obs_y >= y_start, obs_y - y_start, obs_y - y_start + size_y)
        gap_x = jnp.where(off_x < rows, 0, jnp.minimum(off_x - (rows - 1), size_x - off_x))
        gap_y = jnp.where(off_y < columns, 0, jnp.minimum(off_y - (columns - 1), size_y - off_y))
        reaches = gap_x * gap_x + gap_y * gap_y < reach_sq
        flags = jnp.broadcast_to(reaches.astype(jnp.float32), (8, count))
        ranks = jnp.dot(
            flags.astype(jnp.bfloat16), before, preferred_element_type=jnp.float32
        )
        rank = jnp.where(reaches, ranks[0:1, :].astype(jnp.int32) - 1, -1)
        chosen = (slot == rank).astype(jnp.float32)
        count_ref[b] = jnp.sum(flags[0:1, :]).astype(jnp.int32)

        near_anom = lax.dot_general(
            chosen, anom, NT, precision=highest, preferred_element_type=jnp.float32
        )
        high, low = split_bf16(near_anom)
        lhs1_ref[b] = jnp.concatenate([high, high, low], 1)
        near_mix = lax.dot_general(
            mix, chosen, NT, precision=highest, preferred_element_type=jnp.float32
        )
        high, low = split_bf16(near_mix)
        for k in range(count // OBS_BLOCK):
            part = slice(k * OBS_BLOCK, (k + 1) * OBS_BLOCK)
            lhs2_ref[b, k] = jnp.concatenate([high[:, part], high[:, part], low[:, part]], 1)
        where = jnp.concatenate(
            [
                jnp.broadcast_to(obs_x, (LANES, count)),
                jnp.broadcast_to(obs_y, (LANES, count)),
            ],
            0,
        ).astype(jnp.float32)
        place_ref[b] = lax.dot_general(
            chosen, where, NT, precision=highest, preferred_element_type=jnp.float32
        )

        if b + 1 < batches:
            later = slice((b + 1) * count, batches * count)
            ahead = heights[:, later]
            ahead_anom = ahead - jnp.mean(ahead, 0, keepdims=True)
            cross = lax.dot_general(
                anom, ahead_anom, TN, precision=highest, preferred_element_type=jnp.float32
            )
            dist_sq = apart_sq(col_ref[:, b : b + 1], row_ref[0:1, later], size_x) + apart_sq(
                col_ref[:, batches + b : batches + b + 1], row_ref[1:2, later], size_y
            )
            ratio = dist_sq.astype(jnp.float32) / radius_ref[:, later]
            gain = cross * jnp.square(jnp.maximum(1.0 - ratio, 0.0))
            ahead = ahead + jnp.dot(
                mix, gain, precision=highest, preferred_element_type=jnp.float32
            )
            heights = jnp.concatenate([heights[:, : (b + 1) * count], ahead], 1)


def chain(start, heights, radius_sq, obs_x, obs_y, values, variance, cutoff, sizes):
    members = heights.shape[0]
    batches, count = values.shape
    row_form = jnp.stack([obs_x.reshape(-1), obs_y.reshape(-1)], 0)
    col_form = jnp.concatenate([obs_x, obs_y], 0).T
    return pl.pallas_call(
        functools.partial(chain_kernel, sizes),
        in_specs=smem() + vmem(7),
        out_specs=vmem(3) + smem(),
        out_shape=[
            jax.ShapeDtypeStruct((batches, count, 3 * members), jnp.bfloat16),
            jax.ShapeDtypeStruct(
                (batches, count // OBS_BLOCK, members, 3 * OBS_BLOCK), jnp.bfloat16
            ),
            jax.ShapeDtypeStruct((batches, count, 2 * LANES), jnp.float32),
            jax.ShapeDtypeStruct((batches,), jnp.int32),
        ],
        compiler_params=params(),
        name="chain",
    )(start, heights, radius_sq, row_form, col_form, values, variance, cutoff)


def update_kernel(
    sizes,
    first_tile,
    tile_stride,
    continues,
    start_ref,
    count_ref,
    state_ref,
    cutoff_ref,
    lhs1_ref,
    lhs2_ref,
    place_ref,
    *rest,
):
    out_ref, members_ref, rhs_ref, back_ref = rest[1:] if continues else rest
    size_x, size_y = float(sizes[0]), float(sizes[1])
    members, fields, tiles, rows, _ = state_ref.shape
    batches = lhs1_ref.shape[0]
    cells = rows * LANES
    flat = state_ref.reshape(members * fields * tiles * rows, LANES)
    flat_back = back_ref.reshape(members * fields * rows, LANES)
    tile_id = first_tile + tile_stride * pl.program_id(0)
    row0 = (start_ref[0] + tile_id * rows).astype(jnp.float32)
    lane = lax.broadcasted_iota(jnp.int32, (1, LANES), 1).astype(jnp.float32)

    def contribution(b, k, t):
        first = k * OBS_BLOCK
        if not isinstance(k, int):
            first = pl.multiple_of(first, OBS_BLOCK)
        part = pl.ds(first, OBS_BLOCK)
        obs_x = place_ref[b, part, :LANES]
        obs_y = place_ref[b, part, LANES:]
        col0 = (start_ref[1] + t * LANES).astype(jnp.float32)
        dist_y = apart_sq(obs_y, lane + col0, size_y)
        weights = []
        for r in range(rows):
            radius = cutoff_ref[r : r + 1, t * LANES : (t + 1) * LANES].astype(jnp.float32)
            ratio = (dist_y + apart_sq(obs_x, row0 + r, size_x)) * (1.0 / (radius * radius))
            weights.append(jnp.square(jnp.maximum(1.0 - ratio, 0.0)))
        weights = jnp.concatenate(weights, 1)
        cross = jnp.dot(
            lhs1_ref[b, part, :], rhs_ref[...], preferred_element_type=jnp.float32
        )
        gain = cross * jnp.concatenate([weights] * fields, 1)
        high, low = split_bf16(gain)
        return jnp.dot(
            lhs2_ref[b, k],
            jnp.concatenate([high, low, high], 0),
            preferred_element_type=jnp.float32,
        )

    for t in range(tiles):
        for f in range(fields):
            for r in range(rows):
                place = f * cells + r * LANES
                members_ref[:, place : place + LANES] = flat[
                    pl.ds((f * tiles + t) * rows + r, members, stride=fields * tiles * rows), :
                ]
        for b in range(batches):
            state = members_ref[...]
            high, low = split_bf16(state - jnp.mean(state, 0, keepdims=True))
            rhs_ref[...] = jnp.concatenate([high, low, high], 0)
            members_ref[...] = state + contribution(b, 0, t)

            def more(k, _):
                members_ref[...] += contribution(b, k, t)
                return 0

            blocks = (count_ref[b] + (OBS_BLOCK - 1)) // OBS_BLOCK
            lax.fori_loop(1, blocks, more, 0)
        for f in range(fields):
            for r in range(rows):
                place = f * cells + r * LANES
                flat_back[pl.ds(f * rows + r, members, stride=fields * rows), :] = members_ref[
                    :, place : place + LANES
                ]
        out_ref[:, :, :, t * LANES : (t + 1) * LANES] = back_ref[...]


def update(start, counts, state, cutoff, lhs1, lhs2, place, sizes, row_tiles, begun=None):
    members, fields, tiles, _, _ = state.shape
    rows = cutoff.shape[0]
    columns = tiles * LANES
    width = fields * ROW_TILE * LANES
    first, stride = row_tiles[0], row_tiles[1] - row_tiles[0]

    def whole(array):
        return pl.BlockSpec(array.shape, lambda i: (0,) * array.ndim)

    operands = [start, counts, state, cutoff, lhs1, lhs2, place]
    in_specs = smem(2) + [
        pl.BlockSpec((members, fields, tiles, ROW_TILE, LANES), lambda i: (0, 0, 0, i, 0)),
        pl.BlockSpec((ROW_TILE, columns), lambda i: (first + stride * i, 0)),
        whole(lhs1),
        whole(lhs2),
        whole(place),
    ]
    aliases = {}
    if begun is not None:
        aliases = {len(operands): 0}
        operands.append(begun)
        in_specs.append(pl.BlockSpec(memory_space=pl.ANY))
    return pl.pallas_call(
        functools.partial(update_kernel, sizes, first, stride, begun is not None),
        grid=(len(row_tiles),),
        in_specs=in_specs,
        out_specs=pl.BlockSpec(
            (members, fields, ROW_TILE, columns), lambda i: (0, 0, first + stride * i, 0)
        ),
        out_shape=jax.ShapeDtypeStruct((members, fields, rows, columns), jnp.float32),
        scratch_shapes=[
            pltpu.VMEM((members, width), jnp.float32),
            pltpu.VMEM((3 * members, width), jnp.bfloat16),
            pltpu.VMEM((members, fields, ROW_TILE, LANES), jnp.float32),
        ],
        input_output_aliases=aliases,
        compiler_params=params(),
        name="update",
    )(*operands)


def row_halos(block, axis):
    size = lax.axis_size(axis)
    onward = [(i, (i + 1) % size) for i in range(size)]
    backward = [(j, i) for i, j in onward]
    rows = block.shape[-2]
    last = lax.slice_in_dim(block, rows - HALO, rows, axis=block.ndim - 2)
    leading = lax.slice_in_dim(block, 0, HALO, axis=block.ndim - 2)
    return lax.ppermute(last, axis, onward), lax.ppermute(leading, axis, backward)


def local(ensemble, sea_depth, cutoff, obs_index, obs_value, obs_var):
    blocks = lax.axis_size("mem")
    members, fields, rows, size_y = ensemble.shape
    col_block = size_y // blocks
    size_x = rows * lax.axis_size("sub")
    sizes = (size_x, size_y)
    x_start = lax.axis_index("sub") * rows
    y_start = lax.axis_index("mem") * col_block
    start = jnp.stack([x_start, y_start]).astype(jnp.int32)
    obs_x = obs_index // size_y
    obs_y = obs_index % size_y
    flat_x = obs_x.reshape(-1)
    flat_y = obs_y.reshape(-1)

    up, down = row_halos(ensemble, "sub")
    depth_up, depth_down = row_halos(sea_depth, "sub")
    radius_part = pick_radius(cutoff, flat_x, flat_y, x_start, y_start)
    begin = jnp.pad(radius_part[None, :], ((members, -(members + 1) % 8), (0, 0)))
    tiles = col_block // LANES
    inner_list, outer_list, list_counts = list_observations(
        (members, tiles, rows), start, flat_x, flat_y
    )

    sent_inner = forecast(
        inner_kernel, "inner", rows - 2 * HALO, sea_depth, blocks, ensemble
    )
    received_inner = lax.all_to_all(
        sent_inner, "mem", split_axis=0, concat_axis=0, tiled=True
    )
    part = pick_heights(0, inner_list, list_counts, sent_inner, begin)

    depth = jnp.concatenate([depth_up, sea_depth, depth_down], 0)
    sent_outer = forecast(outer_kernel, "outer", 2 * HALO, depth, blocks, ensemble, up, down)
    part = pick_heights(1, outer_list, list_counts, sent_outer, part)
    every = gather_over(sum_over(part, "sub")[None], "mem")
    every, sent_outer = lax.optimization_barrier((every, sent_outer))
    received_outer = lax.all_to_all(
        sent_outer, "mem", split_axis=0, concat_axis=0, tiled=True
    )
    heights = every[:, :members].reshape(blocks * members, -1)
    radius_sq = jnp.sum(every[:, members], 0)[None, :]
    lhs1, lhs2, place, counts = chain(
        start, heights, radius_sq, obs_x, obs_y, obs_value, obs_var, cutoff, sizes
    )

    def analyse(received, row_tiles, begun=None):
        state = received.reshape((blocks * members,) + received.shape[2:])
        return update(
            start, counts, state, cutoff, lhs1, lhs2, place, sizes, row_tiles, begun
        )

    row_tiles = list(range(rows // ROW_TILE))
    done = analyse(received_inner, row_tiles[1:-1])
    return analyse(received_outer, [row_tiles[0], row_tiles[-1]], done)


def solution(mesh):
    return jax.shard_map(
        local,
        mesh=mesh,
        in_specs=(P("mem", None, "sub", None), P("sub", None), P("sub", "mem"), P(), P(), P()),
        out_specs=P(None, None, "sub", "mem"),
        check_vma=False,
    )
```

```python
import functools

import jax
import jax.numpy as jnp
from jax import lax
from jax.experimental import pallas as pl
from jax.experimental.pallas import tpu as pltpu
from jax.sharding import PartitionSpec as P

STEPS = 4
HALO = 2 * STEPS
LANES = 128
OBS_BLOCK = 64
ROW_TILE = 8
VMEM_LIMIT = 48 * 2**20

step_size = 0.3
coriolis = 0.2
highest = lax.Precision.HIGHEST

NT = (((1,), (1,)), ((), ()))
TN = (((0,), (0,)), ((), ()))


def params():
    return pltpu.CompilerParams(vmem_limit_bytes=VMEM_LIMIT)


def vmem(count=1):
    return [pl.BlockSpec(memory_space=pltpu.VMEM)] * count


def smem(count=1):
    return [pl.BlockSpec(memory_space=pltpu.SMEM)] * count


def split_bf16(value):
    high = value.astype(jnp.bfloat16)
    low = (value - high.astype(jnp.float32)).astype(jnp.bfloat16)
    return high, low


def centred(field, axis):
    length = field.shape[axis]
    return pltpu.roll(field, length - 1, axis) - pltpu.roll(field, 1, axis)


def forecast_steps(window, depth):
    height, east, north = window
    half = 0.5 * step_size
    turn = step_size * coriolis
    for _ in range(STEPS):
        east_new = east + turn * north - half * centred(height, 0)
        north_new = north - turn * east - half * centred(height, 1)
        height = height - half * (centred(depth * east_new, 0) + centred(depth * north_new, 1))
        east, north = east_new, north_new
    return height, east, north


def send_rows(out_ref, fields, first_row):
    blocks, _, _, tiles, rows, _ = out_ref.shape
    for f, field in enumerate(fields):
        for d in range(blocks):
            for t in range(tiles):
                first = (d * tiles + t) * LANES
                out_ref[d, 0, f, t] = field[
                    first_row : first_row + rows, first : first + LANES
                ]


def near_kernel(parity_ref, ens_ref, halo_ref, depth_ref, depth_halo_ref, out_ref):
    odd = parity_ref[0] == 1

    def window(block, halo):
        return jnp.where(
            odd, jnp.concatenate([halo, block], 0), jnp.concatenate([block, halo], 0)
        )

    fields = [window(ens_ref[0, f], halo_ref[f]) for f in range(3)]
    done = forecast_steps(fields, window(depth_ref[...], depth_halo_ref[0]))
    send_rows(out_ref, done, HALO)


def far_kernel(parity_ref, ens_ref, halo_ref, depth_ref, depth_halo_ref, out_ref):
    odd = parity_ref[0] == 1
    rows = depth_ref.shape[0]

    def window(block, halo):
        return jnp.where(
            odd,
            jnp.concatenate([block[rows - 2 * HALO :], halo], 0),
            jnp.concatenate([halo, block[: 2 * HALO]], 0),
        )

    fields = [window(ens_ref[0, f], halo_ref[f]) for f in range(3)]
    done = forecast_steps(fields, window(depth_ref[...], depth_halo_ref[0]))
    send_rows(out_ref, done, HALO)


def forecast(kernel, name, out_rows, parity, ensemble, halo, depth, blocks):
    members, fields, rows, columns = ensemble.shape
    tiles = columns // blocks // LANES
    return pl.pallas_call(
        kernel,
        grid=(members,),
        in_specs=smem()
        + [
            pl.BlockSpec((1, fields, rows, columns), lambda m: (m, 0, 0, 0)),
            pl.BlockSpec((fields, HALO, columns), lambda m: (m, 0, 0)),
            pl.BlockSpec((rows, columns), lambda m: (0, 0)),
            pl.BlockSpec((1, HALO, columns), lambda m: (members * fields, 0, 0)),
        ],
        out_specs=pl.BlockSpec(
            (blocks, 1, fields, tiles, out_rows, LANES), lambda m: (0, m, 0, 0, 0, 0)
        ),
        out_shape=jax.ShapeDtypeStruct(
            (blocks, members, fields, tiles, out_rows, LANES), jnp.float32
        ),
        compiler_params=params(),
        name=name,
    )(parity, ensemble, halo, depth, halo)


def pick(row_ref, col_ref, height_ref):
    blocks, members, _, tiles, rows, _ = height_ref.shape
    heights = jnp.concatenate(
        [
            height_ref[d, :, 0, t].reshape(members * rows, LANES)
            for d in range(blocks)
            for t in range(tiles)
        ],
        1,
    )
    high, rest = heights.astype(jnp.bfloat16), heights
    pieces = [high]
    for _ in range(2):
        rest = rest - pieces[-1].astype(jnp.float32)
        pieces.append(rest.astype(jnp.bfloat16))
    count = col_ref.shape[1]
    column = lax.broadcasted_iota(jnp.int32, (heights.shape[1], count), 0)
    in_column = (column == col_ref[...]).astype(jnp.float32).astype(jnp.bfloat16)
    found = jnp.dot(
        jnp.concatenate(pieces, 0), in_column, preferred_element_type=jnp.float32
    )
    size = members * rows
    found = (found[:size] + found[size : 2 * size]) + found[2 * size :]
    found = found.reshape(members, rows, count)
    row = lax.broadcasted_iota(jnp.int32, (1, rows, count), 1)
    return jnp.sum(jnp.where(row == row_ref[...][None], found, 0.0), 1)


def pick_near_kernel(row_ref, col_ref, height_ref, out_ref):
    out_ref[...] = pick(row_ref, col_ref, height_ref)


def pick_far_kernel(row_ref, col_ref, height_ref, near_ref, radius_ref, out_ref):
    heights = pick(row_ref, col_ref, height_ref) + near_ref[...]
    members, count = heights.shape
    pieces = out_ref.shape[0]
    groups = count // pieces // LANES
    out_ref[...] = jnp.zeros_like(out_ref)
    for j in range(pieces):
        for g in range(groups):
            part = slice((j * groups + g) * LANES, (j * groups + g + 1) * LANES)
            for m in range(members):
                row = m * groups + g
                out_ref[j, row : row + 1, :] = heights[m : m + 1, part]
            row = members * groups + g
            out_ref[j, row : row + 1, :] = radius_ref[:, part]


def height_spec(sent):
    blocks, members, _, tiles, rows, _ = sent.shape
    return pl.BlockSpec((blocks, members, 1, tiles, rows, LANES), lambda i: (0,) * 6)


def whole_spec(shape):
    return pl.BlockSpec(shape, lambda i: (0,) * len(shape))


def pick_near(row, col, sent):
    shape = (sent.shape[1], col.shape[1])
    return pl.pallas_call(
        pick_near_kernel,
        grid=(1,),
        in_specs=[whole_spec(row.shape), whole_spec(col.shape), height_spec(sent)],
        out_specs=whole_spec(shape),
        out_shape=jax.ShapeDtypeStruct(shape, jnp.float32),
        compiler_params=params(),
        name="pick_near",
    )(row, col, sent)


def pick_far(row, col, sent, near, radius, pieces):
    members, count = near.shape
    used = (members + 1) * (count // pieces // LANES)
    shape = (pieces, used + -used % 8, LANES)
    return pl.pallas_call(
        pick_far_kernel,
        grid=(1,),
        in_specs=[
            whole_spec(row.shape),
            whole_spec(col.shape),
            height_spec(sent),
            whole_spec(near.shape),
            whole_spec(radius.shape),
        ],
        out_specs=whole_spec(shape),
        out_shape=jax.ShapeDtypeStruct(shape, jnp.float32),
        compiler_params=params(),
        name="pick_far",
    )(row, col, sent, near, radius)


def pick_radius(cutoff, obs_x, obs_y, x_start, y_start):
    rows, columns = cutoff.shape
    radius_sq = jnp.square(cutoff.astype(jnp.float32))
    row_is = (obs_x[:, None] - x_start == jnp.arange(rows)[None, :]).astype(jnp.float32)
    col_is = obs_y[:, None] - y_start == jnp.arange(columns)[None, :]
    by_row = jnp.dot(row_is, radius_sq, precision=highest)
    return jnp.sum(jnp.where(col_is, by_row, 0.0), 1)


def exchange(value, axis, distance):
    size = lax.axis_size(axis)
    return lax.ppermute(value, axis, [(i, i ^ distance) for i in range(size)])


def sum_over(value, axis):
    distance = 1
    while distance < lax.axis_size(axis):
        value = value + exchange(value, axis, distance)
        distance *= 2
    return value


def gather_over(value, axis):
    distance = 1
    while distance < lax.axis_size(axis):
        value = jnp.concatenate([value, exchange(value, axis, distance)], 0)
        distance *= 2
    return value


def apart_sq(a, b, size):
    gap = jnp.abs(a - b)
    gap = jnp.minimum(gap, size - gap)
    return gap * gap


def chain_kernel(
    members,
    sizes,
    start_ref,
    every_ref,
    row_ref,
    col_ref,
    value_ref,
    variance_ref,
    cutoff_ref,
    lhs1_ref,
    lhs2_ref,
    place_ref,
    count_ref,
):
    size_x, size_y = sizes
    pieces, sources, _, _ = every_ref.shape
    batches, count = value_ref.shape
    groups = batches * count // pieces // LANES
    local_members = members // sources
    rows, columns = cutoff_ref.shape
    x_start = start_ref[0]
    y_start = start_ref[1]
    reach = jnp.max(cutoff_ref[...])
    reach_sq = reach * reach

    heights, radius_sq = [], []
    for j in range(pieces):
        piece = jnp.bitwise_xor(start_ref[2], j)
        for g in range(groups):
            found, radius = [], 0.0
            for source in range(sources):
                one = every_ref.at[piece, jnp.bitwise_xor(start_ref[3], source)]
                found += [
                    one[m * groups + g : m * groups + g + 1, :] for m in range(local_members)
                ]
                last = local_members * groups + g
                radius = radius + one[last : last + 1, :]
            heights.append(jnp.concatenate(found, 0))
            radius_sq.append(radius)
    heights = jnp.concatenate(heights, 1)
    radius_sq = jnp.concatenate(radius_sq, 1)
    before = (
        lax.broadcasted_iota(jnp.int32, (count, count), 0)
        <= lax.broadcasted_iota(jnp.int32, (count, count), 1)
    ).astype(jnp.bfloat16)
    slot = lax.broadcasted_iota(jnp.int32, (count, count), 0)
    member_row = lax.broadcasted_iota(jnp.int32, (members, LANES + count), 0)
    eye = (
        lax.broadcasted_iota(jnp.int32, (members, members), 0)
        == lax.broadcasted_iota(jnp.int32, (members, members), 1)
    ).astype(jnp.float32)

    for b in range(batches):
        here = slice(b * count, (b + 1) * count)
        prior = heights[:, here]
        mean = jnp.mean(prior, 0, keepdims=True)
        anom = prior - mean
        precision = 1.0 / variance_ref[b : b + 1, :]
        innov = value_ref[b : b + 1, :] - mean
        scaled = anom * precision
        inner = eye + lax.dot_general(
            scaled, anom, NT, precision=highest, preferred_element_type=jnp.float32
        ) / (members - 1)
        proj = jnp.sum(scaled * innov, 1, keepdims=True)
        system = jnp.concatenate(
            [inner, proj, jnp.zeros((members, LANES - members - 1), jnp.float32), scaled], 1
        )
        for k in range(members):
            pivot_row = system[k : k + 1, :] / system[k : k + 1, k : k + 1]
            system = jnp.where(
                member_row == k, pivot_row, system - system[:, k : k + 1] * pivot_row
            )
        solved_proj = system[:, members : members + 1]
        solved_anom = system[:, LANES:]
        solved_innov = precision * (
            innov - jnp.sum(anom * solved_proj, 0, keepdims=True) / (members - 1)
        )
        mix = (solved_innov - 0.5 * solved_anom) / (members - 1)

        obs_x = row_ref[0:1, here]
        obs_y = row_ref[1:2, here]
        off_x = jnp.where(obs_x >= x_start, obs_x - x_start, obs_x - x_start + size_x)
        off_y = jnp.where(obs_y >= y_start, obs_y - y_start, obs_y - y_start + size_y)
        gap_x = jnp.where(off_x < rows, 0, jnp.minimum(off_x - (rows - 1), size_x - off_x))
        gap_y = jnp.where(off_y < columns, 0, jnp.minimum(off_y - (columns - 1), size_y - off_y))
        reaches = gap_x * gap_x + gap_y * gap_y < reach_sq
        flags = jnp.broadcast_to(reaches.astype(jnp.float32), (8, count))
        ranks = jnp.dot(
            flags.astype(jnp.bfloat16), before, preferred_element_type=jnp.float32
        )
        rank = jnp.where(reaches, ranks[0:1, :].astype(jnp.int32) - 1, -1)
        chosen = (slot == rank).astype(jnp.float32)
        count_ref[b] = jnp.sum(flags[0:1, :]).astype(jnp.int32)

        near_anom = lax.dot_general(
            chosen, anom, NT, precision=highest, preferred_element_type=jnp.float32
        )
        high, low = split_bf16(near_anom)
        lhs1_ref[b] = jnp.concatenate([high, high, low], 1)
        near_mix = lax.dot_general(
            mix, chosen, NT, precision=highest, preferred_element_type=jnp.float32
        )
        high, low = split_bf16(near_mix)
        for k in range(count // OBS_BLOCK):
            part = slice(k * OBS_BLOCK, (k + 1) * OBS_BLOCK)
            lhs2_ref[b, k] = jnp.concatenate([high[:, part], high[:, part], low[:, part]], 1)
        where = jnp.concatenate(
            [
                jnp.broadcast_to(obs_x, (LANES, count)),
                jnp.broadcast_to(obs_y, (LANES, count)),
            ],
            0,
        ).astype(jnp.float32)
        place_ref[b] = lax.dot_general(
            chosen, where, NT, precision=highest, preferred_element_type=jnp.float32
        )

        if b + 1 < batches:
            later = slice((b + 1) * count, batches * count)
            ahead = heights[:, later]
            ahead_anom = ahead - jnp.mean(ahead, 0, keepdims=True)
            cross = lax.dot_general(
                anom, ahead_anom, TN, precision=highest, preferred_element_type=jnp.float32
            )
            dist_sq = apart_sq(col_ref[:, b : b + 1], row_ref[0:1, later], size_x) + apart_sq(
                col_ref[:, batches + b : batches + b + 1], row_ref[1:2, later], size_y
            )
            ratio = dist_sq.astype(jnp.float32) / radius_sq[:, later]
            gain = cross * jnp.square(jnp.maximum(1.0 - ratio, 0.0))
            ahead = ahead + jnp.dot(
                mix, gain, precision=highest, preferred_element_type=jnp.float32
            )
            heights = jnp.concatenate([heights[:, : (b + 1) * count], ahead], 1)


def chain(members, start, every, obs_x, obs_y, values, variance, cutoff, sizes):
    batches, count = values.shape
    row_form = jnp.stack([obs_x.reshape(-1), obs_y.reshape(-1)], 0)
    col_form = jnp.concatenate([obs_x, obs_y], 0).T
    return pl.pallas_call(
        functools.partial(chain_kernel, members, sizes),
        in_specs=smem() + vmem(6),
        out_specs=vmem(3) + smem(),
        out_shape=[
            jax.ShapeDtypeStruct((batches, count, 3 * members), jnp.bfloat16),
            jax.ShapeDtypeStruct(
                (batches, count // OBS_BLOCK, members, 3 * OBS_BLOCK), jnp.bfloat16
            ),
            jax.ShapeDtypeStruct((batches, count, 2 * LANES), jnp.float32),
            jax.ShapeDtypeStruct((batches,), jnp.int32),
        ],
        compiler_params=params(),
        name="chain",
    )(start, every, row_form, col_form, values, variance, cutoff)


def update_kernel(
    sizes,
    continues,
    tile_ref,
    start_ref,
    count_ref,
    state_ref,
    cutoff_ref,
    lhs1_ref,
    lhs2_ref,
    place_ref,
    *rest,
):
    out_ref, members_ref, rhs_ref, back_ref = rest[1:] if continues else rest
    size_x, size_y = float(sizes[0]), float(sizes[1])
    members, fields, tiles, rows, _ = state_ref.shape
    batches = lhs1_ref.shape[0]
    cells = rows * LANES
    flat = state_ref.reshape(members * fields * tiles * rows, LANES)
    flat_back = back_ref.reshape(members * fields * rows, LANES)
    row0 = (start_ref[0] + tile_ref[pl.program_id(0)] * rows).astype(jnp.float32)
    lane = lax.broadcasted_iota(jnp.int32, (1, LANES), 1).astype(jnp.float32)

    def contribution(b, k, t):
        first = k * OBS_BLOCK
        if not isinstance(k, int):
            first = pl.multiple_of(first, OBS_BLOCK)
        part = pl.ds(first, OBS_BLOCK)
        obs_x = place_ref[b, part, :LANES]
        obs_y = place_ref[b, part, LANES:]
        col0 = (start_ref[1] + t * LANES).astype(jnp.float32)
        dist_y = apart_sq(obs_y, lane + col0, size_y)
        weights = []
        for r in range(rows):
            radius = cutoff_ref[r : r + 1, t * LANES : (t + 1) * LANES].astype(jnp.float32)
            ratio = (dist_y + apart_sq(obs_x, row0 + r, size_x)) * (1.0 / (radius * radius))
            weights.append(jnp.square(jnp.maximum(1.0 - ratio, 0.0)))
        weights = jnp.concatenate(weights, 1)
        cross = jnp.dot(
            lhs1_ref[b, part, :], rhs_ref[...], preferred_element_type=jnp.float32
        )
        gain = cross * jnp.concatenate([weights] * fields, 1)
        high, low = split_bf16(gain)
        return jnp.dot(
            lhs2_ref[b, k],
            jnp.concatenate([high, low, high], 0),
            preferred_element_type=jnp.float32,
        )

    for t in range(tiles):
        for f in range(fields):
            for r in range(rows):
                place = f * cells + r * LANES
                members_ref[:, place : place + LANES] = flat[
                    pl.ds((f * tiles + t) * rows + r, members, stride=fields * tiles * rows), :
                ]
        for b in range(batches):
            state = members_ref[...]
            high, low = split_bf16(state - jnp.mean(state, 0, keepdims=True))
            rhs_ref[...] = jnp.concatenate([high, low, high], 0)
            members_ref[...] = state + contribution(b, 0, t)

            def more(k, _):
                members_ref[...] += contribution(b, k, t)
                return 0

            blocks = (count_ref[b] + (OBS_BLOCK - 1)) // OBS_BLOCK
            lax.fori_loop(1, blocks, more, 0)
        for f in range(fields):
            for r in range(rows):
                place = f * cells + r * LANES
                flat_back[pl.ds(f * rows + r, members, stride=fields * rows), :] = members_ref[
                    :, place : place + LANES
                ]
        out_ref[:, :, :, t * LANES : (t + 1) * LANES] = back_ref[...]


def update(row_tiles, start, counts, state, cutoff, lhs1, lhs2, place, sizes, begun=None):
    members, fields, tiles, _, _ = state.shape
    rows = cutoff.shape[0]
    columns = tiles * LANES
    width = fields * ROW_TILE * LANES

    def whole(array):
        return pl.BlockSpec(array.shape, lambda i, tile: (0,) * array.ndim)

    operands = [row_tiles, start, counts, state, cutoff, lhs1, lhs2, place]
    in_specs = smem(2) + [
        pl.BlockSpec(
            (members, fields, tiles, ROW_TILE, LANES), lambda i, tile: (0, 0, 0, i, 0)
        ),
        pl.BlockSpec((ROW_TILE, columns), lambda i, tile: (tile[i], 0)),
        whole(lhs1),
        whole(lhs2),
        whole(place),
    ]
    aliases = {}
    if begun is not None:
        aliases = {len(operands): 0}
        operands.append(begun)
        in_specs.append(pl.BlockSpec(memory_space=pl.ANY))
    return pl.pallas_call(
        functools.partial(update_kernel, sizes, begun is not None),
        grid_spec=pltpu.PrefetchScalarGridSpec(
            num_scalar_prefetch=1,
            grid=row_tiles.shape,
            in_specs=in_specs,
            out_specs=pl.BlockSpec(
                (members, fields, ROW_TILE, columns), lambda i, tile: (0, 0, tile[i], 0)
            ),
            scratch_shapes=[
                pltpu.VMEM((members, width), jnp.float32),
                pltpu.VMEM((3 * members, width), jnp.bfloat16),
                pltpu.VMEM((members, fields, ROW_TILE, LANES), jnp.float32),
            ],
        ),
        out_shape=jax.ShapeDtypeStruct((members, fields, rows, columns), jnp.float32),
        input_output_aliases=aliases,
        compiler_params=params(),
        name="update",
    )(*operands)


def row_halos(ensemble, depth, axis):
    size = lax.axis_size(axis)
    odd = lax.axis_index(axis) % 2 == 1
    columns = depth.shape[1]

    def edge(start):
        return jnp.concatenate(
            [
                ensemble[:, :, start : start + HALO].reshape(-1, HALO, columns),
                depth[None, start : start + HALO],
            ],
            0,
        )

    first, last = edge(0), edge(depth.shape[0] - HALO)
    far = [(i, (i + (1 if i % 2 else -1)) % size) for i in range(size)]
    return (
        exchange(jnp.where(odd, first, last), axis, 1),
        lax.ppermute(jnp.where(odd, last, first), axis, far),
    )


def local(ensemble, sea_depth, cutoff, obs_index, obs_value, obs_var):
    blocks = lax.axis_size("mem")
    subs = lax.axis_size("sub")
    local_members, fields, rows, size_y = ensemble.shape
    members = local_members * blocks
    col_block = size_y // blocks
    size_x = rows * subs
    sizes = (size_x, size_y)
    sub, mem = lax.axis_index("sub"), lax.axis_index("mem")
    odd = sub % 2
    x_start = sub * rows
    y_start = mem * col_block
    start = jnp.stack([x_start, y_start, sub, mem]).astype(jnp.int32)
    parity = odd.astype(jnp.int32)[None]
    obs_x = obs_index // size_y
    obs_y = obs_index % size_y
    flat_x = obs_x.reshape(1, -1)
    flat_y = obs_y.reshape(1, -1)

    near_halo, far_halo = row_halos(ensemble, sea_depth, "sub")
    radius_part = pick_radius(cutoff, flat_x[0], flat_y[0], x_start, y_start)[None]
    near_first = jnp.where(odd == 1, 0, HALO)
    far_first = jnp.where(odd == 1, rows - HALO, 0)

    sent_near = forecast(
        near_kernel, "near", rows - HALO, parity, ensemble, near_halo, sea_depth, blocks
    )
    received_near = lax.all_to_all(sent_near, "mem", split_axis=0, concat_axis=0, tiled=True)
    near_heights = pick_near(flat_x - x_start - near_first, flat_y, sent_near)

    sent_far = forecast(far_kernel, "far", HALO, parity, ensemble, far_halo, sea_depth, blocks)
    part = pick_far(
        flat_x - x_start - far_first, flat_y, sent_far, near_heights, radius_part, subs
    )
    piece = lax.dynamic_index_in_dim(sum_over(part, "sub"), sub, 0, keepdims=True)
    every = gather_over(gather_over(piece, "mem")[None], "sub")
    lhs1, lhs2, place, counts = chain(
        members, start, every, obs_x, obs_y, obs_value, obs_var, cutoff, sizes
    )
    received_far = lax.all_to_all(sent_far, "mem", split_axis=0, concat_axis=0, tiled=True)

    def analyse(received, row_tiles, begun=None):
        state = received.reshape((members,) + received.shape[2:])
        return update(
            row_tiles, start, counts, state, cutoff, lhs1, lhs2, place, sizes, begun
        )

    near_tiles = near_first // ROW_TILE + jnp.arange(rows // ROW_TILE - 1, dtype=jnp.int32)
    far_tiles = (far_first // ROW_TILE).astype(jnp.int32)[None]
    return analyse(received_far, far_tiles, analyse(received_near, near_tiles))


def solution(mesh):
    return jax.shard_map(
        local,
        mesh=mesh,
        in_specs=(P("mem", None, "sub", None), P("sub", None), P("sub", "mem"), P(), P(), P()),
        out_specs=P(None, None, "sub", "mem"),
        check_vma=False,
    )
```

```python
import functools

import jax
import jax.numpy as jnp
from jax import lax
from jax.experimental import pallas as pl
from jax.experimental.pallas import tpu as pltpu
from jax.sharding import PartitionSpec as P

STEPS = 4
HALO = 2 * STEPS
LANES = 128
OBS_BLOCK = 64
ROW_TILE = 8
VMEM_LIMIT = 48 * 2**20
CHAIN_COST = pl.CostEstimate(flops=26 * 10**9, bytes_accessed=85 * 10**6, transcendentals=0)

step_size = 0.3
coriolis = 0.2
highest = lax.Precision.HIGHEST

NT = (((1,), (1,)), ((), ()))
TN = (((0,), (0,)), ((), ()))


def params():
    return pltpu.CompilerParams(vmem_limit_bytes=VMEM_LIMIT)


def vmem(count=1):
    return [pl.BlockSpec(memory_space=pltpu.VMEM)] * count


def smem(count=1):
    return [pl.BlockSpec(memory_space=pltpu.SMEM)] * count


def split_bf16(value):
    high = value.astype(jnp.bfloat16)
    low = (value - high.astype(jnp.float32)).astype(jnp.bfloat16)
    return high, low


def centred(field, axis):
    length = field.shape[axis]
    return pltpu.roll(field, length - 1, axis) - pltpu.roll(field, 1, axis)


def forecast_steps(window, depth):
    height, east, north = window
    half = 0.5 * step_size
    turn = step_size * coriolis
    for _ in range(STEPS):
        east_new = east + turn * north - half * centred(height, 0)
        north_new = north - turn * east - half * centred(height, 1)
        height = height - half * (centred(depth * east_new, 0) + centred(depth * north_new, 1))
        east, north = east_new, north_new
    return height, east, north


def send_rows(out_ref, fields, first_row):
    blocks, _, _, tiles, rows, _ = out_ref.shape
    for f, field in enumerate(fields):
        for d in range(blocks):
            for t in range(tiles):
                first = (d * tiles + t) * LANES
                out_ref[d, 0, f, t] = field[
                    first_row : first_row + rows, first : first + LANES
                ]


def near_kernel(parity_ref, ens_ref, halo_ref, depth_ref, depth_halo_ref, out_ref):
    odd = parity_ref[0] == 1

    def window(block, halo):
        return jnp.where(
            odd, jnp.concatenate([halo, block], 0), jnp.concatenate([block, halo], 0)
        )

    fields = [window(ens_ref[0, f], halo_ref[f]) for f in range(3)]
    done = forecast_steps(fields, window(depth_ref[...], depth_halo_ref[0]))
    send_rows(out_ref, done, HALO)


def far_kernel(parity_ref, ens_ref, halo_ref, depth_ref, depth_halo_ref, out_ref):
    odd = parity_ref[0] == 1
    rows = depth_ref.shape[0]

    def window(block, halo):
        return jnp.where(
            odd,
            jnp.concatenate([block[rows - 2 * HALO :], halo], 0),
            jnp.concatenate([halo, block[: 2 * HALO]], 0),
        )

    fields = [window(ens_ref[0, f], halo_ref[f]) for f in range(3)]
    done = forecast_steps(fields, window(depth_ref[...], depth_halo_ref[0]))
    send_rows(out_ref, done, HALO)


def forecast(kernel, name, out_rows, parity, ensemble, halo, depth, blocks):
    members, fields, rows, columns = ensemble.shape
    tiles = columns // blocks // LANES
    return pl.pallas_call(
        kernel,
        grid=(members,),
        in_specs=smem()
        + [
            pl.BlockSpec((1, fields, rows, columns), lambda m: (m, 0, 0, 0)),
            pl.BlockSpec((fields, HALO, columns), lambda m: (m, 0, 0)),
            pl.BlockSpec((rows, columns), lambda m: (0, 0)),
            pl.BlockSpec((1, HALO, columns), lambda m: (members * fields, 0, 0)),
        ],
        out_specs=pl.BlockSpec(
            (blocks, 1, fields, tiles, out_rows, LANES), lambda m: (0, m, 0, 0, 0, 0)
        ),
        out_shape=jax.ShapeDtypeStruct(
            (blocks, members, fields, tiles, out_rows, LANES), jnp.float32
        ),
        compiler_params=params(),
        name=name,
    )(parity, ensemble, halo, depth, halo)


def pick(row_ref, col_ref, height_ref):
    blocks, members, _, tiles, rows, _ = height_ref.shape
    heights = jnp.concatenate(
        [
            height_ref[d, :, 0, t].reshape(members * rows, LANES)
            for d in range(blocks)
            for t in range(tiles)
        ],
        1,
    )
    high, rest = heights.astype(jnp.bfloat16), heights
    pieces = [high]
    for _ in range(2):
        rest = rest - pieces[-1].astype(jnp.float32)
        pieces.append(rest.astype(jnp.bfloat16))
    count = col_ref.shape[1]
    column = lax.broadcasted_iota(jnp.int32, (heights.shape[1], count), 0)
    in_column = (column == col_ref[...]).astype(jnp.float32).astype(jnp.bfloat16)
    found = jnp.dot(
        jnp.concatenate(pieces, 0), in_column, preferred_element_type=jnp.float32
    )
    size = members * rows
    found = (found[:size] + found[size : 2 * size]) + found[2 * size :]
    found = found.reshape(members, rows, count)
    row = lax.broadcasted_iota(jnp.int32, (1, rows, count), 1)
    return jnp.sum(jnp.where(row == row_ref[...][None], found, 0.0), 1)


def pick_near_kernel(row_ref, col_ref, height_ref, out_ref):
    out_ref[...] = pick(row_ref, col_ref, height_ref)


def pick_far_kernel(row_ref, col_ref, height_ref, near_ref, radius_ref, out_ref):
    heights = pick(row_ref, col_ref, height_ref) + near_ref[...]
    members, count = heights.shape
    pieces = out_ref.shape[0]
    groups = count // pieces // LANES
    out_ref[...] = jnp.zeros_like(out_ref)
    for j in range(pieces):
        for g in range(groups):
            part = slice((j * groups + g) * LANES, (j * groups + g + 1) * LANES)
            for m in range(members):
                row = m * groups + g
                out_ref[j, row : row + 1, :] = heights[m : m + 1, part]
            row = members * groups + g
            out_ref[j, row : row + 1, :] = radius_ref[:, part]


def height_spec(sent):
    blocks, members, _, tiles, rows, _ = sent.shape
    return pl.BlockSpec((blocks, members, 1, tiles, rows, LANES), lambda i: (0,) * 6)


def whole_spec(shape):
    return pl.BlockSpec(shape, lambda i: (0,) * len(shape))


def pick_near(row, col, sent):
    shape = (sent.shape[1], col.shape[1])
    return pl.pallas_call(
        pick_near_kernel,
        grid=(1,),
        in_specs=[whole_spec(row.shape), whole_spec(col.shape), height_spec(sent)],
        out_specs=whole_spec(shape),
        out_shape=jax.ShapeDtypeStruct(shape, jnp.float32),
        compiler_params=params(),
        name="pick_near",
    )(row, col, sent)


def pick_far(row, col, sent, near, radius, pieces):
    members, count = near.shape
    used = (members + 1) * (count // pieces // LANES)
    shape = (pieces, used + -used % 8, LANES)
    return pl.pallas_call(
        pick_far_kernel,
        grid=(1,),
        in_specs=[
            whole_spec(row.shape),
            whole_spec(col.shape),
            height_spec(sent),
            whole_spec(near.shape),
            whole_spec(radius.shape),
        ],
        out_specs=whole_spec(shape),
        out_shape=jax.ShapeDtypeStruct(shape, jnp.float32),
        compiler_params=params(),
        name="pick_far",
    )(row, col, sent, near, radius)


def pick_radius(cutoff, obs_x, obs_y, x_start, y_start):
    rows, columns = cutoff.shape
    radius_sq = jnp.square(cutoff.astype(jnp.float32))
    row_is = (obs_x[:, None] - x_start == jnp.arange(rows)[None, :]).astype(jnp.float32)
    col_is = obs_y[:, None] - y_start == jnp.arange(columns)[None, :]
    by_row = jnp.dot(row_is, radius_sq, precision=highest)
    return jnp.sum(jnp.where(col_is, by_row, 0.0), 1)


def exchange(value, axis, distance):
    size = lax.axis_size(axis)
    return lax.ppermute(value, axis, [(i, i ^ distance) for i in range(size)])


def sum_over(value, axis):
    distance = 1
    while distance < lax.axis_size(axis):
        value = value + exchange(value, axis, distance)
        distance *= 2
    return value


def gather_over(value, axis):
    distance = 1
    while distance < lax.axis_size(axis):
        value = jnp.concatenate([value, exchange(value, axis, distance)], 0)
        distance *= 2
    return value


def apart_sq(a, b, size):
    gap = jnp.abs(a - b)
    gap = jnp.minimum(gap, size - gap)
    return gap * gap


def eliminate_four(system, k, row_id):
    width = system.shape[1]
    row = [system[k + i : k + i + 1, :] for i in range(4)]
    p = [
        [jnp.broadcast_to(row[i][:, k + j : k + j + 1], (1, LANES)) for j in range(4)]
        for i in range(4)
    ]

    def wide(value):
        return jnp.concatenate([value] * (width // LANES), 1)

    def inverse(a00, a01, a10, a11):
        scale = 1.0 / (a00 * a11 - a01 * a10)
        return a11 * scale, -a01 * scale, -a10 * scale, a00 * scale

    i00, i01, i10, i11 = inverse(p[0][0], p[0][1], p[1][0], p[1][1])
    y = [
        [i00 * p[0][2 + j] + i01 * p[1][2 + j] for j in range(2)],
        [i10 * p[0][2 + j] + i11 * p[1][2 + j] for j in range(2)],
    ]
    schur = [
        [p[2 + i][2 + j] - p[2 + i][0] * y[0][j] - p[2 + i][1] * y[1][j] for j in range(2)]
        for i in range(2)
    ]
    s00, s01, s10, s11 = inverse(schur[0][0], schur[0][1], schur[1][0], schur[1][1])
    top0 = wide(i00) * row[0] + wide(i01) * row[1]
    top1 = wide(i10) * row[0] + wide(i11) * row[1]
    low0 = row[2] - wide(p[2][0]) * top0 - wide(p[2][1]) * top1
    low1 = row[3] - wide(p[3][0]) * top0 - wide(p[3][1]) * top1
    new2 = wide(s00) * low0 + wide(s01) * low1
    new3 = wide(s10) * low0 + wide(s11) * low1
    new0 = top0 - wide(y[0][0]) * new2 - wide(y[0][1]) * new3
    new1 = top1 - wide(y[1][0]) * new2 - wide(y[1][1]) * new3
    new = (new0, new1, new2, new3)
    result = system
    for i in range(4):
        result = result - system[:, k + i : k + i + 1] * new[i]
    for i in range(4):
        result = jnp.where(row_id == k + i, new[i], result)
    return result


def chain_kernel(
    members,
    sizes,
    start_ref,
    every_ref,
    row_ref,
    col_ref,
    value_ref,
    variance_ref,
    cutoff_ref,
    lhs1_ref,
    lhs2_ref,
    place_ref,
    count_ref,
):
    size_x, size_y = sizes
    pieces, sources, _, _ = every_ref.shape
    batches, count = value_ref.shape
    groups = batches * count // pieces // LANES
    local_members = members // sources
    rows, columns = cutoff_ref.shape
    x_start = start_ref[0]
    y_start = start_ref[1]
    reach = jnp.max(cutoff_ref[...])
    reach_sq = reach * reach

    heights, radius_sq = [], []
    for j in range(pieces):
        piece = jnp.bitwise_xor(start_ref[2], j)
        for g in range(groups):
            found, radius = [], 0.0
            for source in range(sources):
                one = every_ref.at[piece, jnp.bitwise_xor(start_ref[3], source)]
                found += [
                    one[m * groups + g : m * groups + g + 1, :] for m in range(local_members)
                ]
                last = local_members * groups + g
                radius = radius + one[last : last + 1, :]
            heights.append(jnp.concatenate(found, 0))
            radius_sq.append(radius)
    heights = jnp.concatenate(heights, 1)
    radius_sq = jnp.concatenate(radius_sq, 1)
    before = (
        lax.broadcasted_iota(jnp.int32, (count, count), 0)
        <= lax.broadcasted_iota(jnp.int32, (count, count), 1)
    ).astype(jnp.bfloat16)
    slot = lax.broadcasted_iota(jnp.int32, (count, count), 0)
    member_row = lax.broadcasted_iota(jnp.int32, (members, LANES + count), 0)
    eye = (
        lax.broadcasted_iota(jnp.int32, (members, members), 0)
        == lax.broadcasted_iota(jnp.int32, (members, members), 1)
    ).astype(jnp.float32)

    for b in range(batches):
        here = slice(b * count, (b + 1) * count)
        prior = heights[:, here]
        mean = jnp.mean(prior, 0, keepdims=True)
        anom = prior - mean
        precision = 1.0 / variance_ref[b : b + 1, :]
        innov = value_ref[b : b + 1, :] - mean
        scaled = anom * precision
        inner = eye + lax.dot_general(
            scaled, anom, NT, precision=highest, preferred_element_type=jnp.float32
        ) / (members - 1)
        proj = jnp.sum(scaled * innov, 1, keepdims=True)
        system = jnp.concatenate(
            [inner, proj, jnp.zeros((members, LANES - members - 1), jnp.float32), scaled], 1
        )
        for k in range(0, members, 4):
            system = eliminate_four(system, k, member_row)
        solved_proj = system[:, members : members + 1]
        solved_anom = system[:, LANES:]
        solved_innov = precision * (
            innov - jnp.sum(anom * solved_proj, 0, keepdims=True) / (members - 1)
        )
        mix = (solved_innov - 0.5 * solved_anom) / (members - 1)

        obs_x = row_ref[0:1, here]
        obs_y = row_ref[1:2, here]
        off_x = jnp.where(obs_x >= x_start, obs_x - x_start, obs_x - x_start + size_x)
        off_y = jnp.where(obs_y >= y_start, obs_y - y_start, obs_y - y_start + size_y)
        gap_x = jnp.where(off_x < rows, 0, jnp.minimum(off_x - (rows - 1), size_x - off_x))
        gap_y = jnp.where(off_y < columns, 0, jnp.minimum(off_y - (columns - 1), size_y - off_y))
        reaches = gap_x * gap_x + gap_y * gap_y < reach_sq
        flags = jnp.broadcast_to(reaches.astype(jnp.float32), (8, count))
        ranks = jnp.dot(
            flags.astype(jnp.bfloat16), before, preferred_element_type=jnp.float32
        )
        rank = jnp.where(reaches, ranks[0:1, :].astype(jnp.int32) - 1, -1)
        chosen = (slot == rank).astype(jnp.float32)
        count_ref[b] = jnp.sum(flags[0:1, :]).astype(jnp.int32)

        near_anom = lax.dot_general(
            chosen, anom, NT, precision=highest, preferred_element_type=jnp.float32
        )
        high, low = split_bf16(near_anom)
        lhs1_ref[b] = jnp.concatenate([high, high, low], 1)
        near_mix = lax.dot_general(
            mix, chosen, NT, precision=highest, preferred_element_type=jnp.float32
        )
        high, low = split_bf16(near_mix)
        for k in range(count // OBS_BLOCK):
            part = slice(k * OBS_BLOCK, (k + 1) * OBS_BLOCK)
            lhs2_ref[b, k] = jnp.concatenate([high[:, part], high[:, part], low[:, part]], 1)
        where = jnp.concatenate(
            [
                jnp.broadcast_to(obs_x, (LANES, count)),
                jnp.broadcast_to(obs_y, (LANES, count)),
            ],
            0,
        ).astype(jnp.float32)
        place_ref[b] = lax.dot_general(
            chosen, where, NT, precision=highest, preferred_element_type=jnp.float32
        )

        if b + 1 < batches:
            later = slice((b + 1) * count, batches * count)
            ahead = heights[:, later]
            ahead_anom = ahead - jnp.mean(ahead, 0, keepdims=True)
            cross = lax.dot_general(
                anom, ahead_anom, TN, precision=highest, preferred_element_type=jnp.float32
            )
            dist_sq = apart_sq(col_ref[:, b : b + 1], row_ref[0:1, later], size_x) + apart_sq(
                col_ref[:, batches + b : batches + b + 1], row_ref[1:2, later], size_y
            )
            ratio = dist_sq.astype(jnp.float32) / radius_sq[:, later]
            gain = cross * jnp.square(jnp.maximum(1.0 - ratio, 0.0))
            ahead = ahead + jnp.dot(
                mix, gain, precision=highest, preferred_element_type=jnp.float32
            )
            heights = jnp.concatenate([heights[:, : (b + 1) * count], ahead], 1)


def chain(members, start, every, obs_x, obs_y, values, variance, cutoff, sizes):
    batches, count = values.shape
    row_form = jnp.stack([obs_x.reshape(-1), obs_y.reshape(-1)], 0)
    col_form = jnp.concatenate([obs_x, obs_y], 0).T
    return pl.pallas_call(
        functools.partial(chain_kernel, members, sizes),
        in_specs=smem() + vmem(6),
        out_specs=vmem(3) + smem(),
        out_shape=[
            jax.ShapeDtypeStruct((batches, count, 3 * members), jnp.bfloat16),
            jax.ShapeDtypeStruct(
                (batches, count // OBS_BLOCK, members, 3 * OBS_BLOCK), jnp.bfloat16
            ),
            jax.ShapeDtypeStruct((batches, count, 2 * LANES), jnp.float32),
            jax.ShapeDtypeStruct((batches,), jnp.int32),
        ],
        compiler_params=params(),
        cost_estimate=CHAIN_COST,
        name="chain",
    )(start, every, row_form, col_form, values, variance, cutoff)


def update_kernel(
    sizes,
    continues,
    tile_ref,
    start_ref,
    count_ref,
    state_ref,
    cutoff_ref,
    lhs1_ref,
    lhs2_ref,
    place_ref,
    *rest,
):
    out_ref, members_ref, rhs_ref, back_ref = rest[1:] if continues else rest
    size_x, size_y = float(sizes[0]), float(sizes[1])
    members, fields, tiles, rows, _ = state_ref.shape
    batches = lhs1_ref.shape[0]
    cells = rows * LANES
    flat = state_ref.reshape(members * fields * tiles * rows, LANES)
    flat_back = back_ref.reshape(members * fields * rows, LANES)
    row0 = (start_ref[0] + tile_ref[pl.program_id(0)] * rows).astype(jnp.float32)
    lane = lax.broadcasted_iota(jnp.int32, (1, LANES), 1).astype(jnp.float32)

    def contribution(b, k, t):
        first = k * OBS_BLOCK
        if not isinstance(k, int):
            first = pl.multiple_of(first, OBS_BLOCK)
        part = pl.ds(first, OBS_BLOCK)
        obs_x = place_ref[b, part, :LANES]
        obs_y = place_ref[b, part, LANES:]
        col0 = (start_ref[1] + t * LANES).astype(jnp.float32)
        dist_y = apart_sq(obs_y, lane + col0, size_y)
        weights = []
        for r in range(rows):
            radius = cutoff_ref[r : r + 1, t * LANES : (t + 1) * LANES].astype(jnp.float32)
            ratio = (dist_y + apart_sq(obs_x, row0 + r, size_x)) * (1.0 / (radius * radius))
            weights.append(jnp.square(jnp.maximum(1.0 - ratio, 0.0)))
        weights = jnp.concatenate(weights, 1)
        cross = jnp.dot(
            lhs1_ref[b, part, :], rhs_ref[...], preferred_element_type=jnp.float32
        )
        gain = cross * jnp.concatenate([weights] * fields, 1)
        high, low = split_bf16(gain)
        return jnp.dot(
            lhs2_ref[b, k],
            jnp.concatenate([high, low, high], 0),
            preferred_element_type=jnp.float32,
        )

    for t in range(tiles):
        for f in range(fields):
            for r in range(rows):
                place = f * cells + r * LANES
                members_ref[:, place : place + LANES] = flat[
                    pl.ds((f * tiles + t) * rows + r, members, stride=fields * tiles * rows), :
                ]
        for b in range(batches):
            state = members_ref[...]
            high, low = split_bf16(state - jnp.mean(state, 0, keepdims=True))
            rhs_ref[...] = jnp.concatenate([high, low, high], 0)
            members_ref[...] = state + contribution(b, 0, t)

            def more(k, _):
                members_ref[...] += contribution(b, k, t)
                return 0

            blocks = (count_ref[b] + (OBS_BLOCK - 1)) // OBS_BLOCK
            lax.fori_loop(1, blocks, more, 0)
        for f in range(fields):
            for r in range(rows):
                place = f * cells + r * LANES
                flat_back[pl.ds(f * rows + r, members, stride=fields * rows), :] = members_ref[
                    :, place : place + LANES
                ]
        out_ref[:, :, :, t * LANES : (t + 1) * LANES] = back_ref[...]


def update(row_tiles, start, counts, state, cutoff, lhs1, lhs2, place, sizes, begun=None):
    members, fields, tiles, _, _ = state.shape
    rows = cutoff.shape[0]
    columns = tiles * LANES
    width = fields * ROW_TILE * LANES

    def whole(array):
        return pl.BlockSpec(array.shape, lambda i, tile: (0,) * array.ndim)

    operands = [row_tiles, start, counts, state, cutoff, lhs1, lhs2, place]
    in_specs = smem(2) + [
        pl.BlockSpec(
            (members, fields, tiles, ROW_TILE, LANES), lambda i, tile: (0, 0, 0, i, 0)
        ),
        pl.BlockSpec((ROW_TILE, columns), lambda i, tile: (tile[i], 0)),
        whole(lhs1),
        whole(lhs2),
        whole(place),
    ]
    aliases = {}
    if begun is not None:
        aliases = {len(operands): 0}
        operands.append(begun)
        in_specs.append(pl.BlockSpec(memory_space=pl.ANY))
    return pl.pallas_call(
        functools.partial(update_kernel, sizes, begun is not None),
        grid_spec=pltpu.PrefetchScalarGridSpec(
            num_scalar_prefetch=1,
            grid=row_tiles.shape,
            in_specs=in_specs,
            out_specs=pl.BlockSpec(
                (members, fields, ROW_TILE, columns), lambda i, tile: (0, 0, tile[i], 0)
            ),
            scratch_shapes=[
                pltpu.VMEM((members, width), jnp.float32),
                pltpu.VMEM((3 * members, width), jnp.bfloat16),
                pltpu.VMEM((members, fields, ROW_TILE, LANES), jnp.float32),
            ],
        ),
        out_shape=jax.ShapeDtypeStruct((members, fields, rows, columns), jnp.float32),
        input_output_aliases=aliases,
        compiler_params=params(),
        name="update",
    )(*operands)


def row_halos(ensemble, depth, axis):
    size = lax.axis_size(axis)
    odd = lax.axis_index(axis) % 2 == 1
    columns = depth.shape[1]

    def edge(start):
        return jnp.concatenate(
            [
                ensemble[:, :, start : start + HALO].reshape(-1, HALO, columns),
                depth[None, start : start + HALO],
            ],
            0,
        )

    first, last = edge(0), edge(depth.shape[0] - HALO)
    far = [(i, (i + (1 if i % 2 else -1)) % size) for i in range(size)]
    return (
        exchange(jnp.where(odd, first, last), axis, 1),
        lax.ppermute(jnp.where(odd, last, first), axis, far),
    )


def local(ensemble, sea_depth, cutoff, obs_index, obs_value, obs_var):
    blocks = lax.axis_size("mem")
    subs = lax.axis_size("sub")
    local_members, fields, rows, size_y = ensemble.shape
    members = local_members * blocks
    col_block = size_y // blocks
    size_x = rows * subs
    sizes = (size_x, size_y)
    sub, mem = lax.axis_index("sub"), lax.axis_index("mem")
    odd = sub % 2
    x_start = sub * rows
    y_start = mem * col_block
    start = jnp.stack([x_start, y_start, sub, mem]).astype(jnp.int32)
    parity = odd.astype(jnp.int32)[None]
    obs_x = obs_index // size_y
    obs_y = obs_index % size_y
    flat_x = obs_x.reshape(1, -1)
    flat_y = obs_y.reshape(1, -1)

    near_halo, far_halo = row_halos(ensemble, sea_depth, "sub")
    radius_part = pick_radius(cutoff, flat_x[0], flat_y[0], x_start, y_start)[None]
    near_first = jnp.where(odd == 1, 0, HALO)
    far_first = jnp.where(odd == 1, rows - HALO, 0)

    sent_near = forecast(
        near_kernel, "near", rows - HALO, parity, ensemble, near_halo, sea_depth, blocks
    )
    received_near = lax.all_to_all(sent_near, "mem", split_axis=0, concat_axis=0, tiled=True)
    near_heights = pick_near(flat_x - x_start - near_first, flat_y, sent_near)

    sent_far = forecast(far_kernel, "far", HALO, parity, ensemble, far_halo, sea_depth, blocks)
    part = pick_far(
        flat_x - x_start - far_first, flat_y, sent_far, near_heights, radius_part, subs
    )
    piece = lax.dynamic_index_in_dim(sum_over(part, "sub"), sub, 0, keepdims=True)
    every = gather_over(gather_over(piece, "mem")[None], "sub")
    lhs1, lhs2, place, counts = chain(
        members, start, every, obs_x, obs_y, obs_value, obs_var, cutoff, sizes
    )
    lhs1, sent_far = lax.optimization_barrier((lhs1, sent_far))
    received_far = lax.all_to_all(sent_far, "mem", split_axis=0, concat_axis=0, tiled=True)

    def analyse(received, row_tiles, begun=None):
        state = received.reshape((members,) + received.shape[2:])
        return update(
            row_tiles, start, counts, state, cutoff, lhs1, lhs2, place, sizes, begun
        )

    near_tiles = near_first // ROW_TILE + jnp.arange(rows // ROW_TILE - 1, dtype=jnp.int32)
    far_tiles = (far_first // ROW_TILE).astype(jnp.int32)[None]
    return analyse(received_far, far_tiles, analyse(received_near, near_tiles))


def solution(mesh):
    return jax.shard_map(
        local,
        mesh=mesh,
        in_specs=(P("mem", None, "sub", None), P("sub", None), P("sub", "mem"), P(), P(), P()),
        out_specs=P(None, None, "sub", "mem"),
        check_vma=False,
    )
```

```python
import functools

import jax
import jax.numpy as jnp
from jax import lax
from jax.experimental import pallas as pl
from jax.experimental.pallas import tpu as pltpu
from jax.sharding import PartitionSpec as P

STEPS = 4
HALO = 2 * STEPS
LANES = 128
OBS_BLOCK = 48
ROW_TILE = 8
VMEM_LIMIT = 48 * 2**20
OUTER_COST = pl.CostEstimate(flops=23 * 10**9, bytes_accessed=74 * 10**6, transcendentals=0)
CHAIN_COST = pl.CostEstimate(flops=26 * 10**9, bytes_accessed=85 * 10**6, transcendentals=0)

step_size = 0.3
coriolis = 0.2
highest = lax.Precision.HIGHEST

NT = (((1,), (1,)), ((), ()))
TN = (((0,), (0,)), ((), ()))


def params():
    return pltpu.CompilerParams(vmem_limit_bytes=VMEM_LIMIT)


def vmem(count=1):
    return [pl.BlockSpec(memory_space=pltpu.VMEM)] * count


def smem(count=1):
    return [pl.BlockSpec(memory_space=pltpu.SMEM)] * count


def split_bf16(value):
    high = value.astype(jnp.bfloat16)
    low = (value - high.astype(jnp.float32)).astype(jnp.bfloat16)
    return high, low


def row_centred(field):
    return pltpu.roll(field, field.shape[0] - 1, 0) - pltpu.roll(field, 1, 0)


def column_centred(tile_of, tiles):
    onward, back = [None] * tiles, [None] * tiles

    def at(t):
        for n in ((t - 1) % tiles, t, (t + 1) % tiles):
            if onward[n] is None:
                tile = tile_of(n)
                onward[n] = pltpu.roll(tile, LANES - 1, 1)
                back[n] = pltpu.roll(tile, 1, 1)
        lane = lax.broadcasted_iota(jnp.int32, onward[t].shape, 1)
        return jnp.where(
            lane == LANES - 1, onward[(t + 1) % tiles], onward[t]
        ) - jnp.where(lane == 0, back[(t - 1) % tiles], back[t])

    return at


def forecast_steps(height, east, north, half_depth):
    tiles = height.shape[0]
    half = 0.5 * step_size
    turn = step_size * coriolis
    for _ in range(STEPS):
        slope = column_centred(lambda t: half * height[t], tiles)
        for t in range(tiles):
            u, v = east[t], north[t]
            slope_y = slope(t)
            east[t] = u + turn * v - row_centred(half * height[t])
            north[t] = v - turn * u - slope_y
        inflow = column_centred(lambda t: half_depth[t] * north[t], tiles)
        for t in range(tiles):
            flow_y = inflow(t)
            height[t] = height[t] - (row_centred(half_depth[t] * east[t]) + flow_y)


def forecast_kernel(joins, kept, parity_ref, *refs):
    ens_ref, depth_ref, *halos, out_ref, height, east, north, half_depth = refs
    blocks, _, fields, out_tiles = out_ref.shape[:4]
    odd = parity_ref[0] == 1

    def window(block, near, far):
        if not joins:
            return block
        return jnp.concatenate([jnp.where(odd, near, far), block, jnp.where(odd, far, near)], 0)

    near_ref, far_ref, near_depth_ref, far_depth_ref = halos if joins else [None] * 4
    tiles = height.shape[0]

    def part(ref, index, t):
        return None if ref is None else ref[index][:, t * LANES : (t + 1) * LANES]

    @pl.when(pl.program_id(0) == 0)
    def _():
        for t in range(tiles):
            half_depth[t] = (0.5 * step_size) * window(
                depth_ref[:, t * LANES : (t + 1) * LANES],
                part(near_depth_ref, 0, t),
                part(far_depth_ref, 0, t),
            )

    state = (height, east, north)
    for f in range(fields):
        for t in range(tiles):
            state[f][t] = window(
                ens_ref[0, f, :, t * LANES : (t + 1) * LANES],
                part(near_ref, f, t),
                part(far_ref, f, t),
            )
    forecast_steps(*state, half_depth)
    for f in range(fields):
        for t in range(tiles):
            place = 0
            for first, count in kept:
                out_ref[t // out_tiles, 0, f, t % out_tiles, place : place + count] = state[f][
                    t, first : first + count
                ]
                place += count


def forecast(name, kept, parity, ensemble, depth, blocks, halos=()):
    members, fields, rows, columns = ensemble.shape
    tiles = columns // LANES
    window_rows = rows + (2 * HALO if halos else 0)
    out_shape = (blocks, members, fields, tiles // blocks, sum(n for _, n in kept), LANES)
    in_specs = smem() + [
        pl.BlockSpec((1, fields, rows, columns), lambda m: (m, 0, 0, 0)),
        pl.BlockSpec((rows, columns), lambda m: (0, 0)),
    ]
    operands = [parity, ensemble, depth]
    if halos:
        in_specs += [pl.BlockSpec((fields, HALO, columns), lambda m: (m, 0, 0))] * 2
        in_specs += [pl.BlockSpec((1, HALO, columns), lambda m: (members * fields, 0, 0))] * 2
        operands += [*halos, *halos]
    return pl.pallas_call(
        functools.partial(forecast_kernel, bool(halos), kept),
        grid=(members,),
        in_specs=in_specs,
        out_specs=pl.BlockSpec(
            (blocks, 1) + out_shape[2:], lambda m: (0, m, 0, 0, 0, 0)
        ),
        out_shape=jax.ShapeDtypeStruct(out_shape, jnp.float32),
        scratch_shapes=[pltpu.VMEM((tiles, window_rows, LANES), jnp.float32)] * 4,
        compiler_params=params(),
        cost_estimate=OUTER_COST if halos else None,
        name=name,
    )(*operands)


def pick(row_ref, col_ref, height_ref):
    blocks, members, _, tiles, rows, _ = height_ref.shape
    heights = jnp.concatenate(
        [
            height_ref[d, :, 0, t].reshape(members * rows, LANES)
            for d in range(blocks)
            for t in range(tiles)
        ],
        1,
    )
    high, rest = heights.astype(jnp.bfloat16), heights
    pieces = [high]
    for _ in range(2):
        rest = rest - pieces[-1].astype(jnp.float32)
        pieces.append(rest.astype(jnp.bfloat16))
    count = col_ref.shape[1]
    column = lax.broadcasted_iota(jnp.int32, (heights.shape[1], count), 0)
    in_column = (column == col_ref[...]).astype(jnp.float32).astype(jnp.bfloat16)
    found = jnp.dot(
        jnp.concatenate(pieces, 0), in_column, preferred_element_type=jnp.float32
    )
    size = members * rows
    found = (found[:size] + found[size : 2 * size]) + found[2 * size :]
    found = found.reshape(members, rows, count)
    row = lax.broadcasted_iota(jnp.int32, (1, rows, count), 1)
    return jnp.sum(jnp.where(row == row_ref[...][None], found, 0.0), 1)


def pick_inner_kernel(row_ref, col_ref, height_ref, out_ref):
    out_ref[...] = pick(row_ref, col_ref, height_ref)


def pick_outer_kernel(row_ref, col_ref, height_ref, inner_ref, radius_ref, out_ref):
    heights = pick(row_ref, col_ref, height_ref) + inner_ref[...]
    members, count = heights.shape
    pieces = out_ref.shape[0]
    groups = count // pieces // LANES
    out_ref[...] = jnp.zeros_like(out_ref)
    for j in range(pieces):
        for g in range(groups):
            part = slice((j * groups + g) * LANES, (j * groups + g + 1) * LANES)
            for m in range(members):
                row = g * members + m
                out_ref[j, row : row + 1, :] = heights[m : m + 1, part]
            row = members * groups + g
            out_ref[j, row : row + 1, :] = radius_ref[:, part]


def height_spec(sent):
    blocks, members, _, tiles, rows, _ = sent.shape
    return pl.BlockSpec((blocks, members, 1, tiles, rows, LANES), lambda i: (0,) * 6)


def whole_spec(shape):
    return pl.BlockSpec(shape, lambda i: (0,) * len(shape))


def pick_inner(row, col, sent):
    shape = (sent.shape[1], col.shape[1])
    return pl.pallas_call(
        pick_inner_kernel,
        grid=(1,),
        in_specs=[whole_spec(row.shape), whole_spec(col.shape), height_spec(sent)],
        out_specs=whole_spec(shape),
        out_shape=jax.ShapeDtypeStruct(shape, jnp.float32),
        compiler_params=params(),
        name="pick_inner",
    )(row, col, sent)


def pick_outer(row, col, sent, inner, radius, pieces):
    members, count = inner.shape
    used = (members + 1) * (count // pieces // LANES)
    shape = (pieces, used + -used % 8, LANES)
    return pl.pallas_call(
        pick_outer_kernel,
        grid=(1,),
        in_specs=[
            whole_spec(row.shape),
            whole_spec(col.shape),
            height_spec(sent),
            whole_spec(inner.shape),
            whole_spec(radius.shape),
        ],
        out_specs=whole_spec(shape),
        out_shape=jax.ShapeDtypeStruct(shape, jnp.float32),
        compiler_params=params(),
        name="pick_outer",
    )(row, col, sent, inner, radius)


def pick_radius(cutoff, obs_x, obs_y, x_start, y_start):
    rows, columns = cutoff.shape
    radius_sq = jnp.square(cutoff.astype(jnp.float32))
    row_is = (obs_x[:, None] - x_start == jnp.arange(rows)[None, :]).astype(jnp.float32)
    col_is = obs_y[:, None] - y_start == jnp.arange(columns)[None, :]
    by_row = jnp.dot(row_is, radius_sq, precision=highest)
    return jnp.sum(jnp.where(col_is, by_row, 0.0), 1)


def exchange(value, axis, distance):
    size = lax.axis_size(axis)
    return lax.ppermute(value, axis, [(i, i ^ distance) for i in range(size)])


def sum_over(value, axis):
    distance = 1
    while distance < lax.axis_size(axis):
        value = value + exchange(value, axis, distance)
        distance *= 2
    return value


def gather_over(value, axis, first=1, width=None):
    width = lax.axis_size(axis) if width is None else width
    return jnp.concatenate(
        [value] + [exchange(value, axis, r * first) for r in range(1, width)], 0
    )


def apart_sq(a, b, size):
    gap = jnp.abs(a - b)
    gap = jnp.minimum(gap, size - gap)
    return gap * gap


def eliminate_four(system, k, row_id):
    width = system.shape[1]
    row = [system[k + i : k + i + 1, :] for i in range(4)]
    p = [
        [jnp.broadcast_to(row[i][:, k + j : k + j + 1], (1, LANES)) for j in range(4)]
        for i in range(4)
    ]

    def wide(value):
        return jnp.concatenate([value] * (width // LANES), 1)

    def inverse(a00, a01, a10, a11):
        scale = 1.0 / (a00 * a11 - a01 * a10)
        return a11 * scale, -a01 * scale, -a10 * scale, a00 * scale

    i00, i01, i10, i11 = inverse(p[0][0], p[0][1], p[1][0], p[1][1])
    y = [
        [i00 * p[0][2 + j] + i01 * p[1][2 + j] for j in range(2)],
        [i10 * p[0][2 + j] + i11 * p[1][2 + j] for j in range(2)],
    ]
    schur = [
        [p[2 + i][2 + j] - p[2 + i][0] * y[0][j] - p[2 + i][1] * y[1][j] for j in range(2)]
        for i in range(2)
    ]
    s00, s01, s10, s11 = inverse(schur[0][0], schur[0][1], schur[1][0], schur[1][1])
    top0 = wide(i00) * row[0] + wide(i01) * row[1]
    top1 = wide(i10) * row[0] + wide(i11) * row[1]
    low0 = row[2] - wide(p[2][0]) * top0 - wide(p[2][1]) * top1
    low1 = row[3] - wide(p[3][0]) * top0 - wide(p[3][1]) * top1
    new2 = wide(s00) * low0 + wide(s01) * low1
    new3 = wide(s10) * low0 + wide(s11) * low1
    new0 = top0 - wide(y[0][0]) * new2 - wide(y[0][1]) * new3
    new1 = top1 - wide(y[1][0]) * new2 - wide(y[1][1]) * new3
    new = (new0, new1, new2, new3)
    result = system
    for i in range(4):
        result = result - system[:, k + i : k + i + 1] * new[i]
    for i in range(4):
        result = jnp.where(row_id == k + i, new[i], result)
    return result


def chain_kernel(
    members,
    sizes,
    start_ref,
    every_ref,
    row_ref,
    col_ref,
    value_ref,
    variance_ref,
    cutoff_ref,
    lhs1_ref,
    lhs2_ref,
    place_ref,
    count_ref,
    local_ref,
    anom_ref,
    mix_ref,
    rank_ref,
):
    size_x, size_y = sizes
    pieces, sources, _, _ = every_ref.shape
    batches, count = value_ref.shape
    groups = batches * count // pieces // LANES
    local_members = members // sources
    rows, columns = cutoff_ref.shape
    tiles = columns // LANES
    x_start = start_ref[0]
    y_start = start_ref[1]
    reach = jnp.max(cutoff_ref[...])
    reach_sq = reach * reach

    heights, radius_sq = [], []
    for j in range(pieces):
        piece = jnp.bitwise_xor(start_ref[2], j)
        for g in range(groups):
            found, radius = [], 0.0
            for source in range(sources):
                one = every_ref.at[piece, jnp.bitwise_xor(start_ref[3], source)]
                found.append(one[g * local_members : (g + 1) * local_members, :])
                last = local_members * groups + g
                radius = radius + one[last : last + 1, :]
            heights.append(jnp.concatenate(found, 0))
            radius_sq.append(radius)
    heights = jnp.concatenate(heights, 1)
    inverse_sq = 1.0 / jnp.concatenate(radius_sq, 1)
    before = (
        lax.broadcasted_iota(jnp.int32, (count, count), 0)
        <= lax.broadcasted_iota(jnp.int32, (count, count), 1)
    ).astype(jnp.bfloat16)
    slot = lax.broadcasted_iota(jnp.int32, (OBS_BLOCK, count), 0)
    twice = lax.broadcasted_iota(jnp.int32, (members, 3 * OBS_BLOCK), 1) < 2 * OBS_BLOCK
    member_row = lax.broadcasted_iota(jnp.int32, (members, LANES + count), 0)
    eye = (
        lax.broadcasted_iota(jnp.int32, (members, members), 0)
        == lax.broadcasted_iota(jnp.int32, (members, members), 1)
    ).astype(jnp.float32)

    def rank_reaching(b, t):
        obs_x = row_ref[0:1, b * count : (b + 1) * count]
        obs_y = row_ref[1:2, b * count : (b + 1) * count]
        off_x = jnp.where(obs_x >= x_start, obs_x - x_start, obs_x - x_start + size_x)
        gap_x = jnp.where(off_x < rows, 0, jnp.minimum(off_x - (rows - 1), size_x - off_x))
        off_y = obs_y - (y_start + t * LANES)
        off_y = jnp.where(off_y >= 0, off_y, off_y + size_y)
        gap_y = jnp.where(off_y < LANES, 0, jnp.minimum(off_y - (LANES - 1), size_y - off_y))
        reaches = gap_x * gap_x + gap_y * gap_y < reach_sq
        flags = jnp.broadcast_to(reaches.astype(jnp.float32), (8, count))
        ranks = jnp.dot(
            flags.astype(jnp.bfloat16), before, preferred_element_type=jnp.float32
        )
        rank_ref[b, t] = jnp.where(reaches, ranks.astype(jnp.int32) - 1, -1)
        count_ref[b, t] = jnp.sum(flags[0:1, :]).astype(jnp.int32)

    def gather(b, t, k):
        chosen = (slot == rank_ref[b, t, 0:1, :] - k * OBS_BLOCK).astype(jnp.float32)
        thrice = jnp.concatenate([chosen] * 3, 0).astype(jnp.bfloat16)
        chosen = chosen.astype(jnp.bfloat16)

        def product(x, y):
            return lax.dot_general(x, y, NT, preferred_element_type=jnp.float32)

        lhs1_ref[b, t, k] = product(chosen, anom_ref[b]).astype(jnp.bfloat16)
        lhs2_ref[b, t, k] = jnp.where(
            twice, product(mix_ref[b, 0], thrice), product(mix_ref[b, 1], thrice)
        ).astype(jnp.bfloat16)
        cells = row_ref[:, b * count : (b + 1) * count]
        place_ref[b, t, k] = product(
            chosen,
            jnp.concatenate([cells // 256, cells % 256], 0)
            .astype(jnp.float32)
            .astype(jnp.bfloat16),
        )

    def localize(b, first, size):
        later = slice((b + 1) * count, batches * count)
        part = slice(first, first + size)
        dist_sq = apart_sq(col_ref[part, b : b + 1], row_ref[0:1, later], size_x) + apart_sq(
            col_ref[part, batches + b : batches + b + 1], row_ref[1:2, later], size_y
        )
        ratio = dist_sq.astype(jnp.float32) * inverse_sq[:, later]
        local_ref[part, later] = jnp.square(jnp.maximum(1.0 - ratio, 0.0))

    for b in range(batches):
        here = slice(b * count, (b + 1) * count)
        prior = heights[:, here]
        mean = jnp.mean(prior, 0, keepdims=True)
        anom = prior - mean
        precision = 1.0 / variance_ref[b : b + 1, :]
        innov = value_ref[b : b + 1, :] - mean
        scaled = anom * precision
        inner = eye + lax.dot_general(
            scaled, anom, NT, precision=highest, preferred_element_type=jnp.float32
        ) / (members - 1)
        proj = jnp.sum(scaled * innov, 1, keepdims=True)
        system = jnp.concatenate(
            [inner, proj, jnp.zeros((members, LANES - members - 1), jnp.float32), scaled], 1
        )
        aside = [functools.partial(rank_reaching, b, t) for t in range(tiles)]
        if b > 0:
            aside += [functools.partial(gather, b - 1, t, 0) for t in range(tiles)]
        if b + 1 < batches:
            aside += [functools.partial(localize, b, first, 32) for first in range(0, count, 32)]
        steps = members // 4
        for step in range(steps):
            system = eliminate_four(system, 4 * step, member_row)
            for one in aside[step::steps]:
                one()
        solved_proj = system[:, members : members + 1]
        solved_anom = system[:, LANES:]
        solved_innov = precision * (
            innov - jnp.sum(anom * solved_proj, 0, keepdims=True) / (members - 1)
        )
        mix = (solved_innov - 0.5 * solved_anom) / (members - 1)
        high, low = split_bf16(anom)
        anom_ref[b] = jnp.concatenate([high, high, low], 0)
        mix_high, mix_low = split_bf16(mix)
        mix_ref[b, 0] = mix_high
        mix_ref[b, 1] = mix_low

        if b + 1 < batches:
            later = slice((b + 1) * count, batches * count)
            ahead = heights[:, later]
            ahead_anom = ahead - jnp.mean(ahead, 0, keepdims=True)
            cross = lax.dot_general(
                anom, ahead_anom, TN, precision=highest, preferred_element_type=jnp.float32
            )
            high, low = split_bf16(cross * local_ref[:, later])
            both = jnp.dot(
                jnp.concatenate([mix_high, mix_low], 0), high, preferred_element_type=jnp.float32
            )
            rest = jnp.dot(mix_high, low, preferred_element_type=jnp.float32)
            ahead = ahead + (both[:members] + (both[members:] + rest))
            heights = jnp.concatenate([heights[:, : (b + 1) * count], ahead], 1)

    for t in range(tiles):
        gather(batches - 1, t, 0)
    counts = [[count_ref[b, t] for t in range(tiles)] for b in range(batches)]
    most = functools.reduce(jnp.maximum, sum(counts, []))

    @pl.when(most > OBS_BLOCK)
    def _():
        for b in range(batches):
            for t in range(tiles):

                def more(k, _, b=b, t=t):
                    gather(b, t, k)
                    return 0

                blocks = (counts[b][t] + (OBS_BLOCK - 1)) // OBS_BLOCK
                lax.fori_loop(1, blocks, more, 0)


def chain(members, start, every, obs_x, obs_y, values, variance, cutoff, sizes):
    batches, count = values.shape
    row_form = jnp.stack([obs_x.reshape(-1), obs_y.reshape(-1)], 0)
    col_form = jnp.concatenate([obs_x, obs_y], 0).T
    tiles = cutoff.shape[1] // LANES
    slots = (batches, tiles, -(-count // OBS_BLOCK))
    return pl.pallas_call(
        functools.partial(chain_kernel, members, sizes),
        in_specs=smem() + vmem(6),
        out_specs=vmem(3) + smem(),
        out_shape=[
            jax.ShapeDtypeStruct(slots + (OBS_BLOCK, 3 * members), jnp.bfloat16),
            jax.ShapeDtypeStruct(slots + (members, 3 * OBS_BLOCK), jnp.bfloat16),
            jax.ShapeDtypeStruct(slots + (OBS_BLOCK, 4), jnp.float32),
            jax.ShapeDtypeStruct(slots[:2], jnp.int32),
        ],
        scratch_shapes=[
            pltpu.VMEM((count, batches * count), jnp.float32),
            pltpu.VMEM((batches, 3 * members, count), jnp.bfloat16),
            pltpu.VMEM((batches, 2, members, count), jnp.bfloat16),
            pltpu.VMEM((batches, tiles, 8, count), jnp.int32),
        ],
        compiler_params=params(),
        cost_estimate=CHAIN_COST,
        name="chain",
    )(start, every, row_form, col_form, values, variance, cutoff)


def update_kernel(
    sizes,
    continues,
    tile_ref,
    start_ref,
    count_ref,
    state_ref,
    cutoff_ref,
    lhs1_ref,
    lhs2_ref,
    place_ref,
    *rest,
):
    out_ref, members_ref, rhs_ref = rest[1:] if continues else rest
    size_x, size_y = float(sizes[0]), float(sizes[1])
    members, fields, _, rows, _ = state_ref.shape
    batches = lhs1_ref.shape[0]
    cells = rows * LANES
    t = pl.program_id(1)
    flat = state_ref.reshape(members * fields * rows, LANES)
    flat_out = out_ref.reshape(members * fields * rows, LANES)
    row0 = (start_ref[0] + tile_ref[pl.program_id(0)] * rows).astype(jnp.float32)
    col0 = (start_ref[1] + t * LANES).astype(jnp.float32)
    lane = lax.broadcasted_iota(jnp.int32, (1, LANES), 1).astype(jnp.float32)
    radius = cutoff_ref[...].astype(jnp.float32)
    radius_sq = radius * radius
    inverse = 1.0 / radius_sq

    def localized(b, k):
        place = place_ref[b, 0, k]
        obs_x = jnp.broadcast_to(place[:, 0:1] * 256.0 + place[:, 2:3], (OBS_BLOCK, LANES))
        obs_y = jnp.broadcast_to(place[:, 1:2] * 256.0 + place[:, 3:4], (OBS_BLOCK, LANES))
        dist_y = apart_sq(obs_y, lane + col0, size_y)
        dist_x = apart_sq(obs_x, lane + row0, size_x)
        weights = []
        for r in range(rows):
            ratio = (dist_y + dist_x[:, r : r + 1]) * inverse[r : r + 1, :]
            weights.append(jnp.square(jnp.maximum(1.0 - ratio, 0.0)))
        return jnp.concatenate(weights, 1)

    def contribution(b, k, weights, rhs):
        cross = jnp.dot(lhs1_ref[b, 0, k], rhs, preferred_element_type=jnp.float32)
        high, low = split_bf16(cross * weights)
        return jnp.dot(
            lhs2_ref[b, 0, k],
            jnp.concatenate([high, low, high], 0),
            preferred_element_type=jnp.float32,
        )

    def split_anom(state):
        high, low = split_bf16(state - jnp.mean(state, 0, keepdims=True))
        return jnp.concatenate([high, low, high], 0)

    def load(f):
        return jnp.concatenate(
            [
                flat[pl.ds(f * rows + r, members, stride=fields * rows), :]
                for r in range(rows)
            ],
            1,
        )

    def store(f, state):
        for r in range(rows):
            flat_out[pl.ds(f * rows + r, members, stride=fields * rows), :] = state[
                :, r * LANES : (r + 1) * LANES
            ]

    most = count_ref[0, t]
    for b in range(1, batches):
        most = jnp.maximum(most, count_ref[b, t])

    @pl.when(most <= OBS_BLOCK)
    def _():
        states = [load(f) for f in range(fields)]
        for b in range(batches):
            weights = localized(b, 0)
            rhs = [split_anom(x) for x in states]
            cross = [jnp.dot(lhs1_ref[b, 0, 0], x, preferred_element_type=jnp.float32) for x in rhs]
            gain = []
            for c in cross:
                high, low = split_bf16(c * weights)
                gain.append(jnp.concatenate([high, low, high], 0))
            moved = [jnp.dot(lhs2_ref[b, 0, 0], g, preferred_element_type=jnp.float32) for g in gain]
            states = [x + y for x, y in zip(states, moved)]
        for f in range(fields):
            store(f, states[f])

    @pl.when(most > OBS_BLOCK)
    def _():
        for f in range(fields):
            members_ref[f] = load(f)
        for b in range(batches):
            for f in range(fields):
                rhs_ref[f] = split_anom(members_ref[f])

            def block(k, _, b=b):
                weights = localized(b, k)
                for f in range(fields):
                    members_ref[f] += contribution(b, k, weights, rhs_ref[f])
                return 0

            blocks = (count_ref[b, t] + (OBS_BLOCK - 1)) // OBS_BLOCK
            lax.fori_loop(0, blocks, block, 0)
        for f in range(fields):
            store(f, members_ref[f])


def update(row_tiles, start, counts, state, cutoff, lhs1, lhs2, place, sizes, begun=None):
    members, fields, tiles, _, _ = state.shape
    rows = cutoff.shape[0]
    columns = tiles * LANES
    cells = ROW_TILE * LANES

    def of_tile(array):
        shape = (array.shape[0], 1) + array.shape[2:]
        return pl.BlockSpec(shape, lambda i, t, tile: (0, t) + (0,) * (array.ndim - 2))

    operands = [row_tiles, start, counts, state, cutoff, lhs1, lhs2, place]
    in_specs = smem(2) + [
        pl.BlockSpec(
            (members, fields, 1, ROW_TILE, LANES), lambda i, t, tile: (0, 0, t, i, 0)
        ),
        pl.BlockSpec((ROW_TILE, LANES), lambda i, t, tile: (tile[i], t)),
        of_tile(lhs1),
        of_tile(lhs2),
        of_tile(place),
    ]
    aliases = {}
    if begun is not None:
        aliases = {len(operands): 0}
        operands.append(begun)
        in_specs.append(pl.BlockSpec(memory_space=pl.ANY))
    return pl.pallas_call(
        functools.partial(update_kernel, sizes, begun is not None),
        grid_spec=pltpu.PrefetchScalarGridSpec(
            num_scalar_prefetch=1,
            grid=row_tiles.shape + (tiles,),
            in_specs=in_specs,
            out_specs=pl.BlockSpec(
                (members, fields, ROW_TILE, LANES), lambda i, t, tile: (0, 0, tile[i], t)
            ),
            scratch_shapes=[
                pltpu.VMEM((fields, members, cells), jnp.float32),
                pltpu.VMEM((fields, 3 * members, cells), jnp.bfloat16),
            ],
        ),
        out_shape=jax.ShapeDtypeStruct((members, fields, rows, columns), jnp.float32),
        input_output_aliases=aliases,
        compiler_params=params(),
        name="update",
    )(*operands)


def row_halos(ensemble, depth, axis):
    size = lax.axis_size(axis)
    odd = lax.axis_index(axis) % 2 == 1
    columns = depth.shape[1]

    def edge(start):
        return jnp.concatenate(
            [
                ensemble[:, :, start : start + HALO].reshape(-1, HALO, columns),
                depth[None, start : start + HALO],
            ],
            0,
        )

    first, last = edge(0), edge(depth.shape[0] - HALO)
    far = [(i, (i + (1 if i % 2 else -1)) % size) for i in range(size)]
    return (
        exchange(jnp.where(odd, first, last), axis, 1),
        lax.ppermute(jnp.where(odd, last, first), axis, far),
    )


def local(ensemble, sea_depth, cutoff, obs_index, obs_value, obs_var):
    blocks = lax.axis_size("mem")
    subs = lax.axis_size("sub")
    local_members, fields, rows, size_y = ensemble.shape
    members = local_members * blocks
    col_block = size_y // blocks
    size_x = rows * subs
    sizes = (size_x, size_y)
    sub, mem = lax.axis_index("sub"), lax.axis_index("mem")
    odd = sub % 2
    x_start = sub * rows
    y_start = mem * col_block
    start = jnp.stack([x_start, y_start, sub, mem]).astype(jnp.int32)
    parity = odd.astype(jnp.int32)[None]
    obs_x = obs_index // size_y
    obs_y = obs_index % size_y
    flat_x = obs_x.reshape(1, -1)
    flat_y = obs_y.reshape(1, -1)

    halos = row_halos(ensemble, sea_depth, "sub")
    radius_part = pick_radius(cutoff, flat_x[0], flat_y[0], x_start, y_start)[None]

    inner_rows = rows - 2 * HALO
    sent_inner = forecast(
        "inner", [(HALO, inner_rows)], parity, ensemble, sea_depth, blocks
    )
    received_inner = lax.all_to_all(
        sent_inner, "mem", split_axis=0, concat_axis=0, tiled=True
    )
    row = flat_x - x_start
    inner_heights = pick_inner(row - HALO, flat_y, sent_inner)

    outer_row = jnp.where(
        row < HALO, row, jnp.where(row < rows - HALO, -1, row - inner_rows)
    )
    sent_outer = forecast(
        "outer", [(HALO, HALO), (rows, HALO)], parity, ensemble, sea_depth, blocks, halos
    )
    part = pick_outer(outer_row, flat_y, sent_outer, inner_heights, radius_part, subs)
    piece = lax.dynamic_index_in_dim(sum_over(part, "sub"), sub, 0, keepdims=True)
    low = max(blocks // 4, 1)
    every = gather_over(gather_over(piece, "mem", 1, low), "mem", low, blocks // low)
    every, sent_outer = lax.optimization_barrier((every, sent_outer))
    received_outer = lax.all_to_all(
        sent_outer, "mem", split_axis=0, concat_axis=0, tiled=True
    )
    every = gather_over(every[None], "sub")
    lhs1, lhs2, place, counts = chain(
        members, start, every, obs_x, obs_y, obs_value, obs_var, cutoff, sizes
    )

    def analyse(received, row_tiles, begun=None):
        state = received.reshape((members,) + received.shape[2:])
        row_tiles = jnp.array(row_tiles, jnp.int32)
        return update(
            row_tiles, start, counts, state, cutoff, lhs1, lhs2, place, sizes, begun
        )

    last = rows // ROW_TILE - 1
    return analyse(received_outer, [0, last], analyse(received_inner, list(range(1, last))))


def solution(mesh):
    return jax.shard_map(
        local,
        mesh=mesh,
        in_specs=(P("mem", None, "sub", None), P("sub", None), P("sub", "mem"), P(), P(), P()),
        out_specs=P(None, None, "sub", "mem"),
        check_vma=False,
    )
```

```python
import functools

import jax
import jax.numpy as jnp
from jax import lax
from jax.experimental import pallas as pl
from jax.experimental.pallas import tpu as pltpu
from jax.sharding import PartitionSpec as P

STEPS = 4
HALO = 2 * STEPS
LANES = 128
OBS_BLOCK = 48
ROW_TILE = 8
OUTER_COST = pl.CostEstimate(flops=23 * 10**9, bytes_accessed=74 * 10**6, transcendentals=0)
CHAIN_COST = pl.CostEstimate(flops=26 * 10**9, bytes_accessed=85 * 10**6, transcendentals=0)

step_size = 0.3
coriolis = 0.2
highest = lax.Precision.HIGHEST

NT = (((1,), (1,)), ((), ()))
TN = (((0,), (0,)), ((), ()))


def params(mebibytes):
    return pltpu.CompilerParams(vmem_limit_bytes=mebibytes * 2**20)


def vmem(count=1):
    return [pl.BlockSpec(memory_space=pltpu.VMEM)] * count


def hbm(count=1):
    return [pl.BlockSpec(memory_space=pltpu.HBM)] * count


def smem(count=1):
    return [pl.BlockSpec(memory_space=pltpu.SMEM)] * count


def split_bf16(value):
    high = value.astype(jnp.bfloat16)
    low = (value - high.astype(jnp.float32)).astype(jnp.bfloat16)
    return high, low


def row_centred(field):
    return pltpu.roll(field, field.shape[0] - 1, 0) - pltpu.roll(field, 1, 0)


def column_centred(tile_of, tiles):
    onward, back = [None] * tiles, [None] * tiles

    def at(t):
        for n in ((t - 1) % tiles, t, (t + 1) % tiles):
            if onward[n] is None:
                tile = tile_of(n)
                onward[n] = pltpu.roll(tile, LANES - 1, 1)
                back[n] = pltpu.roll(tile, 1, 1)
        lane = lax.broadcasted_iota(jnp.int32, onward[t].shape, 1)
        return jnp.where(
            lane == LANES - 1, onward[(t + 1) % tiles], onward[t]
        ) - jnp.where(lane == 0, back[(t - 1) % tiles], back[t])

    return at


def forecast_steps(height, east, north, half_depth):
    tiles = height.shape[0]
    half = 0.5 * step_size
    turn = step_size * coriolis
    for _ in range(STEPS):
        slope = column_centred(lambda t: half * height[t], tiles)
        for t in range(tiles):
            u, v = east[t], north[t]
            slope_y = slope(t)
            east[t] = u + turn * v - row_centred(half * height[t])
            north[t] = v - turn * u - slope_y
        inflow = column_centred(lambda t: half_depth[t] * north[t], tiles)
        for t in range(tiles):
            flow_y = inflow(t)
            height[t] = height[t] - (row_centred(half_depth[t] * east[t]) + flow_y)


def forecast_kernel(joins, kept, *refs):
    ens_ref, depth_ref, *halos, out_ref, height, east, north, half_depth = refs
    tiles = height.shape[0]
    out_tiles = out_ref.shape[2]
    fields = ens_ref.shape[1]

    def window(block, above, below, t):
        part = slice(t * LANES, (t + 1) * LANES)
        if not joins:
            return block[:, part]
        return jnp.concatenate([above[:, part], block[:, part], below[:, part]], 0)

    up_ref, down_ref, depth_up_ref, depth_down_ref = halos if joins else [None] * 4

    @pl.when(pl.program_id(0) == 0)
    def _():
        for t in range(tiles):
            above, below = (depth_up_ref.at[0], depth_down_ref.at[0]) if joins else (None, None)
            half_depth[t] = (0.5 * step_size) * window(depth_ref, above, below, t)

    state = (height, east, north)
    for f in range(fields):
        above, below = (up_ref.at[f], down_ref.at[f]) if joins else (None, None)
        for t in range(tiles):
            state[f][t] = window(ens_ref.at[0, f], above, below, t)
    forecast_steps(*state, half_depth)
    for f in range(fields):
        for t in range(tiles):
            for place, tile in enumerate(kept):
                out_ref[t // out_tiles, place, t % out_tiles, 0, f] = state[f][
                    t, tile * ROW_TILE : (tile + 1) * ROW_TILE
                ]


def forecast(name, kept, ensemble, depth, blocks, halos=()):
    members, fields, rows, columns = ensemble.shape
    tiles = columns // LANES
    window_rows = rows + (2 * HALO if halos else 0)
    out_shape = (blocks, len(kept), tiles // blocks, members, fields, ROW_TILE, LANES)
    in_specs = [
        pl.BlockSpec((1, fields, rows, columns), lambda m: (m, 0, 0, 0)),
        pl.BlockSpec((rows, columns), lambda m: (0, 0)),
    ]
    if halos:
        in_specs += [pl.BlockSpec((fields, HALO, columns), lambda m: (m, 0, 0))] * 2
        in_specs += [pl.BlockSpec((1, HALO, columns), lambda m: (members * fields, 0, 0))] * 2
    return pl.pallas_call(
        functools.partial(forecast_kernel, bool(halos), kept),
        grid=(members,),
        in_specs=in_specs,
        out_specs=pl.BlockSpec(
            out_shape[:3] + (1,) + out_shape[4:], lambda m: (0, 0, 0, m, 0, 0, 0)
        ),
        out_shape=jax.ShapeDtypeStruct(out_shape, jnp.float32),
        scratch_shapes=[pltpu.VMEM((tiles, window_rows, LANES), jnp.float32)] * 4,
        compiler_params=params(16),
        cost_estimate=OUTER_COST if halos else None,
        name=name,
    )(ensemble, depth, *halos)


def pick(row_ref, col_ref, height_ref):
    blocks, row_tiles, tiles, members, _, _, _ = height_ref.shape
    rows = row_tiles * ROW_TILE
    heights = jnp.concatenate(
        [
            height_ref[d, :, t, :, 0].reshape(rows * members, LANES)
            for d in range(blocks)
            for t in range(tiles)
        ],
        1,
    )
    high, rest = heights.astype(jnp.bfloat16), heights
    pieces = [high]
    for _ in range(2):
        rest = rest - pieces[-1].astype(jnp.float32)
        pieces.append(rest.astype(jnp.bfloat16))
    count = col_ref.shape[1]
    column = lax.broadcasted_iota(jnp.int32, (heights.shape[1], count), 0)
    in_column = (column == col_ref[...]).astype(jnp.float32).astype(jnp.bfloat16)
    found = jnp.dot(
        jnp.concatenate(pieces, 0), in_column, preferred_element_type=jnp.float32
    )
    size = members * rows
    found = (found[:size] + found[size : 2 * size]) + found[2 * size :]
    found = found.reshape(row_tiles, members, ROW_TILE, count)
    row = lax.broadcasted_iota(jnp.int32, (1, ROW_TILE, count), 1)
    result = 0.0
    for i in range(row_tiles):
        here = row + i * ROW_TILE == row_ref[...][None]
        result = result + jnp.sum(jnp.where(here, found[i], 0.0), 1)
    return result


def pick_inner_kernel(row_ref, col_ref, height_ref, out_ref):
    out_ref[...] = pick(row_ref, col_ref, height_ref)


def pick_outer_kernel(row_ref, col_ref, height_ref, inner_ref, radius_ref, out_ref):
    heights = pick(row_ref, col_ref, height_ref) + inner_ref[...]
    members, count = heights.shape
    pieces = out_ref.shape[0]
    groups = count // pieces // LANES
    out_ref[...] = jnp.zeros_like(out_ref)
    for j in range(pieces):
        for g in range(groups):
            part = slice((j * groups + g) * LANES, (j * groups + g + 1) * LANES)
            for m in range(members):
                row = g * members + m
                out_ref[j, row : row + 1, :] = heights[m : m + 1, part]
            row = members * groups + g
            out_ref[j, row : row + 1, :] = radius_ref[:, part]


def height_spec(sent):
    shape = sent.shape[:4] + (1,) + sent.shape[5:]
    return pl.BlockSpec(shape, lambda i: (0,) * len(shape))


def whole_spec(shape):
    return pl.BlockSpec(shape, lambda i: (0,) * len(shape))


def pick_inner(row, col, sent):
    shape = (sent.shape[3], col.shape[1])
    return pl.pallas_call(
        pick_inner_kernel,
        grid=(1,),
        in_specs=[whole_spec(row.shape), whole_spec(col.shape), height_spec(sent)],
        out_specs=whole_spec(shape),
        out_shape=jax.ShapeDtypeStruct(shape, jnp.float32),
        compiler_params=params(40),
        name="pick_inner",
    )(row, col, sent)


def pick_outer(row, col, sent, inner, radius, pieces):
    members, count = inner.shape
    used = (members + 1) * (count // pieces // LANES)
    shape = (pieces, used + -used % 8, LANES)
    return pl.pallas_call(
        pick_outer_kernel,
        grid=(1,),
        in_specs=[
            whole_spec(row.shape),
            whole_spec(col.shape),
            height_spec(sent),
            whole_spec(inner.shape),
            whole_spec(radius.shape),
        ],
        out_specs=whole_spec(shape),
        out_shape=jax.ShapeDtypeStruct(shape, jnp.float32),
        compiler_params=params(40),
        name="pick_outer",
    )(row, col, sent, inner, radius)


def pick_radius(cutoff, obs_x, obs_y, x_start, y_start):
    rows, columns = cutoff.shape
    radius_sq = jnp.square(cutoff.astype(jnp.float32))
    row_is = (obs_x[:, None] - x_start == jnp.arange(rows)[None, :]).astype(jnp.float32)
    col_is = obs_y[:, None] - y_start == jnp.arange(columns)[None, :]
    by_row = jnp.dot(row_is, radius_sq, precision=highest)
    return jnp.sum(jnp.where(col_is, by_row, 0.0), 1)


def exchange(value, axis, distance):
    size = lax.axis_size(axis)
    return lax.ppermute(value, axis, [(i, i ^ distance) for i in range(size)])


def sum_over(value, axis):
    distance = 1
    while distance < lax.axis_size(axis):
        value = value + exchange(value, axis, distance)
        distance *= 2
    return value


def gather_over(value, axis, first=1, width=None):
    width = lax.axis_size(axis) if width is None else width
    return jnp.concatenate(
        [value] + [exchange(value, axis, r * first) for r in range(1, width)], 0
    )


def apart_sq(a, b, size):
    gap = jnp.abs(a - b)
    gap = jnp.minimum(gap, size - gap)
    return gap * gap


def eliminate_four(system, k, row_id):
    width = system.shape[1]
    row = [system[k + i : k + i + 1, :] for i in range(4)]
    p = [
        [jnp.broadcast_to(row[i][:, k + j : k + j + 1], (1, LANES)) for j in range(4)]
        for i in range(4)
    ]

    def wide(value):
        return jnp.concatenate([value] * (width // LANES), 1)

    def inverse(a00, a01, a10, a11):
        scale = 1.0 / (a00 * a11 - a01 * a10)
        return a11 * scale, -a01 * scale, -a10 * scale, a00 * scale

    i00, i01, i10, i11 = inverse(p[0][0], p[0][1], p[1][0], p[1][1])
    y = [
        [i00 * p[0][2 + j] + i01 * p[1][2 + j] for j in range(2)],
        [i10 * p[0][2 + j] + i11 * p[1][2 + j] for j in range(2)],
    ]
    schur = [
        [p[2 + i][2 + j] - p[2 + i][0] * y[0][j] - p[2 + i][1] * y[1][j] for j in range(2)]
        for i in range(2)
    ]
    s00, s01, s10, s11 = inverse(schur[0][0], schur[0][1], schur[1][0], schur[1][1])
    top0 = wide(i00) * row[0] + wide(i01) * row[1]
    top1 = wide(i10) * row[0] + wide(i11) * row[1]
    low0 = row[2] - wide(p[2][0]) * top0 - wide(p[2][1]) * top1
    low1 = row[3] - wide(p[3][0]) * top0 - wide(p[3][1]) * top1
    new2 = wide(s00) * low0 + wide(s01) * low1
    new3 = wide(s10) * low0 + wide(s11) * low1
    new0 = top0 - wide(y[0][0]) * new2 - wide(y[0][1]) * new3
    new1 = top1 - wide(y[1][0]) * new2 - wide(y[1][1]) * new3
    new = (new0, new1, new2, new3)
    result = system
    for i in range(4):
        result = result - system[:, k + i : k + i + 1] * new[i]
    for i in range(4):
        result = jnp.where(row_id == k + i, new[i], result)
    return result


def chain_kernel(
    members,
    sizes,
    start_ref,
    every_ref,
    row_ref,
    col_ref,
    value_ref,
    variance_ref,
    cutoff_ref,
    lhs1_ref,
    lhs2_ref,
    more1_ref,
    more2_ref,
    count_ref,
    local_ref,
    anom_ref,
    mix_ref,
    rank_ref,
    block1_ref,
    block2_ref,
    sem,
):
    size_x, size_y = sizes
    pieces, sources, _, _ = every_ref.shape
    batches, count = value_ref.shape
    groups = batches * count // pieces // LANES
    local_members = members // sources
    rows, columns = cutoff_ref.shape
    tiles = columns // LANES
    x_start = start_ref[0]
    y_start = start_ref[1]
    reach = jnp.max(cutoff_ref[...])
    reach_sq = reach * reach

    heights, radius_sq = [], []
    for j in range(pieces):
        piece = jnp.bitwise_xor(start_ref[2], j)
        for g in range(groups):
            found, radius = [], 0.0
            for source in range(sources):
                one = every_ref.at[piece, jnp.bitwise_xor(start_ref[3], source)]
                found.append(one[g * local_members : (g + 1) * local_members, :])
                last = local_members * groups + g
                radius = radius + one[last : last + 1, :]
            heights.append(jnp.concatenate(found, 0))
            radius_sq.append(radius)
    heights = jnp.concatenate(heights, 1)
    inverse_sq = 1.0 / jnp.concatenate(radius_sq, 1)
    before = (
        lax.broadcasted_iota(jnp.int32, (count, count), 0)
        <= lax.broadcasted_iota(jnp.int32, (count, count), 1)
    ).astype(jnp.bfloat16)
    slot = lax.broadcasted_iota(jnp.int32, (OBS_BLOCK, count), 0)
    twice = lax.broadcasted_iota(jnp.int32, (members, 3 * OBS_BLOCK), 1) < 2 * OBS_BLOCK
    member_row = lax.broadcasted_iota(jnp.int32, (members, LANES + count), 0)
    eye = (
        lax.broadcasted_iota(jnp.int32, (members, members), 0)
        == lax.broadcasted_iota(jnp.int32, (members, members), 1)
    ).astype(jnp.float32)

    def rank_reaching(b, t):
        obs_x = row_ref[0:1, b * count : (b + 1) * count]
        obs_y = row_ref[1:2, b * count : (b + 1) * count]
        off_x = jnp.where(obs_x >= x_start, obs_x - x_start, obs_x - x_start + size_x)
        gap_x = jnp.where(off_x < rows, 0, jnp.minimum(off_x - (rows - 1), size_x - off_x))
        off_y = obs_y - (y_start + t * LANES)
        off_y = jnp.where(off_y >= 0, off_y, off_y + size_y)
        gap_y = jnp.where(off_y < LANES, 0, jnp.minimum(off_y - (LANES - 1), size_y - off_y))
        reaches = gap_x * gap_x + gap_y * gap_y < reach_sq
        flags = jnp.broadcast_to(reaches.astype(jnp.float32), (8, count))
        ranks = jnp.dot(
            flags.astype(jnp.bfloat16), before, preferred_element_type=jnp.float32
        )
        rank_ref[b, t] = jnp.where(reaches, ranks.astype(jnp.int32) - 1, -1)
        count_ref[b, t] = jnp.sum(flags[0:1, :]).astype(jnp.int32)

    def gather(b, t, k, to1, to2):
        chosen = (slot == rank_ref[b, t, 0:1, :] - k * OBS_BLOCK).astype(jnp.float32)
        thrice = jnp.concatenate([chosen] * 3, 0).astype(jnp.bfloat16)
        chosen = chosen.astype(jnp.bfloat16)

        def product(x, y):
            return lax.dot_general(x, y, NT, preferred_element_type=jnp.float32)

        to1[...] = product(chosen, anom_ref[b]).astype(jnp.bfloat16)
        to2[...] = jnp.where(
            twice, product(mix_ref[b, 0], thrice), product(mix_ref[b, 1], thrice)
        ).astype(jnp.bfloat16)

    def localize(b, first, size):
        later = slice((b + 1) * count, batches * count)
        part = slice(first, first + size)
        dist_sq = apart_sq(col_ref[part, b : b + 1], row_ref[0:1, later], size_x) + apart_sq(
            col_ref[part, batches + b : batches + b + 1], row_ref[1:2, later], size_y
        )
        ratio = dist_sq.astype(jnp.float32) * inverse_sq[:, later]
        local_ref[part, later] = jnp.square(jnp.maximum(1.0 - ratio, 0.0))

    for b in range(batches):
        here = slice(b * count, (b + 1) * count)
        prior = heights[:, here]
        mean = jnp.mean(prior, 0, keepdims=True)
        anom = prior - mean
        precision = 1.0 / variance_ref[b : b + 1, :]
        innov = value_ref[b : b + 1, :] - mean
        scaled = anom * precision
        inner = eye + lax.dot_general(
            scaled, anom, NT, precision=highest, preferred_element_type=jnp.float32
        ) / (members - 1)
        proj = jnp.sum(scaled * innov, 1, keepdims=True)
        system = jnp.concatenate(
            [inner, proj, jnp.zeros((members, LANES - members - 1), jnp.float32), scaled], 1
        )
        aside = [functools.partial(rank_reaching, b, t) for t in range(tiles)]
        if b > 0:
            aside += [
                functools.partial(gather, b - 1, t, 0, lhs1_ref.at[b - 1, t], lhs2_ref.at[b - 1, t])
                for t in range(tiles)
            ]
        if b + 1 < batches:
            aside += [functools.partial(localize, b, first, 32) for first in range(0, count, 32)]
        steps = members // 4
        for step in range(steps):
            system = eliminate_four(system, 4 * step, member_row)
            for one in aside[step::steps]:
                one()
        solved_proj = system[:, members : members + 1]
        solved_anom = system[:, LANES:]
        solved_innov = precision * (
            innov - jnp.sum(anom * solved_proj, 0, keepdims=True) / (members - 1)
        )
        mix = (solved_innov - 0.5 * solved_anom) / (members - 1)
        high, low = split_bf16(anom)
        cells = row_ref[:, here]
        cells = jnp.concatenate([cells // 256, cells % 256] * 4, 0).astype(jnp.float32)
        anom_ref[b] = jnp.concatenate([high, high, low, cells.astype(jnp.bfloat16)], 0)
        mix_high, mix_low = split_bf16(mix)
        mix_ref[b, 0] = mix_high
        mix_ref[b, 1] = mix_low

        if b + 1 < batches:
            later = slice((b + 1) * count, batches * count)
            ahead = heights[:, later]
            ahead_anom = ahead - jnp.mean(ahead, 0, keepdims=True)
            cross = lax.dot_general(
                anom, ahead_anom, TN, precision=highest, preferred_element_type=jnp.float32
            )
            high, low = split_bf16(cross * local_ref[:, later])
            both = jnp.dot(
                jnp.concatenate([mix_high, mix_low], 0), high, preferred_element_type=jnp.float32
            )
            rest = jnp.dot(mix_high, low, preferred_element_type=jnp.float32)
            ahead = ahead + (both[:members] + (both[members:] + rest))
            heights = jnp.concatenate([heights[:, : (b + 1) * count], ahead], 1)

    for t in range(tiles):
        gather(batches - 1, t, 0, lhs1_ref.at[batches - 1, t], lhs2_ref.at[batches - 1, t])
    counts = [[count_ref[b, t] for t in range(tiles)] for b in range(batches)]
    most = functools.reduce(jnp.maximum, sum(counts, []))

    @pl.when(most > OBS_BLOCK)
    def _():
        for b in range(batches):
            for t in range(tiles):

                def more(k, _, b=b, t=t):
                    gather(b, t, k, block1_ref, block2_ref)
                    for i, (block, to) in enumerate(
                        ((block1_ref, more1_ref), (block2_ref, more2_ref))
                    ):
                        copy = pltpu.make_async_copy(block, to.at[b, t, k - 1], sem.at[i])
                        copy.start()
                        copy.wait()
                    return 0

                blocks = (counts[b][t] + (OBS_BLOCK - 1)) // OBS_BLOCK
                lax.fori_loop(1, blocks, more, 0)


def chain(members, start, every, obs_x, obs_y, values, variance, cutoff, sizes):
    batches, count = values.shape
    row_form = jnp.stack([obs_x.reshape(-1), obs_y.reshape(-1)], 0)
    col_form = jnp.concatenate([obs_x, obs_y], 0).T
    tiles = cutoff.shape[1] // LANES
    first = (batches, tiles)
    more = first + (max(-(-count // OBS_BLOCK) - 1, 1),)
    shape1 = (OBS_BLOCK, 3 * members + 16)
    shape2 = (members, 3 * OBS_BLOCK)
    return pl.pallas_call(
        functools.partial(chain_kernel, members, sizes),
        in_specs=smem() + vmem(6),
        out_specs=vmem(2) + hbm(2) + smem(),
        out_shape=[
            jax.ShapeDtypeStruct(lead + shape, jnp.bfloat16)
            for lead in (first, more)
            for shape in (shape1, shape2)
        ]
        + [jax.ShapeDtypeStruct(first, jnp.int32)],
        scratch_shapes=[
            pltpu.VMEM((count, batches * count), jnp.float32),
            pltpu.VMEM((batches, 3 * members + 16, count), jnp.bfloat16),
            pltpu.VMEM((batches, 2, members, count), jnp.bfloat16),
            pltpu.VMEM((batches, tiles, 8, count), jnp.int32),
            pltpu.VMEM(shape1, jnp.bfloat16),
            pltpu.VMEM(shape2, jnp.bfloat16),
            pltpu.SemaphoreType.DMA((2,)),
        ],
        compiler_params=params(16),
        cost_estimate=CHAIN_COST,
        name="chain",
    )(start, every, row_form, col_form, values, variance, cutoff)


def update_kernel(
    sizes,
    continues,
    tile_ref,
    start_ref,
    count_ref,
    state_ref,
    cutoff_ref,
    lhs1_ref,
    lhs2_ref,
    more1_ref,
    more2_ref,
    *rest,
):
    out_ref, members_ref, rhs_ref, block1_ref, block2_ref, sem = rest[1:] if continues else rest
    size_x, size_y = float(sizes[0]), float(sizes[1])
    sources, _, _, local_members, fields, rows, _ = state_ref.shape
    members = sources * local_members
    batches = lhs1_ref.shape[0]
    cells = rows * LANES
    t = pl.program_id(1)
    flat = state_ref.reshape(members * fields * rows, LANES)
    flat_out = out_ref.reshape(members * fields * rows, LANES)
    row0 = (start_ref[0] + tile_ref[pl.program_id(0)] * rows).astype(jnp.float32)
    col0 = (start_ref[1] + t * LANES).astype(jnp.float32)
    lane = lax.broadcasted_iota(jnp.int32, (1, LANES), 1).astype(jnp.float32)
    radius = cutoff_ref[...].astype(jnp.float32)
    radius_sq = radius * radius
    inverse = 1.0 / radius_sq

    def localized(lhs1):
        place = lhs1[:, 3 * members :].astype(jnp.float32)
        obs_x = jnp.broadcast_to(place[:, 0:1] * 256.0 + place[:, 2:3], (OBS_BLOCK, LANES))
        obs_y = jnp.broadcast_to(place[:, 1:2] * 256.0 + place[:, 3:4], (OBS_BLOCK, LANES))
        dist_y = apart_sq(obs_y, lane + col0, size_y)
        dist_x = apart_sq(obs_x, lane + row0, size_x)
        weights = []
        for r in range(rows):
            ratio = (dist_y + dist_x[:, r : r + 1]) * inverse[r : r + 1, :]
            weights.append(jnp.square(jnp.maximum(1.0 - ratio, 0.0)))
        return jnp.concatenate(weights, 1)

    def crossed(lhs1, rhs):
        return jnp.dot(lhs1[:, : 3 * members], rhs, preferred_element_type=jnp.float32)

    def moved(lhs2, cross, weights):
        high, low = split_bf16(cross * weights)
        return jnp.dot(
            lhs2, jnp.concatenate([high, low, high], 0), preferred_element_type=jnp.float32
        )

    def split_anom(state):
        high, low = split_bf16(state - jnp.mean(state, 0, keepdims=True))
        return jnp.concatenate([high, low, high], 0)

    def load(f):
        return jnp.concatenate(
            [
                flat[pl.ds(f * rows + r, members, stride=fields * rows), :]
                for r in range(rows)
            ],
            1,
        )

    def store(f, state):
        for r in range(rows):
            flat_out[pl.ds(f * rows + r, members, stride=fields * rows), :] = state[
                :, r * LANES : (r + 1) * LANES
            ]

    most = count_ref[0, t]
    for b in range(1, batches):
        most = jnp.maximum(most, count_ref[b, t])

    @pl.when(most <= OBS_BLOCK)
    def _():
        states = [load(f) for f in range(fields)]
        for b in range(batches):
            lhs1 = lhs1_ref[b, 0]
            weights = localized(lhs1)
            cross = [crossed(lhs1, x) for x in [split_anom(state) for state in states]]
            steps = [moved(lhs2_ref[b, 0], c, weights) for c in cross]
            states = [state + step for state, step in zip(states, steps)]
        for f in range(fields):
            store(f, states[f])

    @pl.when(most > OBS_BLOCK)
    def _():
        for f in range(fields):
            members_ref[f] = load(f)
        for b in range(batches):
            for f in range(fields):
                rhs_ref[f] = split_anom(members_ref[f])

            def add(lhs1, lhs2):
                weights = localized(lhs1)
                for f in range(fields):
                    members_ref[f] += moved(lhs2, crossed(lhs1, rhs_ref[f]), weights)

            def block(k, _, b=b):
                for i, (more, to) in enumerate(((more1_ref, block1_ref), (more2_ref, block2_ref))):
                    copy = pltpu.make_async_copy(more.at[b, t, k - 1], to, sem.at[i])
                    copy.start()
                    copy.wait()
                add(block1_ref[...], block2_ref[...])
                return 0

            add(lhs1_ref[b, 0], lhs2_ref[b, 0])
            blocks = (count_ref[b, t] + (OBS_BLOCK - 1)) // OBS_BLOCK
            lax.fori_loop(1, blocks, block, 0)
        for f in range(fields):
            store(f, members_ref[f])


def update(row_tiles, start, counts, state, cutoff, lhs, sizes, begun=None):
    sources, _, tiles, local_members, fields, _, _ = state.shape
    members = sources * local_members
    rows = cutoff.shape[0]
    columns = tiles * LANES
    cells = ROW_TILE * LANES

    def of_tile(array):
        shape = (array.shape[0], 1) + array.shape[2:]
        return pl.BlockSpec(shape, lambda i, t, tile: (0, t) + (0,) * (array.ndim - 2))

    operands = [row_tiles, start, counts, state, cutoff, *lhs]
    in_specs = smem(2) + [
        pl.BlockSpec(
            (sources, 1, 1, local_members, fields, ROW_TILE, LANES),
            lambda i, t, tile: (0, i, t, 0, 0, 0, 0),
        ),
        pl.BlockSpec((ROW_TILE, LANES), lambda i, t, tile: (tile[i], t)),
        of_tile(lhs[0]),
        of_tile(lhs[1]),
    ] + hbm(2)
    aliases = {}
    if begun is not None:
        aliases = {len(operands): 0}
        operands.append(begun)
        in_specs.append(pl.BlockSpec(memory_space=pl.ANY))
    return pl.pallas_call(
        functools.partial(update_kernel, sizes, begun is not None),
        grid_spec=pltpu.PrefetchScalarGridSpec(
            num_scalar_prefetch=1,
            grid=row_tiles.shape + (tiles,),
            in_specs=in_specs,
            out_specs=pl.BlockSpec(
                (members, fields, ROW_TILE, LANES), lambda i, t, tile: (0, 0, tile[i], t)
            ),
            scratch_shapes=[
                pltpu.VMEM((fields, members, cells), jnp.float32),
                pltpu.VMEM((fields, 3 * members, cells), jnp.bfloat16),
                pltpu.VMEM(lhs[0].shape[2:], jnp.bfloat16),
                pltpu.VMEM(lhs[1].shape[2:], jnp.bfloat16),
                pltpu.SemaphoreType.DMA((2,)),
            ],
        ),
        out_shape=jax.ShapeDtypeStruct((members, fields, rows, columns), jnp.float32),
        input_output_aliases=aliases,
        compiler_params=params(16),
        name="update",
    )(*operands)


def edge_kernel(ens_ref, depth_ref, first_ref, last_ref, sem):
    members, fields, rows, _ = ens_ref.shape
    copies = []
    for i, (out_ref, row) in enumerate(((first_ref, 0), (last_ref, rows - HALO))):
        part = pl.ds(row, HALO)
        for m in range(members):
            to = out_ref.at[pl.ds(m * fields, fields)]
            copies.append(pltpu.make_async_copy(ens_ref.at[m, :, part], to, sem.at[i, m]))
        to = out_ref.at[members * fields]
        copies.append(pltpu.make_async_copy(depth_ref.at[part], to, sem.at[i, members]))
    for copy in copies:
        copy.start()
    for copy in copies:
        copy.wait()


def row_halos(ensemble, depth, axis):
    size = lax.axis_size(axis)
    onward = [(i, (i + 1) % size) for i in range(size)]
    backward = [(j, i) for i, j in onward]
    members, fields, _, columns = ensemble.shape
    edge = jax.ShapeDtypeStruct((members * fields + 1, HALO, columns), jnp.float32)
    first, last = pl.pallas_call(
        edge_kernel,
        in_specs=hbm(2),
        out_specs=vmem(2),
        out_shape=[edge, edge],
        scratch_shapes=[pltpu.SemaphoreType.DMA((2, members + 1))],
        compiler_params=params(16),
        name="edges",
    )(ensemble, depth)
    return lax.ppermute(last, axis, onward), lax.ppermute(first, axis, backward)


def local(ensemble, sea_depth, cutoff, obs_index, obs_value, obs_var):
    ensemble = pltpu.with_memory_space_constraint(ensemble, pltpu.HBM)
    sea_depth = pltpu.with_memory_space_constraint(sea_depth, pltpu.HBM)
    blocks = lax.axis_size("mem")
    subs = lax.axis_size("sub")
    local_members, fields, rows, size_y = ensemble.shape
    members = local_members * blocks
    col_block = size_y // blocks
    size_x = rows * subs
    sizes = (size_x, size_y)
    sub, mem = lax.axis_index("sub"), lax.axis_index("mem")
    x_start = sub * rows
    y_start = mem * col_block
    start = jnp.stack([x_start, y_start, sub, mem]).astype(jnp.int32)
    obs_x = obs_index // size_y
    obs_y = obs_index % size_y
    flat_x = obs_x.reshape(1, -1)
    flat_y = obs_y.reshape(1, -1)

    halos = row_halos(ensemble, sea_depth, "sub") * 2
    radius_part = pick_radius(cutoff, flat_x[0], flat_y[0], x_start, y_start)[None]

    inner_rows = rows - 2 * HALO
    last = rows // ROW_TILE - 1
    sent_inner = forecast("inner", range(1, last), ensemble, sea_depth, blocks)
    received_inner = lax.all_to_all(
        sent_inner, "mem", split_axis=0, concat_axis=0, tiled=True
    )
    row = flat_x - x_start
    inner_heights = pick_inner(row - HALO, flat_y, sent_inner)

    outer_row = jnp.where(
        row < HALO, row, jnp.where(row < rows - HALO, -1, row - inner_rows)
    )
    sent_outer = forecast("outer", [1, last + 1], ensemble, sea_depth, blocks, halos)
    part = pick_outer(outer_row, flat_y, sent_outer, inner_heights, radius_part, subs)
    piece = lax.dynamic_index_in_dim(sum_over(part, "sub"), sub, 0, keepdims=True)
    low = max(blocks // 4, 1)
    every = gather_over(gather_over(piece, "mem", 1, low), "mem", low, blocks // low)
    every, sent_outer = lax.optimization_barrier((every, sent_outer))
    received_outer = lax.all_to_all(
        sent_outer, "mem", split_axis=0, concat_axis=0, tiled=True
    )
    every = gather_over(every[None], "sub")
    *lhs, counts = chain(
        members, start, every, obs_x, obs_y, obs_value, obs_var, cutoff, sizes
    )

    lhs[2:] = [pltpu.with_memory_space_constraint(more, pltpu.HBM) for more in lhs[2:]]

    def analyse(received, row_tiles, begun=None):
        row_tiles = jnp.array(row_tiles, jnp.int32)
        return update(row_tiles, start, counts, received, cutoff, lhs, sizes, begun)

    return analyse(received_outer, [0, last], analyse(received_inner, list(range(1, last))))


def solution(mesh):
    return jax.shard_map(
        local,
        mesh=mesh,
        in_specs=(P("mem", None, "sub", None), P("sub", None), P("sub", "mem"), P(), P(), P()),
        out_specs=P(None, None, "sub", "mem"),
        check_vma=False,
    )
```

```python
import functools

import jax
import jax.numpy as jnp
from jax import lax
from jax.experimental import pallas as pl
from jax.experimental.pallas import tpu as pltpu
from jax.sharding import PartitionSpec as P

STEPS = 4
HALO = 2 * STEPS
LANES = 128
OBS_BLOCK = 48
ROW_TILE = 8
OUTER_COST = pl.CostEstimate(flops=23 * 10**9, bytes_accessed=74 * 10**6, transcendentals=0)
CHAIN_COST = pl.CostEstimate(flops=26 * 10**9, bytes_accessed=85 * 10**6, transcendentals=0)

step_size = 0.3
coriolis = 0.2
highest = lax.Precision.HIGHEST

NT = (((1,), (1,)), ((), ()))
TN = (((0,), (0,)), ((), ()))


def params(mebibytes):
    return pltpu.CompilerParams(vmem_limit_bytes=mebibytes * 2**20)


def vmem(count=1):
    return [pl.BlockSpec(memory_space=pltpu.VMEM)] * count


def hbm(count=1):
    return [pl.BlockSpec(memory_space=pltpu.HBM)] * count


def smem(count=1):
    return [pl.BlockSpec(memory_space=pltpu.SMEM)] * count


def split_bf16(value):
    high = value.astype(jnp.bfloat16)
    low = (value - high.astype(jnp.float32)).astype(jnp.bfloat16)
    return high, low


def row_centred(field):
    return pltpu.roll(field, field.shape[0] - 1, 0) - pltpu.roll(field, 1, 0)


def column_centred(tile_of, tiles):
    onward, back = [None] * tiles, [None] * tiles

    def at(t):
        for n in ((t - 1) % tiles, t, (t + 1) % tiles):
            if onward[n] is None:
                tile = tile_of(n)
                onward[n] = pltpu.roll(tile, LANES - 1, 1)
                back[n] = pltpu.roll(tile, 1, 1)
        lane = lax.broadcasted_iota(jnp.int32, onward[t].shape, 1)
        return jnp.where(
            lane == LANES - 1, onward[(t + 1) % tiles], onward[t]
        ) - jnp.where(lane == 0, back[(t - 1) % tiles], back[t])

    return at


def forecast_steps(height, east, north, half_depth):
    tiles = height.shape[0]
    half = 0.5 * step_size
    turn = step_size * coriolis
    for _ in range(STEPS):
        slope = column_centred(lambda t: half * height[t], tiles)
        for t in range(tiles):
            u, v = east[t], north[t]
            slope_y = slope(t)
            east[t] = u + turn * v - row_centred(half * height[t])
            north[t] = v - turn * u - slope_y
        inflow = column_centred(lambda t: half_depth[t] * north[t], tiles)
        for t in range(tiles):
            flow_y = inflow(t)
            height[t] = height[t] - (row_centred(half_depth[t] * east[t]) + flow_y)


def forecast_kernel(joins, kept, *refs):
    ens_ref, depth_ref, *halos, out_ref, height, east, north, half_depth = refs
    tiles = height.shape[0]
    out_tiles = out_ref.shape[2]
    fields = ens_ref.shape[1]

    def window(block, above, below, t):
        part = slice(t * LANES, (t + 1) * LANES)
        if not joins:
            return block[:, part]
        return jnp.concatenate([above[:, part], block[:, part], below[:, part]], 0)

    up_ref, down_ref, depth_up_ref, depth_down_ref = halos if joins else [None] * 4

    @pl.when(pl.program_id(0) == 0)
    def _():
        for t in range(tiles):
            above, below = (depth_up_ref.at[0], depth_down_ref.at[0]) if joins else (None, None)
            half_depth[t] = (0.5 * step_size) * window(depth_ref, above, below, t)

    state = (height, east, north)
    for f in range(fields):
        above, below = (up_ref.at[f], down_ref.at[f]) if joins else (None, None)
        for t in range(tiles):
            state[f][t] = window(ens_ref.at[0, f], above, below, t)
    forecast_steps(*state, half_depth)
    for f in range(fields):
        for t in range(tiles):
            for place, tile in enumerate(kept):
                out_ref[t // out_tiles, place, t % out_tiles, 0, f] = state[f][
                    t, tile * ROW_TILE : (tile + 1) * ROW_TILE
                ]


def forecast(name, kept, ensemble, depth, blocks, halos=()):
    members, fields, rows, columns = ensemble.shape
    tiles = columns // LANES
    window_rows = rows + (2 * HALO if halos else 0)
    out_shape = (blocks, len(kept), tiles // blocks, members, fields, ROW_TILE, LANES)
    in_specs = [
        pl.BlockSpec((1, fields, rows, columns), lambda m: (m, 0, 0, 0)),
        pl.BlockSpec((rows, columns), lambda m: (0, 0)),
    ]
    if halos:
        in_specs += [pl.BlockSpec((fields, HALO, columns), lambda m: (m, 0, 0))] * 2
        in_specs += [pl.BlockSpec((1, HALO, columns), lambda m: (members * fields, 0, 0))] * 2
    return pl.pallas_call(
        functools.partial(forecast_kernel, bool(halos), kept),
        grid=(members,),
        in_specs=in_specs,
        out_specs=pl.BlockSpec(
            out_shape[:3] + (1,) + out_shape[4:], lambda m: (0, 0, 0, m, 0, 0, 0)
        ),
        out_shape=jax.ShapeDtypeStruct(out_shape, jnp.float32),
        scratch_shapes=[pltpu.VMEM((tiles, window_rows, LANES), jnp.float32)] * 4,
        compiler_params=params(16),
        cost_estimate=OUTER_COST if halos else None,
        name=name,
    )(ensemble, depth, *halos)


def pick(row_ref, col_ref, height_ref):
    blocks, row_tiles, tiles, members, _, _, _ = height_ref.shape
    rows = row_tiles * ROW_TILE
    heights = jnp.concatenate(
        [
            height_ref[d, :, t, :, 0].reshape(rows * members, LANES)
            for d in range(blocks)
            for t in range(tiles)
        ],
        1,
    )
    high, rest = heights.astype(jnp.bfloat16), heights
    pieces = [high]
    for _ in range(2):
        rest = rest - pieces[-1].astype(jnp.float32)
        pieces.append(rest.astype(jnp.bfloat16))
    count = col_ref.shape[1]
    column = lax.broadcasted_iota(jnp.int32, (heights.shape[1], count), 0)
    in_column = (column == col_ref[...]).astype(jnp.float32).astype(jnp.bfloat16)
    found = jnp.dot(
        jnp.concatenate(pieces, 0), in_column, preferred_element_type=jnp.float32
    )
    size = members * rows
    found = (found[:size] + found[size : 2 * size]) + found[2 * size :]
    found = found.reshape(row_tiles, members, ROW_TILE, count)
    row = lax.broadcasted_iota(jnp.int32, (1, ROW_TILE, count), 1)
    result = 0.0
    for i in range(row_tiles):
        here = row + i * ROW_TILE == row_ref[...][None]
        result = result + jnp.sum(jnp.where(here, found[i], 0.0), 1)
    return result


def pick_inner_kernel(row_ref, col_ref, height_ref, out_ref):
    out_ref[...] = pick(row_ref, col_ref, height_ref)


def pick_outer_kernel(row_ref, col_ref, height_ref, inner_ref, radius_ref, out_ref):
    heights = pick(row_ref, col_ref, height_ref) + inner_ref[...]
    members, count = heights.shape
    pieces = out_ref.shape[0]
    groups = count // pieces // LANES
    out_ref[...] = jnp.zeros_like(out_ref)
    for j in range(pieces):
        for g in range(groups):
            part = slice((j * groups + g) * LANES, (j * groups + g + 1) * LANES)
            for m in range(members):
                row = g * members + m
                out_ref[j, row : row + 1, :] = heights[m : m + 1, part]
            row = members * groups + g
            out_ref[j, row : row + 1, :] = radius_ref[:, part]


def height_spec(sent):
    shape = sent.shape[:4] + (1,) + sent.shape[5:]
    return pl.BlockSpec(shape, lambda i: (0,) * len(shape))


def whole_spec(shape):
    return pl.BlockSpec(shape, lambda i: (0,) * len(shape))


def pick_inner(row, col, sent):
    shape = (sent.shape[3], col.shape[1])
    return pl.pallas_call(
        pick_inner_kernel,
        grid=(1,),
        in_specs=[whole_spec(row.shape), whole_spec(col.shape), height_spec(sent)],
        out_specs=whole_spec(shape),
        out_shape=jax.ShapeDtypeStruct(shape, jnp.float32),
        compiler_params=params(40),
        name="pick_inner",
    )(row, col, sent)


def pick_outer(row, col, sent, inner, radius, pieces):
    members, count = inner.shape
    used = (members + 1) * (count // pieces // LANES)
    shape = (pieces, used + -used % 8, LANES)
    return pl.pallas_call(
        pick_outer_kernel,
        grid=(1,),
        in_specs=[
            whole_spec(row.shape),
            whole_spec(col.shape),
            height_spec(sent),
            whole_spec(inner.shape),
            whole_spec(radius.shape),
        ],
        out_specs=whole_spec(shape),
        out_shape=jax.ShapeDtypeStruct(shape, jnp.float32),
        compiler_params=params(40),
        name="pick_outer",
    )(row, col, sent, inner, radius)


def pick_radius(cutoff, obs_x, obs_y, x_start, y_start):
    rows, columns = cutoff.shape
    radius_sq = jnp.square(cutoff.astype(jnp.float32))
    row_is = (obs_x[:, None] - x_start == jnp.arange(rows)[None, :]).astype(jnp.float32)
    col_is = obs_y[:, None] - y_start == jnp.arange(columns)[None, :]
    by_row = jnp.dot(row_is, radius_sq, precision=highest)
    return jnp.sum(jnp.where(col_is, by_row, 0.0), 1)


def exchange(value, axis, distance):
    size = lax.axis_size(axis)
    return lax.ppermute(value, axis, [(i, i ^ distance) for i in range(size)])


def sum_over(value, axis):
    distance = 1
    while distance < lax.axis_size(axis):
        value = value + exchange(value, axis, distance)
        distance *= 2
    return value


def gather_over(value, axis, first=1, width=None):
    width = lax.axis_size(axis) if width is None else width
    return jnp.concatenate(
        [value] + [exchange(value, axis, r * first) for r in range(1, width)], 0
    )


def apart_sq(a, b, size):
    gap = jnp.abs(a - b)
    gap = jnp.minimum(gap, size - gap)
    return gap * gap


def eliminate_four(system, k, row_id):
    width = system.shape[1]
    row = [system[k + i : k + i + 1, :] for i in range(4)]
    p = [
        [jnp.broadcast_to(row[i][:, k + j : k + j + 1], (1, LANES)) for j in range(4)]
        for i in range(4)
    ]

    def wide(value):
        return jnp.concatenate([value] * (width // LANES), 1)

    def inverse(a00, a01, a10, a11):
        scale = 1.0 / (a00 * a11 - a01 * a10)
        return a11 * scale, -a01 * scale, -a10 * scale, a00 * scale

    i00, i01, i10, i11 = inverse(p[0][0], p[0][1], p[1][0], p[1][1])
    y = [
        [i00 * p[0][2 + j] + i01 * p[1][2 + j] for j in range(2)],
        [i10 * p[0][2 + j] + i11 * p[1][2 + j] for j in range(2)],
    ]
    schur = [
        [p[2 + i][2 + j] - p[2 + i][0] * y[0][j] - p[2 + i][1] * y[1][j] for j in range(2)]
        for i in range(2)
    ]
    s00, s01, s10, s11 = inverse(schur[0][0], schur[0][1], schur[1][0], schur[1][1])
    top0 = wide(i00) * row[0] + wide(i01) * row[1]
    top1 = wide(i10) * row[0] + wide(i11) * row[1]
    low0 = row[2] - wide(p[2][0]) * top0 - wide(p[2][1]) * top1
    low1 = row[3] - wide(p[3][0]) * top0 - wide(p[3][1]) * top1
    new2 = wide(s00) * low0 + wide(s01) * low1
    new3 = wide(s10) * low0 + wide(s11) * low1
    new0 = top0 - wide(y[0][0]) * new2 - wide(y[0][1]) * new3
    new1 = top1 - wide(y[1][0]) * new2 - wide(y[1][1]) * new3
    new = (new0, new1, new2, new3)
    result = system
    for i in range(4):
        result = result - system[:, k + i : k + i + 1] * new[i]
    for i in range(4):
        result = jnp.where(row_id == k + i, new[i], result)
    return result


def chain_kernel(
    members,
    sizes,
    start_ref,
    every_ref,
    row_ref,
    col_ref,
    value_ref,
    variance_ref,
    cutoff_ref,
    lhs1_ref,
    lhs2_ref,
    more1_ref,
    more2_ref,
    count_ref,
    local_ref,
    anom_ref,
    mix_ref,
    rank_ref,
    block1_ref,
    block2_ref,
    sem,
):
    size_x, size_y = sizes
    pieces, sources, _, _ = every_ref.shape
    batches, count = value_ref.shape
    groups = batches * count // pieces // LANES
    local_members = members // sources
    rows, columns = cutoff_ref.shape
    tiles = columns // LANES
    x_start = start_ref[0]
    y_start = start_ref[1]
    reach = jnp.max(cutoff_ref[...])
    reach_sq = reach * reach

    heights, radius_sq = [], []
    for j in range(pieces):
        piece = jnp.bitwise_xor(start_ref[2], j)
        for g in range(groups):
            found, radius = [], 0.0
            for source in range(sources):
                one = every_ref.at[piece, jnp.bitwise_xor(start_ref[3], source)]
                found.append(one[g * local_members : (g + 1) * local_members, :])
                last = local_members * groups + g
                radius = radius + one[last : last + 1, :]
            heights.append(jnp.concatenate(found, 0))
            radius_sq.append(radius)
    heights = jnp.concatenate(heights, 1)
    inverse_sq = 1.0 / jnp.concatenate(radius_sq, 1)
    before = (
        lax.broadcasted_iota(jnp.int32, (count, count), 0)
        <= lax.broadcasted_iota(jnp.int32, (count, count), 1)
    ).astype(jnp.bfloat16)
    slot = lax.broadcasted_iota(jnp.int32, (OBS_BLOCK, count), 0)
    twice = lax.broadcasted_iota(jnp.int32, (members, 3 * OBS_BLOCK), 1) < 2 * OBS_BLOCK
    member_row = lax.broadcasted_iota(jnp.int32, (members, LANES + count), 0)
    eye = (
        lax.broadcasted_iota(jnp.int32, (members, members), 0)
        == lax.broadcasted_iota(jnp.int32, (members, members), 1)
    ).astype(jnp.float32)

    def rank_reaching(b, t):
        obs_x = row_ref[0:1, b * count : (b + 1) * count]
        obs_y = row_ref[1:2, b * count : (b + 1) * count]
        off_x = jnp.where(obs_x >= x_start, obs_x - x_start, obs_x - x_start + size_x)
        gap_x = jnp.where(off_x < rows, 0, jnp.minimum(off_x - (rows - 1), size_x - off_x))
        off_y = obs_y - (y_start + t * LANES)
        off_y = jnp.where(off_y >= 0, off_y, off_y + size_y)
        gap_y = jnp.where(off_y < LANES, 0, jnp.minimum(off_y - (LANES - 1), size_y - off_y))
        reaches = gap_x * gap_x + gap_y * gap_y < reach_sq
        flags = jnp.broadcast_to(reaches.astype(jnp.float32), (8, count))
        ranks = jnp.dot(
            flags.astype(jnp.bfloat16), before, preferred_element_type=jnp.float32
        )
        rank_ref[b, t] = jnp.where(reaches, ranks.astype(jnp.int32) - 1, -1)
        count_ref[b, t] = jnp.sum(flags[0:1, :]).astype(jnp.int32)

    def gather(b, t, k, to1, to2):
        chosen = (slot == rank_ref[b, t, 0:1, :] - k * OBS_BLOCK).astype(jnp.float32)
        thrice = jnp.concatenate([chosen] * 3, 0).astype(jnp.bfloat16)
        chosen = chosen.astype(jnp.bfloat16)

        def product(x, y):
            return lax.dot_general(x, y, NT, preferred_element_type=jnp.float32)

        to1[...] = product(chosen, anom_ref[b]).astype(jnp.bfloat16)
        to2[...] = jnp.where(
            twice, product(mix_ref[b, 0], thrice), product(mix_ref[b, 1], thrice)
        ).astype(jnp.bfloat16)

    def localize(b, first, size):
        later = slice((b + 1) * count, batches * count)
        part = slice(first, first + size)
        dist_sq = apart_sq(col_ref[part, b : b + 1], row_ref[0:1, later], size_x) + apart_sq(
            col_ref[part, batches + b : batches + b + 1], row_ref[1:2, later], size_y
        )
        ratio = dist_sq.astype(jnp.float32) * inverse_sq[:, later]
        local_ref[part, later] = jnp.square(jnp.maximum(1.0 - ratio, 0.0))

    for b in range(batches):
        here = slice(b * count, (b + 1) * count)
        prior = heights[:, here]
        mean = jnp.mean(prior, 0, keepdims=True)
        anom = prior - mean
        precision = 1.0 / variance_ref[b : b + 1, :]
        innov = value_ref[b : b + 1, :] - mean
        scaled = anom * precision
        inner = eye + lax.dot_general(
            scaled, anom, NT, precision=highest, preferred_element_type=jnp.float32
        ) / (members - 1)
        proj = jnp.sum(scaled * innov, 1, keepdims=True)
        system = jnp.concatenate(
            [inner, proj, jnp.zeros((members, LANES - members - 1), jnp.float32), scaled], 1
        )
        aside = [functools.partial(rank_reaching, b, t) for t in range(tiles)]
        if b > 0:
            aside += [
                functools.partial(gather, b - 1, t, 0, lhs1_ref.at[b - 1, t], lhs2_ref.at[b - 1, t])
                for t in range(tiles)
            ]
        if b + 1 < batches:
            aside += [functools.partial(localize, b, first, 32) for first in range(0, count, 32)]
        steps = members // 4
        for step in range(steps):
            system = eliminate_four(system, 4 * step, member_row)
            for one in aside[step::steps]:
                one()
        solved_proj = system[:, members : members + 1]
        solved_anom = system[:, LANES:]
        solved_innov = precision * (
            innov - jnp.sum(anom * solved_proj, 0, keepdims=True) / (members - 1)
        )
        mix = (solved_innov - 0.5 * solved_anom) / (members - 1)
        high, low = split_bf16(anom)
        cells = row_ref[:, here]
        cells = jnp.concatenate([cells // 256, cells % 256] * 4, 0).astype(jnp.float32)
        anom_ref[b] = jnp.concatenate([high, high, low, cells.astype(jnp.bfloat16)], 0)
        mix_high, mix_low = split_bf16(mix)
        mix_ref[b, 0] = mix_high
        mix_ref[b, 1] = mix_low

        if b + 1 < batches:
            later = slice((b + 1) * count, batches * count)
            ahead = heights[:, later]
            ahead_anom = ahead - jnp.mean(ahead, 0, keepdims=True)
            cross = lax.dot_general(
                anom, ahead_anom, TN, precision=highest, preferred_element_type=jnp.float32
            )
            high, low = split_bf16(cross * local_ref[:, later])
            both = jnp.dot(
                jnp.concatenate([mix_high, mix_low], 0), high, preferred_element_type=jnp.float32
            )
            rest = jnp.dot(mix_high, low, preferred_element_type=jnp.float32)
            ahead = ahead + (both[:members] + (both[members:] + rest))
            heights = jnp.concatenate([heights[:, : (b + 1) * count], ahead], 1)

    for t in range(tiles):
        gather(batches - 1, t, 0, lhs1_ref.at[batches - 1, t], lhs2_ref.at[batches - 1, t])
    counts = [[count_ref[b, t] for t in range(tiles)] for b in range(batches)]
    most = functools.reduce(jnp.maximum, sum(counts, []))

    @pl.when(most > OBS_BLOCK)
    def _():
        for b in range(batches):
            for t in range(tiles):

                def more(k, _, b=b, t=t):
                    gather(b, t, k, block1_ref, block2_ref)
                    for i, (block, to) in enumerate(
                        ((block1_ref, more1_ref), (block2_ref, more2_ref))
                    ):
                        copy = pltpu.make_async_copy(block, to.at[b, t, k - 1], sem.at[i])
                        copy.start()
                        copy.wait()
                    return 0

                blocks = (counts[b][t] + (OBS_BLOCK - 1)) // OBS_BLOCK
                lax.fori_loop(1, blocks, more, 0)


def chain(members, start, every, obs_x, obs_y, values, variance, cutoff, sizes):
    batches, count = values.shape
    row_form = jnp.stack([obs_x.reshape(-1), obs_y.reshape(-1)], 0)
    col_form = jnp.concatenate([obs_x, obs_y], 0).T
    tiles = cutoff.shape[1] // LANES
    first = (batches, tiles)
    more = first + (max(-(-count // OBS_BLOCK) - 1, 1),)
    shape1 = (OBS_BLOCK, 3 * members + 16)
    shape2 = (members, 3 * OBS_BLOCK)
    return pl.pallas_call(
        functools.partial(chain_kernel, members, sizes),
        in_specs=smem() + vmem(6),
        out_specs=vmem(2) + hbm(2) + smem(),
        out_shape=[
            jax.ShapeDtypeStruct(lead + shape, jnp.bfloat16)
            for lead in (first, more)
            for shape in (shape1, shape2)
        ]
        + [jax.ShapeDtypeStruct(first, jnp.int32)],
        scratch_shapes=[
            pltpu.VMEM((count, batches * count), jnp.float32),
            pltpu.VMEM((batches, 3 * members + 16, count), jnp.bfloat16),
            pltpu.VMEM((batches, 2, members, count), jnp.bfloat16),
            pltpu.VMEM((batches, tiles, 8, count), jnp.int32),
            pltpu.VMEM(shape1, jnp.bfloat16),
            pltpu.VMEM(shape2, jnp.bfloat16),
            pltpu.SemaphoreType.DMA((2,)),
        ],
        compiler_params=params(16),
        cost_estimate=CHAIN_COST,
        name="chain",
    )(start, every, row_form, col_form, values, variance, cutoff)


def update_kernel(
    sizes,
    continues,
    tile_ref,
    start_ref,
    count_ref,
    state_ref,
    cutoff_ref,
    lhs1_ref,
    lhs2_ref,
    more1_ref,
    more2_ref,
    *rest,
):
    out_ref, members_ref, rhs_ref, block1_ref, block2_ref, sem = rest[1:] if continues else rest
    size_x, size_y = float(sizes[0]), float(sizes[1])
    sources, _, _, local_members, fields, rows, _ = state_ref.shape
    members = sources * local_members
    batches = lhs1_ref.shape[0]
    cells = rows * LANES
    t = pl.program_id(1)
    flat = state_ref.reshape(members * fields * rows, LANES)
    flat_out = out_ref.reshape(members * fields * rows, LANES)
    row0 = (start_ref[0] + tile_ref[pl.program_id(0)] * rows).astype(jnp.float32)
    col0 = (start_ref[1] + t * LANES).astype(jnp.float32)
    lane = lax.broadcasted_iota(jnp.int32, (1, LANES), 1).astype(jnp.float32)
    radius = cutoff_ref[...].astype(jnp.float32)
    radius_sq = radius * radius
    inverse = 1.0 / radius_sq

    def localized(lhs1):
        place = lhs1[:, 3 * members :].astype(jnp.float32)
        obs_x = jnp.broadcast_to(place[:, 0:1] * 256.0 + place[:, 2:3], (OBS_BLOCK, LANES))
        obs_y = jnp.broadcast_to(place[:, 1:2] * 256.0 + place[:, 3:4], (OBS_BLOCK, LANES))
        dist_y = apart_sq(obs_y, lane + col0, size_y)
        dist_x = apart_sq(obs_x, lane + row0, size_x)
        weights = []
        for r in range(rows):
            ratio = (dist_y + dist_x[:, r : r + 1]) * inverse[r : r + 1, :]
            weights.append(jnp.square(jnp.maximum(1.0 - ratio, 0.0)))
        return jnp.concatenate(weights, 1)

    def crossed(lhs1, rhs):
        return jnp.dot(lhs1[:, : 3 * members], rhs, preferred_element_type=jnp.float32)

    def moved(lhs2, cross, weights):
        high, low = split_bf16(cross * weights)
        return jnp.dot(
            lhs2, jnp.concatenate([high, low, high], 0), preferred_element_type=jnp.float32
        )

    def split_anom(state):
        high, low = split_bf16(state - jnp.mean(state, 0, keepdims=True))
        return jnp.concatenate([high, low, high], 0)

    def load(f):
        return jnp.concatenate(
            [
                flat[pl.ds(f * rows + r, members, stride=fields * rows), :]
                for r in range(rows)
            ],
            1,
        )

    def store(f, state):
        for r in range(rows):
            flat_out[pl.ds(f * rows + r, members, stride=fields * rows), :] = state[
                :, r * LANES : (r + 1) * LANES
            ]

    most = count_ref[0, t]
    for b in range(1, batches):
        most = jnp.maximum(most, count_ref[b, t])

    @pl.when(most <= OBS_BLOCK)
    def _():
        states = [load(f) for f in range(fields)]
        for b in range(batches):
            lhs1 = lhs1_ref[b, 0]
            weights = localized(lhs1)
            cross = [crossed(lhs1, x) for x in [split_anom(state) for state in states]]
            steps = [moved(lhs2_ref[b, 0], c, weights) for c in cross]
            states = [state + step for state, step in zip(states, steps)]
        for f in range(fields):
            store(f, states[f])

    @pl.when(most > OBS_BLOCK)
    def _():
        for f in range(fields):
            members_ref[f] = load(f)
        for b in range(batches):
            for f in range(fields):
                rhs_ref[f] = split_anom(members_ref[f])

            def add(lhs1, lhs2):
                weights = localized(lhs1)
                for f in range(fields):
                    members_ref[f] += moved(lhs2, crossed(lhs1, rhs_ref[f]), weights)

            def block(k, _, b=b):
                for i, (more, to) in enumerate(((more1_ref, block1_ref), (more2_ref, block2_ref))):
                    copy = pltpu.make_async_copy(more.at[b, t, k - 1], to, sem.at[i])
                    copy.start()
                    copy.wait()
                add(block1_ref[...], block2_ref[...])
                return 0

            add(lhs1_ref[b, 0], lhs2_ref[b, 0])
            blocks = (count_ref[b, t] + (OBS_BLOCK - 1)) // OBS_BLOCK
            lax.fori_loop(1, blocks, block, 0)
        for f in range(fields):
            store(f, members_ref[f])


def update(row_tiles, start, counts, state, cutoff, lhs, sizes, begun=None):
    sources, _, tiles, local_members, fields, _, _ = state.shape
    members = sources * local_members
    rows = cutoff.shape[0]
    columns = tiles * LANES
    cells = ROW_TILE * LANES

    def of_tile(array):
        shape = (array.shape[0], 1) + array.shape[2:]
        return pl.BlockSpec(shape, lambda i, t, tile: (0, t) + (0,) * (array.ndim - 2))

    operands = [row_tiles, start, counts, state, cutoff, *lhs]
    in_specs = smem(2) + [
        pl.BlockSpec(
            (sources, 1, 1, local_members, fields, ROW_TILE, LANES),
            lambda i, t, tile: (0, i, t, 0, 0, 0, 0),
        ),
        pl.BlockSpec((ROW_TILE, LANES), lambda i, t, tile: (tile[i], t)),
        of_tile(lhs[0]),
        of_tile(lhs[1]),
    ] + hbm(2)
    aliases = {}
    if begun is not None:
        aliases = {len(operands): 0}
        operands.append(begun)
        in_specs.append(pl.BlockSpec(memory_space=pl.ANY))
    return pl.pallas_call(
        functools.partial(update_kernel, sizes, begun is not None),
        grid_spec=pltpu.PrefetchScalarGridSpec(
            num_scalar_prefetch=1,
            grid=row_tiles.shape + (tiles,),
            in_specs=in_specs,
            out_specs=pl.BlockSpec(
                (members, fields, ROW_TILE, LANES), lambda i, t, tile: (0, 0, tile[i], t)
            ),
            scratch_shapes=[
                pltpu.VMEM((fields, members, cells), jnp.float32),
                pltpu.VMEM((fields, 3 * members, cells), jnp.bfloat16),
                pltpu.VMEM(lhs[0].shape[2:], jnp.bfloat16),
                pltpu.VMEM(lhs[1].shape[2:], jnp.bfloat16),
                pltpu.SemaphoreType.DMA((2,)),
            ],
        ),
        out_shape=jax.ShapeDtypeStruct((members, fields, rows, columns), jnp.float32),
        input_output_aliases=aliases,
        compiler_params=params(16),
        name="update",
    )(*operands)


def edge_kernel(ens_ref, depth_ref, first_ref, last_ref, sem):
    members, fields, rows, _ = ens_ref.shape
    copies = []
    for i, (out_ref, row) in enumerate(((first_ref, 0), (last_ref, rows - HALO))):
        part = pl.ds(row, HALO)
        for m in range(members):
            to = out_ref.at[pl.ds(m * fields, fields)]
            copies.append(pltpu.make_async_copy(ens_ref.at[m, :, part], to, sem.at[i, m]))
        to = out_ref.at[members * fields]
        copies.append(pltpu.make_async_copy(depth_ref.at[part], to, sem.at[i, members]))
    for copy in copies:
        copy.start()
    for copy in copies:
        copy.wait()


def row_halos(ensemble, depth, axis):
    size = lax.axis_size(axis)
    onward = [(i, (i + 1) % size) for i in range(size)]
    backward = [(j, i) for i, j in onward]
    members, fields, _, columns = ensemble.shape
    edge = jax.ShapeDtypeStruct((members * fields + 1, HALO, columns), jnp.float32)
    first, last = pl.pallas_call(
        edge_kernel,
        in_specs=hbm(2),
        out_specs=vmem(2),
        out_shape=[edge, edge],
        scratch_shapes=[pltpu.SemaphoreType.DMA((2, members + 1))],
        compiler_params=params(16),
        name="edges",
    )(ensemble, depth)
    return lax.ppermute(last, axis, onward), lax.ppermute(first, axis, backward)


def local(ensemble, sea_depth, cutoff, obs_index, obs_value, obs_var):
    blocks = lax.axis_size("mem")
    subs = lax.axis_size("sub")
    local_members, fields, rows, size_y = ensemble.shape
    members = local_members * blocks
    col_block = size_y // blocks
    size_x = rows * subs
    sizes = (size_x, size_y)
    sub, mem = lax.axis_index("sub"), lax.axis_index("mem")
    x_start = sub * rows
    y_start = mem * col_block
    start = jnp.stack([x_start, y_start, sub, mem]).astype(jnp.int32)
    obs_x = obs_index // size_y
    obs_y = obs_index % size_y
    flat_x = obs_x.reshape(1, -1)
    flat_y = obs_y.reshape(1, -1)

    halos = row_halos(
        pltpu.with_memory_space_constraint(ensemble, pltpu.HBM),
        pltpu.with_memory_space_constraint(sea_depth, pltpu.HBM),
        "sub",
    )
    halos *= 2
    radius_part = pick_radius(cutoff, flat_x[0], flat_y[0], x_start, y_start)[None]

    inner_rows = rows - 2 * HALO
    last = rows // ROW_TILE - 1
    sent_inner = forecast("inner", range(1, last), ensemble, sea_depth, blocks)
    received_inner = lax.all_to_all(
        sent_inner, "mem", split_axis=0, concat_axis=0, tiled=True
    )
    row = flat_x - x_start
    inner_heights = pick_inner(row - HALO, flat_y, sent_inner)

    outer_row = jnp.where(
        row < HALO, row, jnp.where(row < rows - HALO, -1, row - inner_rows)
    )
    sent_outer = forecast("outer", [1, last + 1], ensemble, sea_depth, blocks, halos)
    part = pick_outer(outer_row, flat_y, sent_outer, inner_heights, radius_part, subs)
    piece = lax.dynamic_index_in_dim(sum_over(part, "sub"), sub, 0, keepdims=True)
    low = max(blocks // 4, 1)
    every = gather_over(gather_over(piece, "mem", 1, low), "mem", low, blocks // low)
    every, sent_outer = lax.optimization_barrier((every, sent_outer))
    received_outer = lax.all_to_all(
        sent_outer, "mem", split_axis=0, concat_axis=0, tiled=True
    )
    every = gather_over(every[None], "sub")
    *lhs, counts = chain(
        members, start, every, obs_x, obs_y, obs_value, obs_var, cutoff, sizes
    )

    lhs[2:] = [pltpu.with_memory_space_constraint(more, pltpu.HBM) for more in lhs[2:]]

    def analyse(received, row_tiles, begun=None):
        row_tiles = jnp.array(row_tiles, jnp.int32)
        return update(row_tiles, start, counts, received, cutoff, lhs, sizes, begun)

    return analyse(received_outer, [0, last], analyse(received_inner, list(range(1, last))))


def solution(mesh):
    return jax.shard_map(
        local,
        mesh=mesh,
        in_specs=(P("mem", None, "sub", None), P("sub", None), P("sub", "mem"), P(), P(), P()),
        out_specs=P(None, None, "sub", "mem"),
        check_vma=False,
    )
```

```python
import functools

import jax
import jax.numpy as jnp
from jax import lax
from jax.experimental import pallas as pl
from jax.experimental.pallas import tpu as pltpu
from jax.sharding import PartitionSpec as P

STEPS = 4
HALO = 2 * STEPS
LANES = 128
OBS_BLOCK = 64
ROW_TILE = 8
OUTER_COST = pl.CostEstimate(flops=23 * 10**9, bytes_accessed=74 * 10**6, transcendentals=0)
CHAIN_COST = pl.CostEstimate(flops=26 * 10**9, bytes_accessed=85 * 10**6, transcendentals=0)

step_size = 0.3
coriolis = 0.2
highest = lax.Precision.HIGHEST

NT = (((1,), (1,)), ((), ()))
TN = (((0,), (0,)), ((), ()))


def params(mebibytes):
    return pltpu.CompilerParams(vmem_limit_bytes=mebibytes * 2**20)


def vmem(count=1):
    return [pl.BlockSpec(memory_space=pltpu.VMEM)] * count


def hbm(count=1):
    return [pl.BlockSpec(memory_space=pltpu.HBM)] * count


def smem(count=1):
    return [pl.BlockSpec(memory_space=pltpu.SMEM)] * count


def split_bf16(value):
    high = value.astype(jnp.bfloat16)
    low = (value - high.astype(jnp.float32)).astype(jnp.bfloat16)
    return high, low


def row_centred(field):
    return pltpu.roll(field, field.shape[0] - 1, 0) - pltpu.roll(field, 1, 0)


def column_centred(tile_of, tiles):
    onward, back = [None] * tiles, [None] * tiles

    def at(t):
        for n in ((t - 1) % tiles, t, (t + 1) % tiles):
            if onward[n] is None:
                tile = tile_of(n)
                onward[n] = pltpu.roll(tile, LANES - 1, 1)
                back[n] = pltpu.roll(tile, 1, 1)
        lane = lax.broadcasted_iota(jnp.int32, onward[t].shape, 1)
        return jnp.where(
            lane == LANES - 1, onward[(t + 1) % tiles], onward[t]
        ) - jnp.where(lane == 0, back[(t - 1) % tiles], back[t])

    return at


def forecast_steps(height, east, north, half_depth):
    tiles = height.shape[0]
    half = 0.5 * step_size
    turn = step_size * coriolis
    for _ in range(STEPS):
        slope = column_centred(lambda t: half * height[t], tiles)
        for t in range(tiles):
            u, v = east[t], north[t]
            slope_y = slope(t)
            east[t] = u + turn * v - row_centred(half * height[t])
            north[t] = v - turn * u - slope_y
        inflow = column_centred(lambda t: half_depth[t] * north[t], tiles)
        for t in range(tiles):
            flow_y = inflow(t)
            height[t] = height[t] - (row_centred(half_depth[t] * east[t]) + flow_y)


def forecast_kernel(joins, kept, *refs):
    ens_ref, depth_ref, *halos, out_ref, height, east, north, half_depth = refs
    tiles = height.shape[0]
    out_tiles = out_ref.shape[2]
    fields = ens_ref.shape[1]

    def window(block, above, below, t):
        part = slice(t * LANES, (t + 1) * LANES)
        if not joins:
            return block[:, part]
        return jnp.concatenate([above[:, part], block[:, part], below[:, part]], 0)

    up_ref, down_ref, depth_up_ref, depth_down_ref = halos if joins else [None] * 4

    @pl.when(pl.program_id(0) == 0)
    def _():
        for t in range(tiles):
            above, below = (depth_up_ref.at[0], depth_down_ref.at[0]) if joins else (None, None)
            half_depth[t] = (0.5 * step_size) * window(depth_ref, above, below, t)

    state = (height, east, north)
    for f in range(fields):
        above, below = (up_ref.at[f], down_ref.at[f]) if joins else (None, None)
        for t in range(tiles):
            state[f][t] = window(ens_ref.at[0, f], above, below, t)
    forecast_steps(*state, half_depth)
    for f in range(fields):
        for t in range(tiles):
            for place, tile in enumerate(kept):
                out_ref[t // out_tiles, place, t % out_tiles, 0, f] = state[f][
                    t, tile * ROW_TILE : (tile + 1) * ROW_TILE
                ]


def forecast(name, kept, ensemble, depth, blocks, halos=()):
    members, fields, rows, columns = ensemble.shape
    tiles = columns // LANES
    window_rows = rows + (2 * HALO if halos else 0)
    out_shape = (blocks, len(kept), tiles // blocks, members, fields, ROW_TILE, LANES)
    in_specs = [
        pl.BlockSpec((1, fields, rows, columns), lambda m: (m, 0, 0, 0)),
        pl.BlockSpec((rows, columns), lambda m: (0, 0)),
    ]
    if halos:
        in_specs += [pl.BlockSpec((fields, HALO, columns), lambda m: (m, 0, 0))] * 2
        in_specs += [pl.BlockSpec((1, HALO, columns), lambda m: (members * fields, 0, 0))] * 2
    return pl.pallas_call(
        functools.partial(forecast_kernel, bool(halos), kept),
        grid=(members,),
        in_specs=in_specs,
        out_specs=pl.BlockSpec(
            out_shape[:3] + (1,) + out_shape[4:], lambda m: (0, 0, 0, m, 0, 0, 0)
        ),
        out_shape=jax.ShapeDtypeStruct(out_shape, jnp.float32),
        scratch_shapes=[pltpu.VMEM((tiles, window_rows, LANES), jnp.float32)] * 4,
        compiler_params=params(16),
        cost_estimate=OUTER_COST if halos else None,
        name=name,
    )(ensemble, depth, *halos)


def pick(row_ref, col_ref, height_ref):
    blocks, row_tiles, tiles, members, _, _, _ = height_ref.shape
    rows = row_tiles * ROW_TILE
    heights = jnp.concatenate(
        [
            height_ref[d, :, t, :, 0].reshape(rows * members, LANES)
            for d in range(blocks)
            for t in range(tiles)
        ],
        1,
    )
    high, rest = heights.astype(jnp.bfloat16), heights
    pieces = [high]
    for _ in range(2):
        rest = rest - pieces[-1].astype(jnp.float32)
        pieces.append(rest.astype(jnp.bfloat16))
    count = col_ref.shape[1]
    column = lax.broadcasted_iota(jnp.int32, (heights.shape[1], count), 0)
    in_column = (column == col_ref[...]).astype(jnp.float32).astype(jnp.bfloat16)
    found = jnp.dot(
        jnp.concatenate(pieces, 0), in_column, preferred_element_type=jnp.float32
    )
    size = members * rows
    found = (found[:size] + found[size : 2 * size]) + found[2 * size :]
    found = found.reshape(row_tiles, members, ROW_TILE, count)
    row = lax.broadcasted_iota(jnp.int32, (1, ROW_TILE, count), 1)
    result = 0.0
    for i in range(row_tiles):
        here = row + i * ROW_TILE == row_ref[...][None]
        result = result + jnp.sum(jnp.where(here, found[i], 0.0), 1)
    return result


def pick_inner_kernel(row_ref, col_ref, height_ref, out_ref):
    out_ref[...] = pick(row_ref, col_ref, height_ref)


def pick_outer_kernel(row_ref, col_ref, height_ref, inner_ref, radius_ref, out_ref):
    heights = pick(row_ref, col_ref, height_ref) + inner_ref[...]
    members, count = heights.shape
    pieces = out_ref.shape[0]
    groups = count // pieces // LANES
    out_ref[...] = jnp.zeros_like(out_ref)
    for j in range(pieces):
        for g in range(groups):
            part = slice((j * groups + g) * LANES, (j * groups + g + 1) * LANES)
            for m in range(members):
                row = g * members + m
                out_ref[j, row : row + 1, :] = heights[m : m + 1, part]
            row = members * groups + g
            out_ref[j, row : row + 1, :] = radius_ref[:, part]


def height_spec(sent):
    shape = sent.shape[:4] + (1,) + sent.shape[5:]
    return pl.BlockSpec(shape, lambda i: (0,) * len(shape))


def whole_spec(shape):
    return pl.BlockSpec(shape, lambda i: (0,) * len(shape))


def pick_inner(row, col, sent):
    shape = (sent.shape[3], col.shape[1])
    return pl.pallas_call(
        pick_inner_kernel,
        grid=(1,),
        in_specs=[whole_spec(row.shape), whole_spec(col.shape), height_spec(sent)],
        out_specs=whole_spec(shape),
        out_shape=jax.ShapeDtypeStruct(shape, jnp.float32),
        compiler_params=params(40),
        name="pick_inner",
    )(row, col, sent)


def pick_outer(row, col, sent, inner, radius, pieces):
    members, count = inner.shape
    used = (members + 1) * (count // pieces // LANES)
    shape = (pieces, used + -used % 8, LANES)
    return pl.pallas_call(
        pick_outer_kernel,
        grid=(1,),
        in_specs=[
            whole_spec(row.shape),
            whole_spec(col.shape),
            height_spec(sent),
            whole_spec(inner.shape),
            whole_spec(radius.shape),
        ],
        out_specs=whole_spec(shape),
        out_shape=jax.ShapeDtypeStruct(shape, jnp.float32),
        compiler_params=params(40),
        name="pick_outer",
    )(row, col, sent, inner, radius)


def pick_radius(cutoff, obs_x, obs_y, x_start, y_start):
    rows, columns = cutoff.shape
    radius_sq = jnp.square(cutoff.astype(jnp.float32))
    row_is = (obs_x[:, None] - x_start == jnp.arange(rows)[None, :]).astype(jnp.float32)
    col_is = obs_y[:, None] - y_start == jnp.arange(columns)[None, :]
    by_row = jnp.dot(row_is, radius_sq, precision=highest)
    return jnp.sum(jnp.where(col_is, by_row, 0.0), 1)


def exchange(value, axis, distance):
    size = lax.axis_size(axis)
    return lax.ppermute(value, axis, [(i, i ^ distance) for i in range(size)])


def sum_over(value, axis):
    distance = 1
    while distance < lax.axis_size(axis):
        value = value + exchange(value, axis, distance)
        distance *= 2
    return value


def gather_over(value, axis, first=1, width=None):
    width = lax.axis_size(axis) if width is None else width
    return jnp.concatenate(
        [value] + [exchange(value, axis, r * first) for r in range(1, width)], 0
    )


def apart_sq(a, b, size):
    gap = jnp.abs(a - b)
    gap = jnp.minimum(gap, size - gap)
    return gap * gap


def eliminate_four(system, k, row_id):
    width = system.shape[1]
    row = [system[k + i : k + i + 1, :] for i in range(4)]
    p = [
        [jnp.broadcast_to(row[i][:, k + j : k + j + 1], (1, LANES)) for j in range(4)]
        for i in range(4)
    ]

    def wide(value):
        return jnp.concatenate([value] * (width // LANES), 1)

    def inverse(a00, a01, a10, a11):
        scale = 1.0 / (a00 * a11 - a01 * a10)
        return a11 * scale, -a01 * scale, -a10 * scale, a00 * scale

    i00, i01, i10, i11 = inverse(p[0][0], p[0][1], p[1][0], p[1][1])
    y = [
        [i00 * p[0][2 + j] + i01 * p[1][2 + j] for j in range(2)],
        [i10 * p[0][2 + j] + i11 * p[1][2 + j] for j in range(2)],
    ]
    schur = [
        [p[2 + i][2 + j] - p[2 + i][0] * y[0][j] - p[2 + i][1] * y[1][j] for j in range(2)]
        for i in range(2)
    ]
    s00, s01, s10, s11 = inverse(schur[0][0], schur[0][1], schur[1][0], schur[1][1])
    top0 = wide(i00) * row[0] + wide(i01) * row[1]
    top1 = wide(i10) * row[0] + wide(i11) * row[1]
    low0 = row[2] - wide(p[2][0]) * top0 - wide(p[2][1]) * top1
    low1 = row[3] - wide(p[3][0]) * top0 - wide(p[3][1]) * top1
    new2 = wide(s00) * low0 + wide(s01) * low1
    new3 = wide(s10) * low0 + wide(s11) * low1
    new0 = top0 - wide(y[0][0]) * new2 - wide(y[0][1]) * new3
    new1 = top1 - wide(y[1][0]) * new2 - wide(y[1][1]) * new3
    new = (new0, new1, new2, new3)
    result = system
    for i in range(4):
        result = result - system[:, k + i : k + i + 1] * new[i]
    for i in range(4):
        result = jnp.where(row_id == k + i, new[i], result)
    return result


def chain_kernel(
    members,
    sizes,
    start_ref,
    every_ref,
    row_ref,
    col_ref,
    value_ref,
    variance_ref,
    cutoff_ref,
    lhs1_ref,
    lhs2_ref,
    more1_ref,
    more2_ref,
    count_ref,
    local_ref,
    anom_ref,
    mix_ref,
    rank_ref,
    block1_ref,
    block2_ref,
    sem,
):
    size_x, size_y = sizes
    pieces, sources, _, _ = every_ref.shape
    batches, count = value_ref.shape
    groups = batches * count // pieces // LANES
    local_members = members // sources
    rows, columns = cutoff_ref.shape
    tiles = columns // LANES
    x_start = start_ref[0]
    y_start = start_ref[1]
    reach = jnp.max(cutoff_ref[...])
    reach_sq = reach * reach

    heights, radius_sq = [], []
    for j in range(pieces):
        piece = jnp.bitwise_xor(start_ref[2], j)
        for g in range(groups):
            found, radius = [], 0.0
            for source in range(sources):
                one = every_ref.at[piece, jnp.bitwise_xor(start_ref[3], source)]
                found.append(one[g * local_members : (g + 1) * local_members, :])
                last = local_members * groups + g
                radius = radius + one[last : last + 1, :]
            heights.append(jnp.concatenate(found, 0))
            radius_sq.append(radius)
    heights = jnp.concatenate(heights, 1)
    inverse_sq = 1.0 / jnp.concatenate(radius_sq, 1)
    before = (
        lax.broadcasted_iota(jnp.int32, (count, count), 0)
        <= lax.broadcasted_iota(jnp.int32, (count, count), 1)
    ).astype(jnp.bfloat16)
    slot = lax.broadcasted_iota(jnp.int32, (OBS_BLOCK, count), 0)
    twice = lax.broadcasted_iota(jnp.int32, (members, 3 * OBS_BLOCK), 1) < 2 * OBS_BLOCK
    member_row = lax.broadcasted_iota(jnp.int32, (members, LANES + count), 0)
    eye = (
        lax.broadcasted_iota(jnp.int32, (members, members), 0)
        == lax.broadcasted_iota(jnp.int32, (members, members), 1)
    ).astype(jnp.float32)

    def rank_reaching(b, t):
        obs_x = row_ref[0:1, b * count : (b + 1) * count]
        obs_y = row_ref[1:2, b * count : (b + 1) * count]
        off_x = jnp.where(obs_x >= x_start, obs_x - x_start, obs_x - x_start + size_x)
        gap_x = jnp.where(off_x < rows, 0, jnp.minimum(off_x - (rows - 1), size_x - off_x))
        off_y = obs_y - (y_start + t * LANES)
        off_y = jnp.where(off_y >= 0, off_y, off_y + size_y)
        gap_y = jnp.where(off_y < LANES, 0, jnp.minimum(off_y - (LANES - 1), size_y - off_y))
        reaches = gap_x * gap_x + gap_y * gap_y < reach_sq
        flags = jnp.broadcast_to(reaches.astype(jnp.float32), (8, count))
        ranks = jnp.dot(
            flags.astype(jnp.bfloat16), before, preferred_element_type=jnp.float32
        )
        rank_ref[b, t] = jnp.where(reaches, ranks.astype(jnp.int32) - 1, -1)
        count_ref[b, t] = jnp.sum(flags[0:1, :]).astype(jnp.int32)

    def gather(b, t, k, to1, to2):
        chosen = (slot == rank_ref[b, t, 0:1, :] - k * OBS_BLOCK).astype(jnp.float32)
        thrice = jnp.concatenate([chosen] * 3, 0).astype(jnp.bfloat16)
        chosen = chosen.astype(jnp.bfloat16)

        def product(x, y):
            return lax.dot_general(x, y, NT, preferred_element_type=jnp.float32)

        to1[...] = product(chosen, anom_ref[b]).astype(jnp.bfloat16)
        to2[...] = jnp.where(
            twice, product(mix_ref[b, 0], thrice), product(mix_ref[b, 1], thrice)
        ).astype(jnp.bfloat16)

    def localize(b, first, size):
        later = slice((b + 1) * count, batches * count)
        part = slice(first, first + size)
        dist_sq = apart_sq(col_ref[part, b : b + 1], row_ref[0:1, later], size_x) + apart_sq(
            col_ref[part, batches + b : batches + b + 1], row_ref[1:2, later], size_y
        )
        ratio = dist_sq.astype(jnp.float32) * inverse_sq[:, later]
        local_ref[part, later] = jnp.square(jnp.maximum(1.0 - ratio, 0.0))

    for b in range(batches):
        here = slice(b * count, (b + 1) * count)
        prior = heights[:, here]
        mean = jnp.mean(prior, 0, keepdims=True)
        anom = prior - mean
        precision = 1.0 / variance_ref[b : b + 1, :]
        innov = value_ref[b : b + 1, :] - mean
        scaled = anom * precision
        inner = eye + lax.dot_general(
            scaled, anom, NT, precision=highest, preferred_element_type=jnp.float32
        ) / (members - 1)
        proj = jnp.sum(scaled * innov, 1, keepdims=True)
        system = jnp.concatenate(
            [inner, proj, jnp.zeros((members, LANES - members - 1), jnp.float32), scaled], 1
        )
        aside = [functools.partial(rank_reaching, b, t) for t in range(tiles)]
        if b > 0:
            aside += [
                functools.partial(gather, b - 1, t, 0, lhs1_ref.at[b - 1, t], lhs2_ref.at[b - 1, t])
                for t in range(tiles)
            ]
        if b + 1 < batches:
            aside += [functools.partial(localize, b, first, 32) for first in range(0, count, 32)]
        steps = members // 4
        for step in range(steps):
            system = eliminate_four(system, 4 * step, member_row)
            for one in aside[step::steps]:
                one()
        solved_proj = system[:, members : members + 1]
        solved_anom = system[:, LANES:]
        solved_innov = precision * (
            innov - jnp.sum(anom * solved_proj, 0, keepdims=True) / (members - 1)
        )
        mix = (solved_innov - 0.5 * solved_anom) / (members - 1)
        high, low = split_bf16(anom)
        cells = row_ref[:, here]
        cells = jnp.concatenate([cells // 256, cells % 256] * 4, 0).astype(jnp.float32)
        anom_ref[b] = jnp.concatenate([high, high, low, cells.astype(jnp.bfloat16)], 0)
        mix_high, mix_low = split_bf16(mix)
        mix_ref[b, 0] = mix_high
        mix_ref[b, 1] = mix_low

        if b + 1 < batches:
            later = slice((b + 1) * count, batches * count)
            ahead = heights[:, later]
            ahead_anom = ahead - jnp.mean(ahead, 0, keepdims=True)
            cross = lax.dot_general(
                anom, ahead_anom, TN, precision=highest, preferred_element_type=jnp.float32
            )
            high, low = split_bf16(cross * local_ref[:, later])
            both = jnp.dot(
                jnp.concatenate([mix_high, mix_low], 0), high, preferred_element_type=jnp.float32
            )
            rest = jnp.dot(mix_high, low, preferred_element_type=jnp.float32)
            ahead = ahead + (both[:members] + (both[members:] + rest))
            heights = jnp.concatenate([heights[:, : (b + 1) * count], ahead], 1)

    for t in range(tiles):
        gather(batches - 1, t, 0, lhs1_ref.at[batches - 1, t], lhs2_ref.at[batches - 1, t])
    counts = [[count_ref[b, t] for t in range(tiles)] for b in range(batches)]
    most = functools.reduce(jnp.maximum, sum(counts, []))

    @pl.when(most > OBS_BLOCK)
    def _():
        for b in range(batches):
            for t in range(tiles):

                def more(k, _, b=b, t=t):
                    gather(b, t, k, block1_ref, block2_ref)
                    for i, (block, to) in enumerate(
                        ((block1_ref, more1_ref), (block2_ref, more2_ref))
                    ):
                        copy = pltpu.make_async_copy(block, to.at[b, t, k - 1], sem.at[i])
                        copy.start()
                        copy.wait()
                    return 0

                blocks = (counts[b][t] + (OBS_BLOCK - 1)) // OBS_BLOCK
                lax.fori_loop(1, blocks, more, 0)


def chain(members, start, every, obs_x, obs_y, values, variance, cutoff, sizes):
    batches, count = values.shape
    row_form = jnp.stack([obs_x.reshape(-1), obs_y.reshape(-1)], 0)
    col_form = jnp.concatenate([obs_x, obs_y], 0).T
    tiles = cutoff.shape[1] // LANES
    first = (batches, tiles)
    more = first + (max(-(-count // OBS_BLOCK) - 1, 1),)
    shape1 = (OBS_BLOCK, 3 * members + 16)
    shape2 = (members, 3 * OBS_BLOCK)
    return pl.pallas_call(
        functools.partial(chain_kernel, members, sizes),
        in_specs=smem() + vmem(6),
        out_specs=vmem(2) + hbm(2) + smem(),
        out_shape=[
            jax.ShapeDtypeStruct(lead + shape, jnp.bfloat16)
            for lead in (first, more)
            for shape in (shape1, shape2)
        ]
        + [jax.ShapeDtypeStruct(first, jnp.int32)],
        scratch_shapes=[
            pltpu.VMEM((count, batches * count), jnp.float32),
            pltpu.VMEM((batches, 3 * members + 16, count), jnp.bfloat16),
            pltpu.VMEM((batches, 2, members, count), jnp.bfloat16),
            pltpu.VMEM((batches, tiles, 8, count), jnp.int32),
            pltpu.VMEM(shape1, jnp.bfloat16),
            pltpu.VMEM(shape2, jnp.bfloat16),
            pltpu.SemaphoreType.DMA((2,)),
        ],
        compiler_params=params(16),
        cost_estimate=CHAIN_COST,
        name="chain",
    )(start, every, row_form, col_form, values, variance, cutoff)


def update_kernel(
    sizes,
    continues,
    tile_ref,
    start_ref,
    count_ref,
    state_ref,
    cutoff_ref,
    lhs1_ref,
    lhs2_ref,
    more1_ref,
    more2_ref,
    *rest,
):
    out_ref, members_ref, rhs_ref, block1_ref, block2_ref, sem = rest[1:] if continues else rest
    size_x, size_y = float(sizes[0]), float(sizes[1])
    sources, _, _, local_members, fields, rows, _ = state_ref.shape
    members = sources * local_members
    batches = lhs1_ref.shape[0]
    cells = rows * LANES
    t = pl.program_id(1)
    flat = state_ref.reshape(members * fields * rows, LANES)
    flat_out = out_ref.reshape(members * fields * rows, LANES)
    row0 = (start_ref[0] + tile_ref[pl.program_id(0)] * rows).astype(jnp.float32)
    col0 = (start_ref[1] + t * LANES).astype(jnp.float32)
    lane = lax.broadcasted_iota(jnp.int32, (1, LANES), 1).astype(jnp.float32)
    radius = cutoff_ref[...].astype(jnp.float32)
    radius_sq = radius * radius
    inverse = 1.0 / radius_sq

    def localized(lhs1):
        place = lhs1[:, 3 * members :].astype(jnp.float32)
        obs_x = jnp.broadcast_to(place[:, 0:1] * 256.0 + place[:, 2:3], (OBS_BLOCK, LANES))
        obs_y = jnp.broadcast_to(place[:, 1:2] * 256.0 + place[:, 3:4], (OBS_BLOCK, LANES))
        dist_y = apart_sq(obs_y, lane + col0, size_y)
        dist_x = apart_sq(obs_x, lane + row0, size_x)
        weights = []
        for r in range(rows):
            ratio = (dist_y + dist_x[:, r : r + 1]) * inverse[r : r + 1, :]
            weights.append(jnp.square(jnp.maximum(1.0 - ratio, 0.0)))
        return jnp.concatenate(weights, 1)

    def crossed(lhs1, rhs):
        return jnp.dot(lhs1[:, : 3 * members], rhs, preferred_element_type=jnp.float32)

    def moved(lhs2, cross, weights):
        high, low = split_bf16(cross * weights)
        return jnp.dot(
            lhs2, jnp.concatenate([high, low, high], 0), preferred_element_type=jnp.float32
        )

    def split_anom(state):
        high, low = split_bf16(state - jnp.mean(state, 0, keepdims=True))
        return jnp.concatenate([high, low, high], 0)

    def load(f):
        return jnp.concatenate(
            [
                flat[pl.ds(f * rows + r, members, stride=fields * rows), :]
                for r in range(rows)
            ],
            1,
        )

    def store(f, state):
        for r in range(rows):
            flat_out[pl.ds(f * rows + r, members, stride=fields * rows), :] = state[
                :, r * LANES : (r + 1) * LANES
            ]

    most = count_ref[0, t]
    for b in range(1, batches):
        most = jnp.maximum(most, count_ref[b, t])

    @pl.when(most <= OBS_BLOCK)
    def _():
        states = [load(f) for f in range(fields)]
        for b in range(batches):
            lhs1 = lhs1_ref[b, 0]
            weights = localized(lhs1)
            cross = [crossed(lhs1, x) for x in [split_anom(state) for state in states]]
            steps = [moved(lhs2_ref[b, 0], c, weights) for c in cross]
            states = [state + step for state, step in zip(states, steps)]
        for f in range(fields):
            store(f, states[f])

    @pl.when(most > OBS_BLOCK)
    def _():
        for f in range(fields):
            members_ref[f] = load(f)
        for b in range(batches):
            for f in range(fields):
                rhs_ref[f] = split_anom(members_ref[f])

            def add(lhs1, lhs2):
                weights = localized(lhs1)
                for f in range(fields):
                    members_ref[f] += moved(lhs2, crossed(lhs1, rhs_ref[f]), weights)

            def block(k, _, b=b):
                for i, (more, to) in enumerate(((more1_ref, block1_ref), (more2_ref, block2_ref))):
                    copy = pltpu.make_async_copy(more.at[b, t, k - 1], to, sem.at[i])
                    copy.start()
                    copy.wait()
                add(block1_ref[...], block2_ref[...])
                return 0

            add(lhs1_ref[b, 0], lhs2_ref[b, 0])
            blocks = (count_ref[b, t] + (OBS_BLOCK - 1)) // OBS_BLOCK
            lax.fori_loop(1, blocks, block, 0)
        for f in range(fields):
            store(f, members_ref[f])


def update(row_tiles, start, counts, state, cutoff, lhs, sizes, begun=None):
    sources, _, tiles, local_members, fields, _, _ = state.shape
    members = sources * local_members
    rows = cutoff.shape[0]
    columns = tiles * LANES
    cells = ROW_TILE * LANES

    def of_tile(array):
        shape = (array.shape[0], 1) + array.shape[2:]
        return pl.BlockSpec(shape, lambda i, t, tile: (0, t) + (0,) * (array.ndim - 2))

    operands = [row_tiles, start, counts, state, cutoff, *lhs]
    in_specs = smem(2) + [
        pl.BlockSpec(
            (sources, 1, 1, local_members, fields, ROW_TILE, LANES),
            lambda i, t, tile: (0, i, t, 0, 0, 0, 0),
        ),
        pl.BlockSpec((ROW_TILE, LANES), lambda i, t, tile: (tile[i], t)),
        of_tile(lhs[0]),
        of_tile(lhs[1]),
    ] + hbm(2)
    aliases = {}
    if begun is not None:
        aliases = {len(operands): 0}
        operands.append(begun)
        in_specs.append(pl.BlockSpec(memory_space=pl.ANY))
    return pl.pallas_call(
        functools.partial(update_kernel, sizes, begun is not None),
        grid_spec=pltpu.PrefetchScalarGridSpec(
            num_scalar_prefetch=1,
            grid=row_tiles.shape + (tiles,),
            in_specs=in_specs,
            out_specs=pl.BlockSpec(
                (members, fields, ROW_TILE, LANES), lambda i, t, tile: (0, 0, tile[i], t)
            ),
            scratch_shapes=[
                pltpu.VMEM((fields, members, cells), jnp.float32),
                pltpu.VMEM((fields, 3 * members, cells), jnp.bfloat16),
                pltpu.VMEM(lhs[0].shape[2:], jnp.bfloat16),
                pltpu.VMEM(lhs[1].shape[2:], jnp.bfloat16),
                pltpu.SemaphoreType.DMA((2,)),
            ],
        ),
        out_shape=jax.ShapeDtypeStruct((members, fields, rows, columns), jnp.float32),
        input_output_aliases=aliases,
        compiler_params=params(16),
        name="update",
    )(*operands)


def edge_kernel(ens_ref, depth_ref, first_ref, last_ref, sem):
    members, fields, rows, _ = ens_ref.shape
    copies = []
    for i, (out_ref, row) in enumerate(((first_ref, 0), (last_ref, rows - HALO))):
        part = pl.ds(row, HALO)
        for m in range(members):
            to = out_ref.at[pl.ds(m * fields, fields)]
            copies.append(pltpu.make_async_copy(ens_ref.at[m, :, part], to, sem.at[i, m]))
        to = out_ref.at[members * fields]
        copies.append(pltpu.make_async_copy(depth_ref.at[part], to, sem.at[i, members]))
    for copy in copies:
        copy.start()
    for copy in copies:
        copy.wait()


def row_halos(ensemble, depth, axis):
    size = lax.axis_size(axis)
    onward = [(i, (i + 1) % size) for i in range(size)]
    backward = [(j, i) for i, j in onward]
    members, fields, _, columns = ensemble.shape
    edge = jax.ShapeDtypeStruct((members * fields + 1, HALO, columns), jnp.float32)
    first, last = pl.pallas_call(
        edge_kernel,
        in_specs=hbm(2),
        out_specs=vmem(2),
        out_shape=[edge, edge],
        scratch_shapes=[pltpu.SemaphoreType.DMA((2, members + 1))],
        compiler_params=params(16),
        name="edges",
    )(ensemble, depth)
    return lax.ppermute(last, axis, onward), lax.ppermute(first, axis, backward)


def local(ensemble, sea_depth, cutoff, obs_index, obs_value, obs_var):
    blocks = lax.axis_size("mem")
    subs = lax.axis_size("sub")
    local_members, fields, rows, size_y = ensemble.shape
    members = local_members * blocks
    col_block = size_y // blocks
    size_x = rows * subs
    sizes = (size_x, size_y)
    sub, mem = lax.axis_index("sub"), lax.axis_index("mem")
    x_start = sub * rows
    y_start = mem * col_block
    start = jnp.stack([x_start, y_start, sub, mem]).astype(jnp.int32)
    obs_x = obs_index // size_y
    obs_y = obs_index % size_y
    flat_x = obs_x.reshape(1, -1)
    flat_y = obs_y.reshape(1, -1)

    halos = row_halos(
        pltpu.with_memory_space_constraint(ensemble, pltpu.HBM),
        pltpu.with_memory_space_constraint(sea_depth, pltpu.HBM),
        "sub",
    )
    halos *= 2
    radius_part = pick_radius(cutoff, flat_x[0], flat_y[0], x_start, y_start)[None]

    inner_rows = rows - 2 * HALO
    last = rows // ROW_TILE - 1
    sent_inner = forecast("inner", range(1, last), ensemble, sea_depth, blocks)
    received_inner = lax.all_to_all(
        sent_inner, "mem", split_axis=0, concat_axis=0, tiled=True
    )
    row = flat_x - x_start
    inner_heights = pick_inner(row - HALO, flat_y, sent_inner)

    outer_row = jnp.where(
        row < HALO, row, jnp.where(row < rows - HALO, -1, row - inner_rows)
    )
    sent_outer = forecast("outer", [1, last + 1], ensemble, sea_depth, blocks, halos)
    part = pick_outer(outer_row, flat_y, sent_outer, inner_heights, radius_part, subs)
    piece = lax.dynamic_index_in_dim(sum_over(part, "sub"), sub, 0, keepdims=True)
    low = max(blocks // 4, 1)
    every = gather_over(gather_over(piece, "mem", 1, low), "mem", low, blocks // low)
    every, sent_outer = lax.optimization_barrier((every, sent_outer))
    received_outer = lax.all_to_all(
        sent_outer, "mem", split_axis=0, concat_axis=0, tiled=True
    )
    every = gather_over(every[None], "sub")
    *lhs, counts = chain(
        members, start, every, obs_x, obs_y, obs_value, obs_var, cutoff, sizes
    )

    lhs[2:] = [pltpu.with_memory_space_constraint(more, pltpu.HBM) for more in lhs[2:]]

    def analyse(received, row_tiles, begun=None):
        row_tiles = jnp.array(row_tiles, jnp.int32)
        return update(row_tiles, start, counts, received, cutoff, lhs, sizes, begun)

    return analyse(received_outer, [0, last], analyse(received_inner, list(range(1, last))))


def solution(mesh):
    return jax.shard_map(
        local,
        mesh=mesh,
        in_specs=(P("mem", None, "sub", None), P("sub", None), P("sub", "mem"), P(), P(), P()),
        out_specs=P(None, None, "sub", "mem"),
        check_vma=False,
    )
```
